32 devices in a mesh: member: 4 (over y, core), dp: 8 (over z, x).
Axes of the slice: x: 2, y: 2, z: 4, core: 2. Of those that a mesh axis runs over, the one named last changes fastest.
Arguments:
- states: float32 [8192, 17], P('dp'), may hold values from -6 to 6
- actions: float32 [8192, 6], P('dp'), may hold values from -0.95 to 0.95
- rewards: float32 [8192], P('dp'), may hold values from -6 to 6
- next_states: float32 [8192, 17], P('dp'), may hold values from -6 to 6
- terminal: int32 [8192], P('dp'), may hold values 0 or 1
- valid_rows: int32 [8192], P('dp'), may hold values from 0 to 1
- noise_seeds: int32 [8192, 2], P('dp'), may hold values from 0 to 255
- member_live: int32 [8], P('member'), may hold values from 0 to 1, as said below
- critic_body: float32 [8, 538, 256], P('member'), may hold values from -0.75 to 0.75
- critic_body_mom: float32 [8, 538, 256], P('member'), may hold values from -0.0048828125 to 0.0048828125
- critic_body_sq: float32 [8, 538, 256], P('member'), may hold values from 8.044036e-07 to 3.2176144e-06
- critic_body_tgt: float32 [8, 538, 256], P('member'), may hold values from -0.75 to 0.75
- critic_head: float32 [8, 257], P('member'), may hold values from -0.375 to 0.375
- critic_head_mom: float32 [8, 257], P('member'), may hold values from -0.0390625 to 0.0390625
- critic_head_sq: float32 [8, 257], P('member'), may hold values from 5.148183e-05 to 0.00020592732
- critic_head_tgt: float32 [8, 257], P('member'), may hold values from -0.375 to 0.375
- policy_body: float32 [532, 256], replicated, may hold values from -0.75 to 0.75
- policy_body_mom: float32 [532, 256], replicated, may hold values from -0.0048828125 to 0.0048828125
- policy_body_sq: float32 [532, 256], replicated, may hold values from 8.044036e-07 to 3.2176144e-06
- policy_head: float32 [257, 12], replicated, may hold values from -0.375 to 0.375
- policy_head_mom: float32 [257, 12], replicated, may hold values from -0.0390625 to 0.0390625
- policy_head_sq: float32 [257, 12], replicated, may hold values from 5.148183e-05 to 0.00020592732
- log_temp: float32 [1], replicated, may hold values from -2 to -0.5
- log_temp_mom: float32 [1], replicated, may hold values from -0.05 to 0.05
- log_temp_sq: float32 [1], replicated, may hold values from 0.001 to 0.004
Outputs:
- loss_parts: float32 [5], replicated
- grad_norm: float32 [1], replicated
- critic_body_new: float32 [8, 538, 256], P('member')
- critic_body_mom_new: float32 [8, 538, 256], P('member')
- critic_body_sq_new: float32 [8, 538, 256], P('member')
- critic_body_tgt_new: float32 [8, 538, 256], P('member')
- critic_body_half: bfloat16 [8, 538, 256], P('member')
- critic_head_new: float32 [8, 257], P('member')
- critic_head_mom_new: float32 [8, 257], P('member')
- critic_head_sq_new: float32 [8, 257], P('member')
- critic_head_tgt_new: float32 [8, 257], P('member')
- critic_head_half: bfloat16 [8, 257], P('member')
- policy_body_new: float32 [532, 256], replicated
- policy_body_mom_new: float32 [532, 256], replicated
- policy_body_sq_new: float32 [532, 256], replicated
- policy_body_half: bfloat16 [532, 256], replicated
- policy_head_new: float32 [257, 12], replicated
- policy_head_mom_new: float32 [257, 12], replicated
- policy_head_sq_new: float32 [257, 12], replicated
- policy_head_half: bfloat16 [257, 12], replicated
- log_temp_new: float32 [1], replicated
- log_temp_mom_new: float32 [1], replicated
- log_temp_sq_new: float32 [1], replicated
The draws below stay inside these ranges and needn't reach their ends.
Inputs may be any that keep to these rules, and one draw needn't show every extreme that they name: `member_live`: in each group of 2 consecutive slots the first k are 1 and the rest 0, k from 1 to 2; some group has all 2.
All inputs are finite; a program needn't handle non-finite values. No bound on the sum of `terminal` on one device may be relied on, other than what follows from the above.
Results may differ from the reference program's by a relative error of at most 0.001.
Values sent between devices are 32-bit elements; how exact they have to be, the bound alone decides.
No kernel may reach another device: no remote copies, remote signals or barrier semaphores. Data moves between devices by JAX's collectives and lax.ppermute only.
A program may use at most 64 MiB of HBM per device.

```python
import math
import jax
import jax.numpy as jnp
from jax import lax

S_DIM = 17
A_DIM = 6
HID = 256
CAP = 2
STEPS_DONE = 5
CRITICS = 8
TRANS = 8192
CB_ROWS = 538
AB_ROWS = 532
NPARAM = 1243157


def draw_valid_rows(key, part):
    key = jax.random.fold_in(key, 11)
    position = jnp.arange(TRANS, dtype=jnp.int32)
    threshold = 300 + 600 * position // TRANS
    ticket = jax.random.randint(key, (TRANS,), 0, 1000, dtype=jnp.int32)
    return (ticket < threshold).astype(jnp.int32)


def draw_member_live(key, part):
    key = jax.random.fold_in(key, 23)
    groups = CRITICS // CAP
    first_key, second_key = jax.random.split(key)
    counts = jax.random.randint(first_key, (groups,), CAP // 2, CAP + 1, dtype=jnp.int32)
    full_group = jax.random.randint(second_key, (), 0, groups, dtype=jnp.int32)
    counts = jnp.where(jnp.arange(groups, dtype=jnp.int32) == full_group, CAP, counts)
    slots = jnp.arange(CRITICS, dtype=jnp.int32)
    return (slots % CAP < counts[slots // CAP]).astype(jnp.int32)


def with_ends(result, own_key, least, high):
    extent = result.shape
    index_at = [jax.random.randint(jax.random.fold_in(own_key, axis), (), 0, extent[axis]) for axis in range(len(extent))]
    result = result.at[tuple(index_at)].set(least)
    longest = extent.index(max(extent))
    index_at[longest] = (index_at[longest] + 1) % extent[longest]
    return result.at[tuple(index_at)].set(high)


def block_levels(stream_key, extent, cuts, least, largest):
    loudness = 1.0
    for dim, blocks in cuts:
        steps = jax.random.uniform(jax.random.fold_in(jax.random.fold_in(stream_key, 6), dim), (blocks,), jnp.float32, least / len(cuts), largest / len(cuts))
        loudness = loudness * jnp.repeat(jnp.exp(steps), extent[dim] // blocks).reshape((-1,) + (1,) * (len(extent) - 1 - dim))
    return loudness


def bell_draw(key, shape, scale, limit, cuts=(), kind=jnp.bfloat16):
    values = jax.random.normal(key, shape, jnp.float32) * scale
    if len(cuts) > 0:
        values = block_levels(key, shape, cuts, -0.22, 0.18) * values
    return jnp.clip(values, min=-limit, max=limit).astype(kind)


def setup_inputs(seed: int = 0) -> dict:
    key_list = jax.random.split(jax.random.key(seed), 26)
    states = bell_draw(key_list[0], (TRANS, S_DIM), 1.0, 6.0, ((0, 8),), jnp.float32)
    actions = jnp.clip(jax.random.uniform(key_list[1], (TRANS, A_DIM), jnp.float32, -0.95, 0.95) * block_levels(key_list[1], (TRANS, A_DIM), ((0, 8),), -0.4, 0.0), -0.95, 0.95)
    rewards = bell_draw(key_list[2], (TRANS,), 1.0, 6.0, ((0, 8),), jnp.float32)
    next_states = bell_draw(key_list[3], (TRANS, S_DIM), 1.0, 6.0, ((0, 8),), jnp.float32)
    terminal = with_ends((jax.random.randint(key_list[4], (TRANS,), 0, 8) < 1).astype(jnp.int32), jax.random.fold_in(key_list[4], 1), 0, 1)
    valid_rows = draw_valid_rows(jax.random.fold_in(key_list[25], 71), 0)
    noise_seeds = with_ends(jax.random.randint(key_list[6], (TRANS, 2), 0, 256), jax.random.fold_in(key_list[6], 1), 0, 255).astype(jnp.int32)
    member_live = draw_member_live(jax.random.fold_in(key_list[25], 71), 0)
    critic_body = bell_draw(key_list[8], (CRITICS, CB_ROWS, HID), 64 ** -0.5, 0.75, ((0, 4),), jnp.float32)
    critic_body_mom = bell_draw(key_list[9], (CRITICS, CB_ROWS, HID), (NPARAM ** -0.5), 0.0048828125, ((0, 4),), jnp.float32)
    critic_body_sq = jnp.clip(jnp.exp(math.log(3.2176144486584235e-06) - 1.3862944 * jax.random.uniform(key_list[10], (CRITICS, CB_ROWS, HID), jnp.float32) ** block_levels(key_list[10], (CRITICS, CB_ROWS, HID), ((0, 4),), -0.2, 0.2)), 8.044036121646059e-07, 3.2176144486584235e-06)
    critic_body_tgt = bell_draw(key_list[11], (CRITICS, CB_ROWS, HID), 64 ** -0.5, 0.75, ((0, 4),), jnp.float32)
    critic_head = bell_draw(key_list[12], (CRITICS, HID + 1), HID ** -0.5, 0.375, ((0, 4),), jnp.float32)
    critic_head_mom = bell_draw(key_list[13], (CRITICS, HID + 1), (8 * NPARAM ** -0.5), 0.0390625, ((0, 4),), jnp.float32)
    critic_head_sq = jnp.clip(jnp.exp(math.log(0.00020592732) - 1.3862944 * jax.random.uniform(key_list[14], (CRITICS, HID + 1), jnp.float32) ** block_levels(key_list[14], (CRITICS, HID + 1), ((0, 4),), -0.2, 0.2)), 5.1481831178534776e-05, 0.00020592732)
    critic_head_tgt = bell_draw(key_list[15], (CRITICS, HID + 1), HID ** -0.5, 0.375, ((0, 4),), jnp.float32)
    policy_body = bell_draw(key_list[16], (AB_ROWS, HID), 64 ** -0.5, 0.75, (), jnp.float32)
    policy_body_mom = bell_draw(key_list[17], (AB_ROWS, HID), (NPARAM ** -0.5), 0.0048828125, (), jnp.float32)
    policy_body_sq = jnp.clip(jnp.exp(jax.random.uniform(key_list[18], (AB_ROWS, HID), jnp.float32, math.log(8.044036121646059e-07), math.log(3.2176144486584235e-06))), 8.044036121646059e-07, 3.2176144486584235e-06)
    policy_head = bell_draw(key_list[19], (HID + 1, 2 * A_DIM), HID ** -0.5, 0.375, (), jnp.float32)
    policy_head_mom = bell_draw(key_list[20], (HID + 1, 2 * A_DIM), (8 * NPARAM ** -0.5), 0.0390625, (), jnp.float32)
    policy_head_sq = jnp.clip(jnp.exp(jax.random.uniform(key_list[21], (HID + 1, 2 * A_DIM), jnp.float32, math.log(5.1481831178534776e-05), math.log(0.00020592732))), 5.1481831178534776e-05, 0.00020592732)
    log_temp = jnp.clip(jax.random.uniform(key_list[22], (1,), jnp.float32, -2.0, -0.5), -2.0, -0.5)
    log_temp_mom = jnp.clip(jax.random.uniform(key_list[23], (1,), jnp.float32, -0.05, 0.05), -0.05, 0.05)
    log_temp_sq = jnp.clip(jnp.exp(jax.random.uniform(key_list[24], (1,), jnp.float32, math.log(0.001), math.log(0.004))), 0.001, 0.004)
    return dict(states=states, actions=actions, rewards=rewards, next_states=next_states, terminal=terminal, valid_rows=valid_rows, noise_seeds=noise_seeds, member_live=member_live, critic_body=critic_body, critic_body_mom=critic_body_mom, critic_body_sq=critic_body_sq, critic_body_tgt=critic_body_tgt, critic_head=critic_head, critic_head_mom=critic_head_mom, critic_head_sq=critic_head_sq, critic_head_tgt=critic_head_tgt, policy_body=policy_body, policy_body_mom=policy_body_mom, policy_body_sq=policy_body_sq, policy_head=policy_head, policy_head_mom=policy_head_mom, policy_head_sq=policy_head_sq, log_temp=log_temp, log_temp_mom=log_temp_mom, log_temp_sq=log_temp_sq)


HIGHEST = lax.Precision.HIGHEST
DISCOUNT = 0.99
POLYAK_RATE = 0.005
ENTROPY_TARGET = -6.0
DIVERSITY_WEIGHT = 1.0
LEARN_RATE = 0.05
BETA_ONE = 0.5
BETA_TWO = 0.5
DECAY_RATE = 0.01
ADAM_EPSILON = 1e-08
GRAD_FLOOR = 0.0001
CLIP_NORM = 1.0
LOGSTD_LOW = -5.0
LOGSTD_HIGH = 2.0
LOG_TWO = 0.6931471805599453
HALF_LOG_TWOPI = 0.9189385332046727
FAR_VALUE = 1e+30

def matmul(inputs, weights):
    return jnp.dot(inputs, weights, precision=HIGHEST)

def hidden(weights, inputs, n_in):
    hid_width = weights.shape[1]
    hidden_act = jax.nn.silu(matmul(inputs, weights[:n_in]) + weights[n_in])
    offset = n_in + 1
    for layer_idx in range(2):
        hidden_act = jax.nn.silu(matmul(hidden_act, weights[offset:offset + hid_width]) + weights[offset + hid_width])
        offset = offset + hid_width + 1
    return hidden_act

def critic_q(body_w, head_w, inputs, action):
    joined = jnp.concatenate([inputs, action], axis=1)
    hidden_act = hidden(body_w, joined, joined.shape[1])
    hid_width = body_w.shape[1]
    return matmul(hidden_act, head_w[:hid_width]) + head_w[hid_width]

def critic_pair(body_w, head_w, inputs, action_in):
    q_vals, pull_back = jax.vjp(lambda action: critic_q(body_w, head_w, inputs, action), action_in)
    grad_a = pull_back(jnp.ones_like(q_vals))[0]
    return (q_vals, grad_a / jnp.sqrt(lax.optimization_barrier(jnp.sum(grad_a * grad_a, axis=1, keepdims=True)) + GRAD_FLOOR))

def noise_of(seed_col):
    index_k = jnp.arange(6, dtype=jnp.float32)
    return 1.7 * jnp.sin(0.618034 * seed_col.astype(jnp.float32)[:, None] + 2.39996 * index_k)

def policy(body_w, head_w, inputs, noise_draw):
    head_out = matmul(hidden(body_w, inputs, inputs.shape[1]), head_w[:-1]) + head_w[-1]
    split_at = head_out.shape[1] // 2
    mean_out = head_out[:, :split_at]
    log_std = LOGSTD_LOW + 0.5 * (LOGSTD_HIGH - LOGSTD_LOW) * (jnp.tanh(head_out[:, split_at:]) + 1.0)
    pre_tanh = mean_out + jnp.exp(log_std) * noise_draw
    squash = 2.0 * (LOG_TWO - pre_tanh - jax.nn.softplus(-2.0 * pre_tanh))
    log_prob = lax.optimization_barrier(jnp.sum(-0.5 * noise_draw * noise_draw - log_std - HALF_LOG_TWOPI - squash, axis=1))
    return (jnp.tanh(pre_tanh), log_prob)

def adam_step(weights, moment, second, grads):
    moment_new = BETA_ONE * moment + (1.0 - BETA_ONE) * grads
    second_new = BETA_TWO * second + (1.0 - BETA_TWO) * grads * grads
    corrected = moment_new / (1.0 - BETA_ONE ** STEPS_DONE)
    scale_sq = second_new / (1.0 - BETA_TWO ** STEPS_DONE)
    return (weights - LEARN_RATE * (corrected / (jnp.sqrt(scale_sq) + ADAM_EPSILON) + DECAY_RATE * weights), moment_new, second_new)

def reference(states, actions, rewards, next_states, terminal, valid_rows, noise_seeds, member_live, critic_body, critic_body_mom, critic_body_sq, critic_body_tgt, critic_head, critic_head_mom, critic_head_sq, critic_head_tgt, policy_body, policy_body_mom, policy_body_sq, policy_head, policy_head_mom, policy_head_sq, log_temp, log_temp_mom, log_temp_sq):
    noise_now = noise_of(noise_seeds[:, 0])
    noise_next = noise_of(noise_seeds[:, 1])
    temper = jnp.exp(log_temp[0])
    alive_slots = member_live.astype(jnp.float32)
    row_mask = valid_rows.astype(jnp.float32)
    carry_on = 1.0 - terminal.astype(jnp.float32)
    row_count = jnp.sum(row_mask)
    members = jnp.sum(alive_slots)
    action_next, log_prob_next = policy(policy_body, policy_head, next_states, noise_next)
    target_q = lax.map(lambda pieces: critic_q(pieces[0], pieces[1], next_states, action_next), (critic_body_tgt, critic_head_tgt))
    lowest = lax.optimization_barrier(jnp.min(jnp.where(alive_slots[:, None] > 0, target_q, FAR_VALUE), axis=0))
    target = rewards + DISCOUNT * carry_on * (lowest - temper * log_prob_next)

    def critic_loss(body_all, head_all):
        pair_fn = jax.checkpoint(lambda pieces: critic_pair(pieces[0], pieces[1], states, actions))
        q_values, unit_grads = lax.map(pair_fn, (body_all, head_all))
        bellman = jnp.sum(alive_slots[:, None] * row_mask[None, :] * (q_values - target) ** 2)
        unit_total = lax.optimization_barrier(jnp.sum(alive_slots[:, None, None] * unit_grads, axis=0))
        spread = jnp.sum(row_mask * (lax.optimization_barrier(jnp.sum(unit_total * unit_total, axis=1)) - members))
        return (bellman + DIVERSITY_WEIGHT / (members - 1.0) * spread, (bellman, spread))
    closs, pull_critic, critic_aux = jax.vjp(critic_loss, critic_body, critic_head, has_aux=True)
    grad_cbody, grad_chead = pull_critic(jnp.ones_like(closs))

    def actor_loss(body_w, head_w):
        action_now, log_prob = policy(body_w, head_w, states, noise_now)
        q_policy = lax.map(jax.checkpoint(lambda pieces: critic_q(pieces[0], pieces[1], states, action_now)), (critic_body, critic_head))
        q_mean = lax.optimization_barrier(jnp.sum(alive_slots[:, None] * q_policy, axis=0)) / members
        return (jnp.sum(row_mask * (temper * log_prob - q_mean)), log_prob)
    aloss, pull_actor, log_prob = jax.vjp(actor_loss, policy_body, policy_head, has_aux=True)
    grad_pbody, grad_phead = pull_actor(jnp.ones_like(aloss))
    entropy_sum = jnp.sum(row_mask * (log_prob + ENTROPY_TARGET))
    loss_parts = jnp.stack([critic_aux[0], critic_aux[1], aloss, -log_temp[0] * entropy_sum, row_count])
    grad_cbody = grad_cbody / row_count
    grad_chead = grad_chead / row_count
    grad_pbody = grad_pbody / row_count
    grad_phead = grad_phead / row_count
    grad_temp = -entropy_sum[None] / row_count
    total_sq = jnp.sum(grad_cbody * grad_cbody) + jnp.sum(grad_chead * grad_chead) + jnp.sum(grad_pbody * grad_pbody) + jnp.sum(grad_phead * grad_phead) + jnp.sum(grad_temp * grad_temp)
    norm_value = jnp.sqrt(total_sq)
    factor = CLIP_NORM / jnp.maximum(norm_value, CLIP_NORM)
    cb_new, cb_mom, cb_sq = adam_step(critic_body, critic_body_mom, critic_body_sq, factor * grad_cbody)
    ch_new, ch_mom, ch_sq = adam_step(critic_head, critic_head_mom, critic_head_sq, factor * grad_chead)
    pb_new, pb_mom, pb_sq = adam_step(policy_body, policy_body_mom, policy_body_sq, factor * grad_pbody)
    ph_new, ph_mom, ph_sq = adam_step(policy_head, policy_head_mom, policy_head_sq, factor * grad_phead)
    lt_new, lt_mom, lt_sq = adam_step(log_temp, log_temp_mom, log_temp_sq, factor * grad_temp)
    cb_tgt = (1.0 - POLYAK_RATE) * critic_body_tgt + POLYAK_RATE * cb_new
    ch_tgt = (1.0 - POLYAK_RATE) * critic_head_tgt + POLYAK_RATE * ch_new
    return (loss_parts, norm_value[None], cb_new, cb_mom, cb_sq, cb_tgt, cb_new.astype(jnp.bfloat16), ch_new, ch_mom, ch_sq, ch_tgt, ch_new.astype(jnp.bfloat16), pb_new, pb_mom, pb_sq, pb_new.astype(jnp.bfloat16), ph_new, ph_mom, ph_sq, ph_new.astype(jnp.bfloat16), lt_new, lt_mom, lt_sq)
```

```python
import functools

import jax
import jax.numpy as jnp
from jax import lax
from jax.experimental import pallas as pl
from jax.experimental.pallas import tpu as pltpu
from jax.sharding import PartitionSpec as P

STEPS_DONE = 5
DISCOUNT = 0.99
POLYAK_RATE = 0.005
ENTROPY_TARGET = -6.0
DIVERSITY_WEIGHT = 1.0
LEARN_RATE = 0.05
BETA_ONE = 0.5
BETA_TWO = 0.5
DECAY_RATE = 0.01
ADAM_EPSILON = 1e-08
GRAD_FLOOR = 0.0001
CLIP_NORM = 1.0
LOGSTD_LOW = -5.0
LOGSTD_HIGH = 2.0
LOG_TWO = 0.6931471805599453
HALF_LOG_TWOPI = 0.9189385332046727
FAR_VALUE = 1e30

F32 = jnp.float32
BF16 = jnp.bfloat16
HID = 256
S_DIM = 17
A_DIM = 6
ROW_TWO = 24
ROW_TWO_BIAS = 280
ROW_THREE = 288
ROW_THREE_BIAS = 544
CRITIC_ROWS = 552
POLICY_HEAD_ROW = 552
POLICY_ROWS = 576
VMEM = pl.BlockSpec(memory_space=pltpu.VMEM)
SMEM = pl.BlockSpec(memory_space=pltpu.SMEM)


def call(kernel, outs, in_specs, scratch=(), flops=0, moved=0):
    return pl.pallas_call(
        kernel,
        out_shape=outs,
        in_specs=in_specs,
        out_specs=jax.tree.map(lambda _: VMEM, outs),
        scratch_shapes=list(scratch),
        compiler_params=pltpu.CompilerParams(vmem_limit_bytes=50 * 2**20),
        cost_estimate=pl.CostEstimate(flops=flops, bytes_accessed=moved, transcendentals=0),
    )


def shape(*dims, dtype=F32):
    return jax.ShapeDtypeStruct(dims, dtype)


def dot(a, b):
    return lax.dot_general(a, b, (((1,), (0,)), ((), ())), preferred_element_type=F32)


def dot_rows(a, b):
    return lax.dot_general(a, b, (((1,), (1,)), ((), ())), preferred_element_type=F32)


def halves(w):
    high = w.astype(BF16)
    return high, (w - high.astype(F32)).astype(BF16)


def times(pair, h):
    return dot(pair[0], h) + dot(pair[1], h)


def times_exact(pair, h):
    high, low = halves(h)
    return dot(pair[0], high) + dot(pair[1], high) + dot(pair[0], low)


def stack_weights(w):
    high = w.astype(BF16).astype(F32)
    low = w - high
    return jnp.concatenate([high, high, low], axis=0).T.astype(BF16)


def stack_inputs(v):
    high = v.astype(BF16).astype(F32)
    return jnp.concatenate([high, v - high, high], axis=0).astype(BF16)


def sigmoid(z):
    return 0.5 * jnp.tanh(0.5 * z) + 0.5


def silu(z):
    return z * sigmoid(z)


def silu_slope(z):
    s = sigmoid(z)
    h = z * s
    return h, s + h - h * s


def silu_curve(z):
    s = sigmoid(z)
    h = z * s
    rest = 1.0 - s
    slope = s + h * rest
    return h, slope, s * rest * (2.0 + z - 2.0 * h)


def action_rows(v):
    k = lax.broadcasted_iota(jnp.int32, v.shape, 0)
    return jnp.where((k >= 1) & (k <= A_DIM), v, 0.0)


def row_at(v, k, like):
    return jnp.where(lax.broadcasted_iota(jnp.int32, like.shape, 0) == k, v, like)


def lane_row(block):
    return jnp.concatenate([block[i : i + 1] for i in range(block.shape[0])], axis=1)


def trunk_weights(body, n_in, forward=True, backward=False):
    out = {"one": stack_weights(body(0, n_in + 1))}
    second, third = n_in + 1, n_in + 2 + HID
    for name, start in (("two", second), ("three", third)):
        w = body(start, start + HID)
        if forward:
            high, low = halves(w)
            out[name] = (high.T, low.T)
            out[name + "_bias"] = body(start + HID, start + HID + 1).T
        if backward:
            out[name + "_back"] = halves(w)
    return out


def policy_head_weights(head):
    turned = head.T
    one = jnp.zeros((1, HID + 1), F32)
    spread = jnp.concatenate([one, turned[:A_DIM], one, one, turned[A_DIM:], one], axis=0)
    return halves(spread[:, :HID]), spread[:, HID:]


def policy_trunk(w, x, keep=False):
    z1 = dot(w["one"], stack_inputs(x))
    if keep:
        h1, d1 = silu_slope(z1)
    else:
        h1 = silu(z1)
    z2 = times(w["two"], h1.astype(BF16)) + w["two_bias"]
    if keep:
        h2, d2 = silu_slope(z2)
    else:
        h2 = silu(z2)
    z3 = times(w["three"], h2.astype(BF16)) + w["three_bias"]
    if keep:
        h3, d3 = silu_slope(z3)
        return (h1, h2, h3), (d1, d2, d3)
    return silu(z3)


def noise_of(seed_row, like_rows):
    k = lax.broadcasted_iota(jnp.int32, (8, seed_row.shape[1]), 0).astype(F32) - 1.0
    return 1.7 * jnp.sin(0.618034 * seed_row + 2.39996 * k)


def policy_out(head, bias, h3, noise):
    out = times_exact(head, h3) + bias
    mean, raw = out[:8], out[8:]
    turned = jnp.tanh(raw)
    log_std = LOGSTD_LOW + 0.5 * (LOGSTD_HIGH - LOGSTD_LOW) * (turned + 1.0)
    spread = jnp.exp(log_std) * noise
    u = mean + spread
    soft = jnp.maximum(-2.0 * u, 0.0) + jnp.log(1.0 + jnp.exp(-jnp.abs(2.0 * u)))
    squash = 2.0 * (LOG_TWO - u - soft)
    terms = -0.5 * noise * noise - log_std - HALF_LOG_TWOPI - squash
    log_prob = jnp.sum(action_rows(terms), axis=0, keepdims=True)
    return jnp.tanh(u), turned, spread, log_prob


def actor_kernel(
    states, actions, next_states, seeds, rewards, terminal, valid, body, head, log_temp, xs, xn, xp, aux
):
    rows = states.shape[0]
    st, at, nt = states[...].T, actions[...].T, next_states[...].T
    ones = jnp.ones((1, rows), F32)
    xs[...] = jnp.concatenate([st, at, ones], axis=0)
    seed = seeds[...].astype(F32).T
    w = trunk_weights(lambda a, b: body[a:b], S_DIM)
    head_w, head_b = policy_head_weights(head[...])
    mask = lane_row(valid[...].astype(F32))
    carry = 1.0 - lane_row(terminal[...].astype(F32))
    temper = jnp.exp(log_temp[0])
    h3 = policy_trunk(w, jnp.concatenate([nt, ones], axis=0))
    action, _, _, log_prob = policy_out(head_w, head_b, h3, noise_of(seed[1:2], 8))
    xn[...] = jnp.concatenate([nt, action[1 : 1 + A_DIM], ones], axis=0)
    aux[0:1, :] = lane_row(rewards[...]) - DISCOUNT * carry * temper * log_prob
    aux[1:2, :] = DISCOUNT * carry
    aux[2:3, :] = mask
    noise = noise_of(seed[0:1], 8)
    h3 = policy_trunk(w, jnp.concatenate([st, ones], axis=0))
    action, turned, spread, log_prob = policy_out(head_w, head_b, h3, noise)
    xp[...] = jnp.concatenate([st, action[1 : 1 + A_DIM], ones], axis=0)
    aux[3:4, :] = log_prob
    aux[4:8, :] = jnp.zeros((4, rows), F32)
    aux[8:16, :] = action_rows(action)
    aux[16:24, :] = action_rows(turned)
    aux[24:32, :] = action_rows(spread)


def critic_forward(w, x, exact=False, single=False):
    z1 = dot(w["one"], stack_inputs(x))
    h1, d1 = silu_slope(z1)
    if exact:
        z2 = times_exact(w["two"], h1) + w["two_bias"]
    elif single:
        z2 = dot(w["two"][0], h1.astype(BF16)) + w["two_bias"]
    else:
        z2 = times(w["two"], h1.astype(BF16)) + w["two_bias"]
    h2, d2 = silu_slope(z2)
    if exact:
        z3 = times_exact(w["three"], h2) + w["three_bias"]
    elif single:
        z3 = dot(w["three"][0], h2.astype(BF16)) + w["three_bias"]
    else:
        z3 = times(w["three"], h2.astype(BF16)) + w["three_bias"]
    h3, d3 = silu_slope(z3)
    return h3, (d1, d2, d3)


def critic_value(w, x):
    h1 = silu(dot(w["one"], stack_inputs(x)))
    h2 = silu(times(w["two"], h1.astype(BF16)) + w["two_bias"])
    return silu(times(w["three"], h2.astype(BF16)) + w["three_bias"])


def head_column(head):
    return head[:, :HID].T, head[:, HID:]


def critic_kernel(live, xs, xn, xp, body, head, body_tgt, head_tgt, out):
    total_n = total_g = total_q = lowest = count = None
    for c in range(2):
        alive = live[c].astype(F32)
        w = trunk_weights(lambda a, b: body[c, a:b], S_DIM + A_DIM, backward=True)
        column, last = head_column(head[c : c + 1])
        inner = halves(body[c, 16:24])
        _, (d1, d2, d3) = critic_forward(w, xs[...], exact=True)
        b2 = times(w["three_back"], (column * d3).astype(BF16)) * d2
        b1 = times(w["two_back"], b2.astype(BF16)) * d1
        grad = action_rows(times(inner, b1.astype(BF16)))
        size = jnp.sum(grad * grad, axis=0, keepdims=True) + GRAD_FLOOR
        unit = grad * (alive * lax.rsqrt(size))
        wt = trunk_weights(lambda a, b: body_tgt[c, a:b], S_DIM + A_DIM)
        column_t, last_t = head_column(head_tgt[c : c + 1])
        h3 = critic_value(wt, xn[...])
        value = jnp.sum(column_t * h3, axis=0, keepdims=True) + last_t
        value = jnp.where(alive > 0, value, FAR_VALUE)
        h3, (d1, d2, d3) = critic_forward(w, xp[...], single=True)
        q = jnp.sum(column * h3, axis=0, keepdims=True) + last
        b2 = dot(w["three_back"][0], (column * d3).astype(BF16)) * d2
        b1 = dot(w["two_back"][0], b2.astype(BF16)) * d1
        grad = action_rows(times(inner, b1.astype(BF16))) * alive
        q = q * alive
        if c == 0:
            total_n, total_g, total_q, lowest, count = unit, grad, q, value, alive
        else:
            total_n, total_g, total_q = total_n + unit, total_g + grad, total_q + q
            lowest, count = jnp.minimum(lowest, value), count + alive
    out[0:8, :] = row_at(lowest, 7, row_at(count, 0, total_n))
    out[8:16, :] = row_at(total_q, 0, total_g)


def merge(a, b):
    k = lax.broadcasted_iota(jnp.int32, a.shape, 0)
    return jnp.where(k == 7, jnp.minimum(a, b), a + b)


def joint_kernel(mine, other, aux, log_temp, place, sx, gx, sums):
    both = merge(mine[...], other[...])
    unit, grad = both[:8], both[8:]
    mask, log_prob = aux[2:3, :], aux[3:4, :]
    members = both[0:1]
    target = aux[0:1, :] + aux[1:2, :] * both[7:8]
    unit = action_rows(unit)
    sx[...] = row_at(target, 7, row_at(mask, 0, mask * unit))
    gx[...] = row_at(members, 7, grad)
    temper = jnp.exp(log_temp[0])
    spread = jnp.sum(mask * (jnp.sum(unit * unit, axis=0, keepdims=True) - members), axis=1, keepdims=True)
    actor = jnp.sum(mask * (temper * log_prob - both[8:9] / members), axis=1, keepdims=True)
    entropy = jnp.sum(mask * (log_prob + ENTROPY_TARGET), axis=1, keepdims=True)
    count = jnp.sum(mask, axis=1, keepdims=True)
    first = (place[0] == 0).astype(F32)
    lane = lax.broadcasted_iota(jnp.int32, (1, 128), 1)
    row = jnp.where(lane == 1, spread, 0.0) + jnp.where(lane == 2, actor, 0.0)
    row = row + jnp.where(lane == 3, entropy, 0.0) + jnp.where(lane == 4, count, 0.0)
    sums[...] = row * first


def policy_kernel(place, xs, aux, gx, body, head, log_temp, keep, give, full):
    rows = xs.shape[1]
    n = S_DIM
    w = trunk_weights(lambda a, b: body[a:b], n, backward=True)
    (head_high, head_low), _ = policy_head_weights(head[...])
    x = row_at(1.0, n, xs[0:24, :])
    (h1, h2, h3), (d1, d2, d3) = policy_trunk(w, x[: n + 1], keep=True)
    mask, members = aux[2:3, :], gx[7:8, :]
    action, turned, spread = aux[8:16, :], aux[16:24, :], aux[24:32, :]
    temper = jnp.exp(log_temp[0])
    by_action = -(mask / members) * action_rows(gx[...])
    by_log = temper * mask
    by_u = by_action * (1.0 - action * action) + by_log * 2.0 * action
    by_std = by_u * spread - by_log
    by_raw = action_rows(by_std * (0.5 * (LOGSTD_HIGH - LOGSTD_LOW)) * (1.0 - turned * turned))
    by_out = jnp.concatenate([action_rows(by_u), by_raw], axis=0)
    out_high, out_low = halves(by_out)
    head_back = jnp.concatenate([head_high, head_high, head_low], axis=0).astype(F32).T.astype(BF16)
    f3 = dot(head_back, jnp.concatenate([out_high, out_low, out_high], axis=0)) * d3
    f2 = times(w["three_back"], f3.astype(BF16)) * d2
    f1 = times(w["two_back"], f2.astype(BF16)) * d1
    ones = row_at(1.0, 0, jnp.zeros((16, rows), F32)).astype(BF16)
    h1, h2, h3 = h1.astype(BF16), h2.astype(BF16), h3.astype(BF16)
    f1, f2, f3 = f1.astype(BF16), f2.astype(BF16), f3.astype(BF16)
    low = jnp.where(lax.broadcasted_iota(jnp.int32, x.shape, 0) <= n, x, 0.0).astype(BF16)
    full[0:ROW_TWO, :] = dot_rows(low, f1)
    full[ROW_TWO:ROW_TWO_BIAS, :] = dot_rows(h1, f2)
    full[ROW_TWO_BIAS:ROW_THREE, :] = dot_rows(ones, f2)[:8]
    full[ROW_THREE:ROW_THREE_BIAS, :] = dot_rows(h2, f3)
    bias = dot_rows(ones, f3)[:8]
    last = dot_rows(ones, out_high) + dot_rows(ones, out_low)
    last = jnp.concatenate([last[:8], jnp.zeros((8, HID - 16), F32)], axis=1)
    last = jnp.concatenate([jnp.zeros((1, HID), F32), last[:7]], axis=0)
    full[ROW_THREE_BIAS:POLICY_HEAD_ROW, :] = bias + last
    full[POLICY_HEAD_ROW : POLICY_HEAD_ROW + 16, :] = dot_rows(out_high, h3) + dot_rows(out_low, h3)
    full[POLICY_HEAD_ROW + 16 :, :] = jnp.zeros((full.shape[0] - POLICY_HEAD_ROW - 16, HID), F32)
    part = keep.shape[0]
    mine = place[0] * 2 + place[1]
    theirs = place[0] * 2 + 1 - place[1]
    keep[...] = full[pl.ds(pl.multiple_of(mine * part, 8), part), :]
    give[...] = full[pl.ds(pl.multiple_of(theirs * part, 8), part), :]


def second_kernel(live, place, xs, xs_far, sx, sx_far, gx, body, head, grads, sums, left3, right3, left2, right2, left1, right1, lefth, righth):
    rows = xs.shape[1]
    mine = place[1]
    alive = jnp.where(mine == 0, live[0], live[1]).astype(F32)
    w = trunk_weights(lambda a, b: body[mine, a:b], S_DIM + A_DIM, backward=True)
    column, last = head_column(head[pl.ds(mine, 1), :])
    inner = halves(body[mine, 16:24])
    inner_stack = stack_weights(body[mine, 16:24])
    members = gx[7:8, :]
    weight = 2.0 * DIVERSITY_WEIGHT * alive / (members - 1.0)
    td = jnp.zeros((1, 1), F32)
    bias_sum = jnp.zeros((1, 1), F32)
    one_row = row_at(1.0, 0, jnp.zeros((16, rows), F32))
    none = jnp.zeros((16, rows), BF16)
    for part, (x_ref, s_ref) in enumerate(((xs, sx), (xs_far, sx_far))):
        here = slice(2 * part * rows, (2 * part + 1) * rows)
        there = slice((2 * part + 1) * rows, (2 * part + 2) * rows)
        x = x_ref[...]
        mask, target = s_ref[0:1, :], s_ref[7:8, :]
        z1 = dot(w["one"], stack_inputs(x))
        h1, d1, e1 = silu_curve(z1)
        z2 = times_exact(w["two"], h1) + w["two_bias"]
        h2, d2, e2 = silu_curve(z2)
        z3 = times_exact(w["three"], h2) + w["three_bias"]
        h3, d3, e3 = silu_curve(z3)
        q = jnp.sum(column * h3, axis=0, keepdims=True) + last
        b3 = column * d3
        c2 = times(w["three_back"], b3.astype(BF16))
        b2 = c2 * d2
        c1 = times(w["two_back"], b2.astype(BF16))
        b1 = c1 * d1
        grad = action_rows(times(inner, b1.astype(BF16)))
        size = jnp.sum(grad * grad, axis=0, keepdims=True) + GRAD_FLOOR
        turn = lax.rsqrt(size)
        cot = action_rows(s_ref[...]) * weight
        along = jnp.sum(grad * cot, axis=0, keepdims=True)
        v = turn * (cot - grad * (along / size))
        miss = q - target
        a = 2.0 * alive * mask * miss
        td = td + jnp.sum(alive * mask * miss * miss, axis=1, keepdims=True)
        bias_sum = bias_sum + jnp.sum(a, axis=1, keepdims=True)
        t1 = dot(inner_stack, stack_inputs(v))
        g1 = d1 * t1
        t2 = times(w["two"], g1.astype(BF16))
        g2 = d2 * t2
        t3 = times(w["three"], g2.astype(BF16))
        g3 = d3 * t3
        r3 = column * e3 * t3
        r2 = dot(w["three_back"][0], r3.astype(BF16)) * d2 + c2 * e2 * t2
        r1 = dot(w["two_back"][0], r2.astype(BF16)) * d1 + c1 * e1 * t1
        left3[0:HID, here] = h2.astype(BF16)
        left3[HID : HID + 16, here] = one_row.astype(BF16)
        left3[0:HID, there] = g2.astype(BF16)
        left3[HID : HID + 16, there] = none
        right3[:, here] = (a * b3 + r3).astype(BF16)
        right3[:, there] = b3.astype(BF16)
        left2[0:HID, here] = h1.astype(BF16)
        left2[HID : HID + 16, here] = one_row.astype(BF16)
        left2[0:HID, there] = g1.astype(BF16)
        left2[HID : HID + 16, there] = none
        right2[:, here] = (a * b2 + r2).astype(BF16)
        right2[:, there] = b2.astype(BF16)
        left1[:, here] = jnp.concatenate([x, jnp.zeros((8, rows), F32)], axis=0).astype(BF16)
        left1[:, there] = jnp.concatenate([jnp.zeros((16, rows), F32), v, jnp.zeros((8, rows), F32)], axis=0).astype(BF16)
        right1[:, here] = (a * b1 + r1).astype(BF16)
        right1[:, there] = b1.astype(BF16)
        a_high = a.astype(BF16).astype(F32)
        lefth[:, here] = row_at(a_high, 0, row_at(a - a_high, 1, jnp.zeros((16, rows), F32))).astype(BF16)
        lefth[:, there] = one_row.astype(BF16)
        righth[:, here] = h3.astype(BF16)
        righth[:, there] = g3.astype(BF16)
    total3 = dot_rows(left3[...], right3[...])
    total2 = dot_rows(left2[...], right2[...])
    total1 = dot_rows(left1[...], right1[...])
    totalh = dot_rows(lefth[...], righth[...])
    head_w = totalh[0:1] + totalh[1:2]
    grads[0:ROW_TWO, :] = total1[0:ROW_TWO]
    grads[ROW_TWO:ROW_THREE, :] = total2[0 : HID + 8]
    tail = total3[HID : HID + 8]
    tail = row_at(head_w, 1, tail)
    lane = lax.broadcasted_iota(jnp.int32, (1, HID), 1)
    tail = row_at(jnp.where(lane == 0, bias_sum, 0.0), 2, tail)
    grads[ROW_THREE:ROW_THREE_BIAS, :] = total3[0:HID]
    grads[ROW_THREE_BIAS:CRITIC_ROWS, :] = tail
    if grads.shape[0] > CRITIC_ROWS:
        grads[CRITIC_ROWS:, :] = jnp.zeros((grads.shape[0] - CRITIC_ROWS, HID), F32)
    sums[...] = jnp.where(lax.broadcasted_iota(jnp.int32, (1, 128), 1) == 0, td, 0.0)


def deal_kernel(place, critic, keep, got, *out):
    n = len(out)
    part, small = critic.shape[0] // n, keep.shape[0] // n
    for k in range(n):
        to = lax.rem(place[2] + k, n)
        out[k][0:part, :] = critic[pl.ds(pl.multiple_of(to * part, 8), part), :]
        here = pl.ds(pl.multiple_of(to * small, 8), small)
        out[k][part:, :] = keep[here, :] + got[here, :]


def reduce_kernel(part, one, two, *refs):
    ins, (out, sums) = refs[:-2], refs[-2:]
    total = ins[0][...]
    for r in ins[1:]:
        total = total + r[...]
    out[...] = total
    square = jnp.sum(jnp.sum(total * total, axis=0, keepdims=True), axis=1, keepdims=True)
    lane = lax.broadcasted_iota(jnp.int32, (1, 128), 1)
    row = one[...] + two[...] + jnp.where(lane == 5, square, 0.0)
    sums[...] = jnp.broadcast_to(row, sums.shape)


def adam(weights, moment, second, grads):
    moment_new = BETA_ONE * moment + (1.0 - BETA_ONE) * grads
    second_new = BETA_TWO * second + (1.0 - BETA_TWO) * grads * grads
    corrected = moment_new * (1.0 / (1.0 - BETA_ONE**STEPS_DONE))
    scale_sq = second_new * (1.0 / (1.0 - BETA_TWO**STEPS_DONE))
    step = corrected / (jnp.sqrt(scale_sq) + ADAM_EPSILON) + DECAY_RATE * weights
    return weights - LEARN_RATE * step, moment_new, second_new


def pool_kernel(place, n_z, part, small, *refs):
    pass


def place_critics(place, n_z, part, pieces, sources, total):
    for piece, (dx, dz) in zip(pieces, sources):
        c = lax.rem(place[1] + dx, 2)
        z = lax.rem(place[2] + dz, n_z)
        total[c, pl.ds(pl.multiple_of(z * part, 8), part), :] = piece[0:part, :]


def gather_policy_kernel(n_z, part, small, sources, place, *refs):
    pieces, out = refs[:-1], refs[-1]
    for piece, (dx, dz) in zip(pieces, sources):
        x = lax.rem(place[1] + dx, 2)
        z = lax.rem(place[2] + dz, n_z)
        out[pl.ds(pl.multiple_of((x * n_z + z) * small, 8), small), :] = piece[part:, :]


def scalars_of(sums, log_temp):
    total = jnp.sum(sums[...], axis=0, keepdims=True)
    entropy, count = total[:, 3:4], total[:, 4:5]
    grad_temp = -entropy / count
    norm = jnp.sqrt(total[:, 5:6] / (count * count) + grad_temp * grad_temp)
    factor = CLIP_NORM / jnp.maximum(norm, CLIP_NORM)
    return total, entropy, count, grad_temp, norm, factor


def put(refs, at, got, extra=None):
    for r, value in zip(refs, got):
        r[at] = value.astype(r.dtype)


def critic_update_kernel(n_z, part, sources, place, log_temp, sums, *refs):
    pieces = refs[: len(sources)]
    (w, m, v, t, hw, hm, hv, ht, w_o, m_o, v_o, t_o, half_o, hw_o, hm_o, hv_o, ht_o, hhalf_o, total) = refs[len(sources) :]
    place_critics(place, n_z, part, pieces, sources, total)
    _, _, count, _, _, factor = scalars_of(sums, log_temp)
    scale = factor / count
    for c in range(2):
        for mine, rows in ((slice(0, ROW_TWO_BIAS + 1), slice(0, ROW_TWO_BIAS + 1)), (slice(ROW_THREE, ROW_THREE_BIAS + 1), slice(ROW_TWO_BIAS + 1, 538))):
            at = (c, rows)
            new, mom, sq = adam(w[at], m[at], v[at], total[c, mine, :] * scale)
            tgt = (1.0 - POLYAK_RATE) * t[at] + POLYAK_RATE * new
            put((w_o, m_o, v_o, t_o, half_o), at, (new, mom, sq, tgt, new))
        for mine, lanes in (
            ((c, slice(ROW_THREE_BIAS + 1, ROW_THREE_BIAS + 2), slice(0, HID)), slice(0, HID)),
            ((c, slice(ROW_THREE_BIAS + 2, ROW_THREE_BIAS + 3), slice(0, 1)), slice(HID, HID + 1)),
        ):
            at = (slice(c, c + 1), lanes)
            new, mom, sq = adam(hw[at], hm[at], hv[at], total[mine] * scale)
            tgt = (1.0 - POLYAK_RATE) * ht[at] + POLYAK_RATE * new
            put((hw_o, hm_o, hv_o, ht_o, hhalf_o), at, (new, mom, sq, tgt, new))


def policy_update_kernel(places, block, place, log_temp, log_mom, log_sq, sums, *refs):
    pieces = refs[: len(places)]
    (w, m, v, hw, hm, hv, w_o, m_o, v_o, half_o, hw_o, hm_o, hv_o, hhalf_o, loss, norm_o, lt_o, lm_o, ls_o, total) = refs[len(places) :]
    for piece, dm in zip(pieces, places):
        at = jnp.bitwise_xor(place[0], dm) * block
        total[pl.ds(pl.multiple_of(at, 8), block), :] = piece[...]
    row, entropy, count, grad_temp, norm, factor = scalars_of(sums, log_temp)
    scale = factor / count
    n = S_DIM
    for mine, rows in (
        (slice(0, n + 1), slice(0, n + 1)),
        (slice(ROW_TWO, ROW_TWO_BIAS + 1), slice(n + 1, n + 2 + HID)),
        (slice(ROW_THREE, ROW_THREE_BIAS + 1), slice(n + 2 + HID, n + 3 + 2 * HID)),
    ):
        new, mom, sq = adam(w[rows], m[rows], v[rows], total[mine, :] * scale)
        put((w_o, m_o, v_o, half_o), (rows,), (new, mom, sq, new))
    by_head = total[POLICY_HEAD_ROW : POLICY_HEAD_ROW + 16, :].T
    by_head = jnp.concatenate([by_head[:, 1 : 1 + A_DIM], by_head[:, 9 : 9 + A_DIM]], axis=1)
    by_last = total[ROW_THREE_BIAS + 1 : ROW_THREE_BIAS + 2, 0:16]
    by_last = jnp.concatenate([by_last[:, 1 : 1 + A_DIM], by_last[:, 9 : 9 + A_DIM]], axis=1)
    for rows, g in ((slice(0, HID), by_head), (slice(HID, HID + 1), by_last)):
        new, mom, sq = adam(hw[rows], hm[rows], hv[rows], g * scale)
        put((hw_o, hm_o, hv_o, hhalf_o), (rows,), (new, mom, sq, new))
    lane = lax.broadcasted_iota(jnp.int32, (1, 128), 1)
    loss[...] = jnp.where(lane == 3, -log_temp[0] * entropy, row)
    norm_o[...] = jnp.broadcast_to(norm, (1, 128))
    new, mom, sq = adam(
        jnp.full((1, 128), log_temp[0]), jnp.full((1, 128), log_mom[0]), jnp.full((1, 128), log_sq[0]), factor * grad_temp
    )
    put((lt_o, lm_o, ls_o), (slice(0, 1),), (new, mom, sq))


def per_device(
    members,
    dp,
    states,
    actions,
    rewards,
    next_states,
    terminal,
    valid_rows,
    noise_seeds,
    member_live,
    critic_body,
    critic_body_mom,
    critic_body_sq,
    critic_body_tgt,
    critic_head,
    critic_head_mom,
    critic_head_sq,
    critic_head_tgt,
    policy_body,
    policy_body_mom,
    policy_body_sq,
    policy_head,
    policy_head_mom,
    policy_head_sq,
    log_temp,
    log_temp_mom,
    log_temp_sq,
):
    rows = states.shape[0]
    n_z = dp // 2
    part = -(-CRITIC_ROWS // (8 * n_z)) * 8
    small = -(-POLICY_ROWS // (8 * members * dp)) * 8
    m, d = lax.axis_index("member"), lax.axis_index("dp")
    place = jnp.stack([m, d % 2, d // 2]).astype(jnp.int32)

    def across(value, axis, n, to):
        return lax.ppermute(value, axis, [(i, to(i)) for i in range(n)])

    def to_member(value, bit):
        return across(value, "member", members, lambda i: i ^ bit)

    def to_pair(value):
        return across(value, "dp", dp, lambda i: i ^ 1)

    def along(value, step):
        return across(value, "dp", dp, lambda i: (i + 2 * step) % dp)

    square = lambda v: v.reshape(rows // 128, 128)
    xs, xn, xp, aux = call(
        actor_kernel,
        [shape(24, rows), shape(24, rows), shape(24, rows), shape(32, rows)],
        [VMEM] * 9 + [SMEM],
    )(
        states, actions, next_states, noise_seeds, square(rewards), square(terminal), square(valid_rows),
        policy_body, policy_head, log_temp,
    )
    xs_far = to_pair(xs)
    ensemble = call(critic_kernel, shape(16, rows), [SMEM] + [VMEM] * 7)(
        member_live, xs, xn, xp, critic_body, critic_head, critic_body_tgt, critic_head_tgt
    )
    bit = 1
    while bit * 2 < members:
        other = to_member(ensemble, bit)
        k = lax.broadcasted_iota(jnp.int32, ensemble.shape, 0)
        ensemble = jnp.where(k == 7, jnp.minimum(ensemble, other), ensemble + other)
        bit *= 2
    sx, gx, sums_joint = call(
        joint_kernel, [shape(8, rows), shape(8, rows), shape(1, 128)], [VMEM, VMEM, VMEM, SMEM, SMEM]
    )(ensemble, to_member(ensemble, bit), aux, log_temp, place)
    sx_far = to_pair(sx)
    eighth = small * n_z
    keep, give = call(
        policy_kernel,
        [shape(eighth, HID), shape(eighth, HID)],
        [SMEM] + [VMEM] * 5 + [SMEM],
        [pltpu.VMEM((2 * members * eighth, HID), F32)],
    )(place, xs, aux, gx, policy_body, policy_head, log_temp)
    got = to_pair(give)
    wide = 4 * rows
    grads, sums_second = call(
        second_kernel,
        [shape(part * n_z, HID), shape(1, 128)],
        [SMEM, SMEM] + [VMEM] * 7,
        [
            pltpu.VMEM((HID + 16, wide), BF16),
            pltpu.VMEM((HID, wide), BF16),
            pltpu.VMEM((HID + 16, wide), BF16),
            pltpu.VMEM((HID, wide), BF16),
            pltpu.VMEM((32, wide), BF16),
            pltpu.VMEM((HID, wide), BF16),
            pltpu.VMEM((16, wide), BF16),
            pltpu.VMEM((HID, wide), BF16),
        ],
    )(member_live, place, xs, xs_far, sx, sx_far, gx, critic_body, critic_head)
    message = shape(part + small, HID)
    dealt = call(deal_kernel, [message] * n_z, [SMEM, VMEM, VMEM, VMEM])(place, grads, keep, got)
    arrived = [dealt[0]] + [along(dealt[k], k) for k in range(1, n_z)]
    piece, sums = call(
        functools.partial(reduce_kernel, part),
        [message, shape(members * dp, 128)],
        [VMEM] * (2 + n_z),
    )(sums_joint, sums_second, *arrived)
    sums = lax.all_to_all(sums, ("member", "dp"), 0, 0, tiled=True)
    pieces = [piece] + [along(piece, k) for k in range(1, n_z)]
    sources = [(0, (n_z - k) % n_z) for k in range(n_z)]
    pieces = pieces + [to_pair(p) for p in pieces]
    sources = sources + [(1, z) for _, z in sources]
    block = 2 * eighth
    quarter = call(
        functools.partial(gather_policy_kernel, n_z, part, small, sources), shape(block, HID), [SMEM] + [VMEM] * len(pieces)
    )(place, *pieces)
    blocks, places, bit = [quarter], [0], 1
    while bit < members:
        blocks = blocks + [to_member(b, bit) for b in blocks]
        places = places + [p | bit for p in places]
        bit *= 2
    like = lambda *arrays: [shape(*a.shape, dtype=a.dtype) for a in arrays]
    halved = lambda a: shape(*a.shape, dtype=BF16)
    cb_new, cb_mom, cb_sq, cb_tgt, cb_half, ch_new, ch_mom, ch_sq, ch_tgt, ch_half = call(
        functools.partial(critic_update_kernel, n_z, part, sources),
        like(critic_body, critic_body, critic_body, critic_body)
        + [halved(critic_body)]
        + like(critic_head, critic_head, critic_head, critic_head)
        + [halved(critic_head)],
        [SMEM, SMEM] + [VMEM] * (1 + len(pieces) + 8),
        [pltpu.VMEM((2, n_z * part, HID), F32)],
    )(
        place, log_temp, sums, *pieces, critic_body, critic_body_mom, critic_body_sq, critic_body_tgt,
        critic_head, critic_head_mom, critic_head_sq, critic_head_tgt,
    )
    line = shape(1, 128)
    (pb_new, pb_mom, pb_sq, pb_half, ph_new, ph_mom, ph_sq, ph_half, loss, norm, lt_new, lt_mom, lt_sq) = call(
        functools.partial(policy_update_kernel, places, block),
        like(policy_body, policy_body, policy_body)
        + [halved(policy_body)]
        + like(policy_head, policy_head, policy_head)
        + [halved(policy_head), line, line, line, line, line],
        [SMEM] * 4 + [VMEM] * (1 + len(blocks) + 6),
        [pltpu.VMEM((members * block, HID), F32)],
    )(
        place, log_temp, log_temp_mom, log_temp_sq, sums, *blocks, policy_body, policy_body_mom, policy_body_sq,
        policy_head, policy_head_mom, policy_head_sq,
    )
    return (
        loss[0, :5], norm[0, :1], cb_new, cb_mom, cb_sq, cb_tgt, cb_half, ch_new, ch_mom, ch_sq, ch_tgt, ch_half,
        pb_new, pb_mom, pb_sq, pb_half, ph_new, ph_mom, ph_sq, ph_half, lt_new[0, :1], lt_mom[0, :1], lt_sq[0, :1],
    )


def solution(mesh):
    row, line = P("dp", None), P("dp")
    stack, flat = P("member", None, None), P("member", None)
    return jax.shard_map(
        functools.partial(per_device, mesh.shape["member"], mesh.shape["dp"]),
        mesh=mesh,
        in_specs=(row, row, line, row, line, line, row, P("member")) + (stack,) * 4 + (flat,) * 4 + (P(),) * 9,
        out_specs=(P(), P()) + (stack,) * 5 + (flat,) * 5 + (P(),) * 11,
        check_vma=False,
    )
```

```python
import functools

import jax
import jax.numpy as jnp
from jax import lax
from jax.experimental import pallas as pl
from jax.experimental.pallas import tpu as pltpu
from jax.sharding import PartitionSpec as P

STEPS_DONE = 5
DISCOUNT = 0.99
POLYAK_RATE = 0.005
ENTROPY_TARGET = -6.0
DIVERSITY_WEIGHT = 1.0
LEARN_RATE = 0.05
BETA_ONE = 0.5
BETA_TWO = 0.5
DECAY_RATE = 0.01
ADAM_EPSILON = 1e-08
GRAD_FLOOR = 0.0001
CLIP_NORM = 1.0
LOGSTD_LOW = -5.0
LOGSTD_HIGH = 2.0
LOG_TWO = 0.6931471805599453
HALF_LOG_TWOPI = 0.9189385332046727
FAR_VALUE = 1e30

F32 = jnp.float32
BF16 = jnp.bfloat16
HID = 256
S_DIM = 17
A_DIM = 6
X_DIM = S_DIM + A_DIM
TWO = X_DIM + 1
THREE = TWO + HID + 1
BODY = THREE + HID + 1
CRITIC_ROWS = 544
P_TWO = 24
P_THREE = 288
P_LAST = 544
P_HEAD = 552
POLICY_ROWS = 576
VMEM = pl.BlockSpec(memory_space=pltpu.VMEM)
SMEM = pl.BlockSpec(memory_space=pltpu.SMEM)
HBM = pl.BlockSpec(memory_space=pltpu.HBM)


def call(kernel, outs, in_specs, scratch=(), us=1.0, out_specs=None, limit=32):
    return pl.pallas_call(
        kernel,
        out_shape=outs,
        in_specs=in_specs,
        out_specs=out_specs or jax.tree.map(lambda _: VMEM, outs),
        scratch_shapes=list(scratch),
        compiler_params=pltpu.CompilerParams(vmem_limit_bytes=limit * 2**20),
        cost_estimate=pl.CostEstimate(flops=int(us * 1.15e9), bytes_accessed=0, transcendentals=0),
    )


def buffers(*arrays):
    return [pltpu.VMEM(a.shape, a.dtype) for a in arrays] + [pltpu.SemaphoreType.DMA((len(arrays),))]


def start_copies(sources, targets, sem):
    copies = [pltpu.make_async_copy(a, b, sem.at[i]) for i, (a, b) in enumerate(zip(sources, targets))]
    for copy in copies:
        copy.start()
    return copies


def shape(*dims, dtype=F32):
    return jax.ShapeDtypeStruct(dims, dtype)


def dot(a, b):
    return lax.dot_general(a, b, (((1,), (0,)), ((), ())), preferred_element_type=F32)


def dot_rows(a, b):
    return lax.dot_general(a, b, (((1,), (1,)), ((), ())), preferred_element_type=F32)


def halves(w):
    high = w.astype(BF16)
    return high, (w - high.astype(F32)).astype(BF16)


def stack_weights(w):
    high = (0.5 * w).astype(BF16).astype(F32)
    return jnp.concatenate([high, high, 0.5 * w - high], axis=0).T.astype(BF16)


def stack_inputs(v):
    high = v.astype(BF16).astype(F32)
    return jnp.concatenate([high, v - high, high], axis=0).astype(BF16)


def act(z):
    t = jnp.tanh(z)
    return z + z * t, t


def slope(h, t):
    return (1.0 + h) + t * (1.0 - h)


def curve(z, t):
    return (1.0 - t * t) * (1.0 - z * t)


def wide(column):
    return jnp.broadcast_to(column, (column.shape[0], 128))


def spread(column, rows):
    return jnp.concatenate([column] * (rows // 128), axis=1)


def action_rows(v):
    k = lax.broadcasted_iota(jnp.int32, v.shape, 0)
    return jnp.where((k >= 1) & (k <= A_DIM), v, 0.0)


def row_at(v, k, like):
    return jnp.where(lax.broadcasted_iota(jnp.int32, like.shape, 0) == k, v, like)


def lane_row(block):
    return jnp.concatenate([block[i : i + 1] for i in range(block.shape[0])], axis=1)


def interleave(*streams):
    results, active = [None] * len(streams), list(enumerate(streams))
    while active:
        left = []
        for i, stream in active:
            try:
                next(stream)
                left.append((i, stream))
            except StopIteration as end:
                results[i] = end.value
        active = left
    return results


def critic_rows(ref, c):
    def read(a, b):
        return jnp.concatenate([ref[pl.ds(4 * a + 2 * t + c, b - a, stride=4), :] for t in range(2)], axis=1)

    return read


def load_trunk(body, n_in, one, mats, bias, i, backward=False):
    one[i] = stack_weights(body(0, n_in + 1))
    for k, start in enumerate((n_in + 1, n_in + 2 + HID)):
        high, low = halves(0.5 * body(start, start + HID))
        mats[i, 4 * k] = high.T
        mats[i, 4 * k + 1] = low.T
        if backward:
            mats[i, 4 * k + 2] = high
            mats[i, 4 * k + 3] = low
        bias[i, k] = wide(0.5 * body(start + HID, start + HID + 1).T)


def trunk_scratch(n, n_in):
    return [pltpu.VMEM((n, HID, 3 * (n_in + 1)), BF16), pltpu.VMEM((n, 8, HID, HID), BF16), pltpu.VMEM((n, 2, HID, 128), F32)]


def times(w, k, h):
    mats, i = w
    return dot(mats[i, k], h) + dot(mats[i, k + 1], h)


def times_exact(w, k, h):
    mats, i = w
    high, low = halves(h)
    return dot(mats[i, k], high) + dot(mats[i, k + 1], high) + dot(mats[i, k], low)


def policy_head_rows(turned):
    one = jnp.zeros((1, HID + 1), F32)
    return jnp.concatenate([one, turned[:A_DIM], one, one, turned[A_DIM:], one], axis=0)


def noise_of(seed_row):
    k = lax.broadcasted_iota(jnp.int32, (8, seed_row.shape[1]), 0).astype(F32) - 1.0
    return 1.7 * jnp.sin(0.618034 * seed_row + 2.39996 * k)


def actor_stream(one, mats, bias, head, head_bias, x, noise):
    rows = x.shape[1]
    z = dot(one[0], stack_inputs(x))
    yield
    z = times((mats, 0), 0, act(z)[0].astype(BF16))
    yield
    z = times((mats, 0), 4, act(z + spread(bias[0, 0], rows))[0].astype(BF16))
    yield
    high, low = halves(act(z + spread(bias[0, 1], rows))[0])
    out = dot(head, high)
    out = out[:16] + out[16:] + dot(head[:16], low) + spread(head_bias, rows)
    yield
    mean, raw = out[:8], out[8:]
    turned = jnp.tanh(raw)
    log_std = LOGSTD_LOW + 0.5 * (LOGSTD_HIGH - LOGSTD_LOW) * (turned + 1.0)
    deviation = jnp.exp(log_std) * noise
    u = mean + deviation
    soft = jnp.maximum(-2.0 * u, 0.0) + jnp.log(1.0 + jnp.exp(-jnp.abs(2.0 * u)))
    squash = 2.0 * (LOG_TWO - u - soft)
    terms = -0.5 * noise * noise - log_std - HALF_LOG_TWOPI - squash
    log_prob = jnp.sum(action_rows(terms), axis=0, keepdims=True)
    return jnp.tanh(u), turned, deviation, log_prob


def first_kernel(place, out):
    out[...] = jnp.full(out.shape, (place[0] == 0).astype(F32))


def actor_kernel(
    first, states, actions, next_states, seeds, rewards, terminal, valid, body, head, log_temp, xs, xn, xp, aux, one, mats, bias
):
    rows = states.shape[1]
    ones = jnp.ones((1, rows), F32)
    for x, source in ((xs, states), (xn, next_states), (xp, states)):
        x[0:S_DIM, :] = source[...]
        x[X_DIM : X_DIM + 1, :] = ones
    xs[S_DIM:X_DIM, :] = actions[...]
    seed = seeds[...].astype(F32)
    load_trunk(lambda a, b: body[a:b], S_DIM, one, mats, bias, 0)
    head_rows = policy_head_rows(head[...])
    head_w, head_b = jnp.concatenate(halves(head_rows[:, :HID]), axis=0), wide(head_rows[:, HID:])
    carry = 1.0 - lane_row(terminal[...].astype(F32))
    temper = jnp.exp(log_temp[0])
    now_in = jnp.concatenate([states[...], ones], axis=0)
    later_in = jnp.concatenate([next_states[...], ones], axis=0)
    half = rows // 2
    done = interleave(
        *[
            actor_stream(one, mats, bias, head_w, head_b, x[:, i : i + half], noise_of(seed[k : k + 1, i : i + half]))
            for i in (0, half)
            for x, k in ((later_in, 1), (now_in, 0))
        ]
    )
    later = [jnp.concatenate(v, axis=1) for v in zip(*done[0::2])]
    now = [jnp.concatenate(v, axis=1) for v in zip(*done[1::2])]
    xn[S_DIM:X_DIM, :] = later[0][1 : 1 + A_DIM]
    aux[0:1, :] = lane_row(rewards[...]) - DISCOUNT * carry * temper * later[3]
    aux[1:2, :] = DISCOUNT * carry
    aux[2:3, :] = lane_row(valid[...].astype(F32))
    action, turned, deviation, log_prob = now
    xp[S_DIM:X_DIM, :] = action[1 : 1 + A_DIM]
    aux[3:4, :] = log_prob
    aux[4:5, :] = spread(first[0:1], rows)
    aux[5:8, :] = jnp.zeros((3, rows), F32)
    aux[8:16, :] = action_rows(action)
    aux[16:24, :] = action_rows(turned)
    aux[24:32, :] = action_rows(deviation)


def head_column(head, c):
    row = head[pl.ds(c, 1), :]
    return row[:, :HID].T, row[:, HID:]


def inner_rows(read):
    return jnp.concatenate(halves(0.5 * read(16, 24)), axis=0)


def action_gradient(inner, y):
    grad = dot(inner, y)
    return action_rows(grad[:8] + grad[8:])


def data_stream(one, mats, bias, i, column, inner, x):
    rows, w = x.shape[1], (mats, i)
    z = dot(one[i], x)
    yield
    h, t = act(z)
    d1 = slope(h, t)
    z = times_exact(w, 0, h)
    yield
    h, t = act(z + spread(bias[i, 0], rows))
    d2 = slope(h, t)
    z = times_exact(w, 4, h)
    yield
    h, t = act(z + spread(bias[i, 1], rows))
    c = times(w, 6, (spread(column, rows) * slope(h, t)).astype(BF16))
    yield
    c = times(w, 2, (c * d2).astype(BF16))
    yield
    grad = action_gradient(inner, (c * d1).astype(BF16))
    yield
    size = jnp.sum(grad * grad, axis=0, keepdims=True) + GRAD_FLOOR
    return grad * lax.rsqrt(size)


def target_stream(one, mats, bias, i, column, last, x):
    rows, w = x.shape[1], (mats, i)
    z = dot(one[i], x)
    yield
    z = times(w, 0, act(z)[0].astype(BF16))
    yield
    z = times(w, 4, act(z + spread(bias[i, 0], rows))[0].astype(BF16))
    yield
    h = act(z + spread(bias[i, 1], rows))[0]
    return jnp.sum(spread(column, rows) * h, axis=0, keepdims=True) + last


def chosen_stream(one, mats, bias, i, column, last, inner, x):
    rows = x.shape[1]
    z = dot(one[i], x)
    yield
    h, t = act(z)
    d1 = slope(h, t)
    z = dot(mats[i, 0], h.astype(BF16))
    yield
    h, t = act(z + spread(bias[i, 0], rows))
    d2 = slope(h, t)
    z = dot(mats[i, 4], h.astype(BF16))
    yield
    h, t = act(z + spread(bias[i, 1], rows))
    column = spread(column, rows)
    q = jnp.sum(column * h, axis=0, keepdims=True) + last
    c = dot(mats[i, 6], (column * slope(h, t)).astype(BF16))
    yield
    c = dot(mats[i, 2], (c * d2).astype(BF16))
    yield
    return q, action_gradient(inner, (c * d1).astype(BF16))


def critic_kernel(live, xs, xn, xp, body, head, body_tgt, head_tgt, out, one, mats, bias, columns):
    lasts, inners = [], []
    for i in range(4):
        c = i % 2
        read = critic_rows((body, body_tgt)[i // 2], c)
        load_trunk(read, X_DIM, one, mats, bias, i, backward=i < 2)
        column, last = head_column((head, head_tgt)[i // 2], c)
        columns[i] = wide(column)
        lasts.append(last)
        if i < 2:
            inners.append(inner_rows(read))
    alive = [live[c].astype(F32) for c in range(2)]
    rows = xs.shape[1]
    step = 256
    for start in range(0, rows, step):
        at = slice(start, start + step)
        data, later, chosen = stack_inputs(xs[:, at]), stack_inputs(xn[:, at]), stack_inputs(xp[:, at])
        unit, now, value = [], [], []
        done = interleave(
            *[data_stream(one, mats, bias, c, columns[c], inners[c], data) for c in range(2)],
            *[chosen_stream(one, mats, bias, c, columns[c], lasts[c], inners[c], chosen) for c in range(2)],
            *[target_stream(one, mats, bias, 2 + c, columns[2 + c], lasts[2 + c], later) for c in range(2)],
        )
        unit, now, value = done[0:2], done[2:4], done[4:6]
        lowest = [jnp.where(alive[c] > 0, value[c], FAR_VALUE) for c in range(2)]
        total_n, total_q, total_g = [alive[0] * a + alive[1] * b for a, b in (unit, *zip(*now))]
        out[0:8, at] = row_at(jnp.minimum(lowest[0], lowest[1]), 7, row_at(alive[0] + alive[1], 0, total_n))
        out[8:16, at] = row_at(total_q, 0, total_g)


def merge(a, b):
    k = lax.broadcasted_iota(jnp.int32, a.shape, 0)
    return jnp.where(k == 7, jnp.minimum(a, b), a + b)


def joint_kernel(mine, other, aux, log_temp, sx, gx, sums):
    both = merge(mine[...], other[...])
    unit, grad = both[:8], both[8:]
    mask, log_prob = aux[2:3, :], aux[3:4, :]
    members = both[0:1]
    target = aux[0:1, :] + aux[1:2, :] * both[7:8]
    unit = action_rows(unit)
    sx[...] = row_at(target, 7, row_at(mask, 0, mask * unit))
    gx[...] = row_at(members, 7, grad)
    temper = jnp.exp(log_temp[0])
    spread = jnp.sum(mask * (jnp.sum(unit * unit, axis=0, keepdims=True) - members), axis=1, keepdims=True)
    actor = jnp.sum(mask * (temper * log_prob - both[8:9] / members), axis=1, keepdims=True)
    entropy = jnp.sum(mask * (log_prob + ENTROPY_TARGET), axis=1, keepdims=True)
    count = jnp.sum(mask, axis=1, keepdims=True)
    lane = lax.broadcasted_iota(jnp.int32, (1, 128), 1)
    row = jnp.where(lane == 1, spread, 0.0) + jnp.where(lane == 2, actor, 0.0)
    row = row + jnp.where(lane == 3, entropy, 0.0) + jnp.where(lane == 4, count, 0.0)
    sums[...] = row * aux[4:5, 0:128]


def policy_stream(one, mats, bias, head_back, x, rows8, by_log):
    rows, w = x.shape[1], (mats, 0)
    z = dot(one[0], stack_inputs(x))
    yield
    h, t = act(z)
    d1, h1 = slope(h, t), h.astype(BF16)
    z = times(w, 0, h1)
    yield
    h, t = act(z + spread(bias[0, 0], rows))
    d2, h2 = slope(h, t), h.astype(BF16)
    z = times(w, 4, h2)
    yield
    h, t = act(z + spread(bias[0, 1], rows))
    action, turned, deviation, by_action = rows8
    by_u = by_action * (1.0 - action * action) + by_log * 2.0 * action
    by_std = by_u * deviation - by_log
    by_raw = action_rows(by_std * (0.5 * (LOGSTD_HIGH - LOGSTD_LOW)) * (1.0 - turned * turned))
    by_out = jnp.concatenate([action_rows(by_u), by_raw], axis=0)
    high, low = halves(by_out)
    f3 = (dot(head_back, jnp.concatenate([high, low, high], axis=0)) * slope(h, t)).astype(BF16)
    yield
    f2 = (times(w, 6, f3) * d2).astype(BF16)
    yield
    f1 = (times(w, 2, f2) * d1).astype(BF16)
    yield
    return h1, h2, h.astype(BF16), f1, f2, f3, high, low, by_out


def policy_kernel(place, xs, aux, gx, body, head, log_temp, keep, give, full, one, mats, bias):
    rows = xs.shape[1]
    n = S_DIM
    load_trunk(lambda a, b: body[a:b], n, one, mats, bias, 0, backward=True)
    head_high, head_low = halves(0.5 * policy_head_rows(head[...])[:, :HID])
    head_back = jnp.concatenate([head_high, head_high, head_low], axis=0).astype(F32).T.astype(BF16)
    x = row_at(1.0, n, xs[...])
    mask, members = aux[2:3, :], gx[7:8, :]
    by_action = -(mask / members) * action_rows(gx[...])
    by_log = jnp.exp(log_temp[0]) * mask
    rows8 = (aux[8:16, :], aux[16:24, :], aux[24:32, :], by_action)
    step = rows // 4
    cut = lambda v, i: v[:, i * step : (i + 1) * step]
    streams = [
        policy_stream(one, mats, bias, head_back, cut(x[: n + 1], i), [cut(v, i) for v in rows8], cut(by_log, i))
        for i in range(4)
    ]
    h1, h2, h3, f1, f2, f3, high, low, by_out = [jnp.concatenate(v, axis=1) for v in zip(*interleave(*streams))]
    ones = row_at(1.0, 0, jnp.zeros((16, rows), F32)).astype(BF16)
    start = jnp.where(lax.broadcasted_iota(jnp.int32, x.shape, 0) <= n, x, 0.0).astype(BF16)
    full[0:P_TWO, :] = dot_rows(start, f1)
    full[P_TWO:P_THREE, :] = dot_rows(jnp.concatenate([h1, ones], axis=0), f2)[: HID + 8]
    layer = dot_rows(jnp.concatenate([h2, ones], axis=0), f3)
    full[P_THREE : P_THREE + HID, :] = layer[:HID]
    last = wide(jnp.sum(by_out, axis=1, keepdims=True)).T[0:1]
    last = jnp.concatenate([last, jnp.zeros((1, HID - 16), F32)], axis=1)
    full[P_LAST:P_HEAD, :] = row_at(last, 1, layer[HID : HID + 8])
    by_head = dot_rows(jnp.concatenate([high, low], axis=0), h3)
    full[P_HEAD : P_HEAD + 16, :] = by_head[:16] + by_head[16:]
    full[P_HEAD + 16 :, :] = jnp.zeros((full.shape[0] - P_HEAD - 16, HID), F32)
    size = keep.shape[0]
    for out, x in ((keep, place[1]), (give, 1 - place[1])):
        out[...] = full[pl.ds(pl.multiple_of((2 * place[0] + x) * size, 8), size), :]


def second_stream(
    one, mats, bias, column, last, inner, inner_stack, alive, weight, x, s, here, left3, here3, there3, left2, here2, there2,
    left1, here1, there1, lefth, righth,
):
    rows, w = x.shape[1], (mats, 0)
    total = left3.shape[1] // 2
    there = slice(total + here.start, total + here.stop)
    one_row = row_at(1.0, 0, jnp.zeros((16, rows), F32))
    none = jnp.zeros((16, rows), BF16)
    mask, target = s[0:1], s[7:8]
    left1[:, here] = jnp.concatenate([x, jnp.zeros((8, rows), F32)], axis=0).astype(BF16)
    for left in (left2, left3):
        left[HID : HID + 16, here] = one_row.astype(BF16)
        left[HID : HID + 16, there] = none
    lefth[:, there] = one_row.astype(BF16)
    z = dot(one[0], stack_inputs(x))
    yield
    h, t = act(z)
    d1, e1 = slope(h, t), curve(z, t)
    left2[0:HID, here] = h.astype(BF16)
    z = times_exact(w, 0, h)
    yield
    z = z + spread(bias[0, 0], rows)
    h, t = act(z)
    d2, e2 = slope(h, t), curve(z, t)
    left3[0:HID, here] = h.astype(BF16)
    z = times_exact(w, 4, h)
    yield
    z = z + spread(bias[0, 1], rows)
    h, t = act(z)
    d3, e3 = slope(h, t), curve(z, t)
    righth[:, here] = h.astype(BF16)
    column = spread(column, rows)
    q = jnp.sum(column * h, axis=0, keepdims=True) + last
    b3 = column * d3
    e3 = column * e3
    cut = b3.astype(BF16)
    there3[:, here] = cut
    c2 = times(w, 6, cut)
    yield
    b2 = c2 * d2
    e2 = c2 * e2
    cut = b2.astype(BF16)
    there2[:, here] = cut
    c1 = times(w, 2, cut)
    yield
    b1 = c1 * d1
    e1 = c1 * e1
    cut = b1.astype(BF16)
    there1[:, here] = cut
    grad = action_gradient(inner, cut)
    miss = q - target
    half_a = alive * mask * miss
    td = jnp.sum(half_a * miss, axis=1, keepdims=True)
    a_high = half_a.astype(BF16).astype(F32)
    lefth[:, here] = row_at(a_high, 0, row_at(half_a - a_high, 1, jnp.zeros((16, rows), F32))).astype(BF16)
    yield
    size = jnp.sum(grad * grad, axis=0, keepdims=True) + GRAD_FLOOR
    cot = action_rows(s) * weight
    along = jnp.sum(grad * cot, axis=0, keepdims=True)
    v = lax.rsqrt(size) * (cot - grad * (along / size))
    left1[:, there] = jnp.concatenate([jnp.zeros((16, rows), F32), v, jnp.zeros((8, rows), F32)], axis=0).astype(BF16)
    t1 = dot(inner_stack, stack_inputs(v))
    yield
    cut = (d1 * t1).astype(BF16)
    left2[0:HID, there] = cut
    t2 = times(w, 0, cut)
    yield
    cut = (d2 * t2).astype(BF16)
    left3[0:HID, there] = cut
    t3 = times(w, 4, cut)
    yield
    righth[:, there] = (d3 * t3).astype(BF16)
    r = e3 * t3
    here3[:, here] = (half_a * b3 + r).astype(BF16)
    r = dot(mats[0, 6], r.astype(BF16)) * d2 + e2 * t2
    yield
    here2[:, here] = (half_a * b2 + r).astype(BF16)
    r = dot(mats[0, 2], r.astype(BF16)) * d1 + e1 * t1
    yield
    here1[:, here] = (half_a * b1 + r).astype(BF16)
    return td, jnp.sum(half_a, axis=1, keepdims=True)


def second_kernel(live, place, xs, xs_far, sx, sx_far, gx, body, head, *refs):
    (grads, sums, one, mats, bias), scratch = refs[:5], refs[5:]
    left3, here3, there3, left2, here2, there2, left1, here1, there1, lefth, righth = scratch
    rows = xs.shape[1]
    mine = place[1]
    alive = jnp.where(mine == 0, live[0], live[1]).astype(F32)
    read = critic_rows(body, mine)
    load_trunk(read, X_DIM, one, mats, bias, 0, backward=True)
    column, last = head_column(head, mine)
    column = wide(column)
    inner, inner_stack = inner_rows(read), stack_weights(read(16, 24))
    weight = 2.0 * DIVERSITY_WEIGHT * alive / (gx[7:8, :] - 1.0)
    td = bias_sum = jnp.zeros((1, 1), F32)
    step = rows // 2
    for td_part, bias_part in interleave(
        *[
            second_stream(
                one, mats, bias, column, last, inner, inner_stack, alive, weight[:, start : start + step],
                x[:, start : start + step], s[:, start : start + step],
                slice(i * rows + start, i * rows + start + step), *scratch,
            )
            for start in range(0, rows, step)
            for i, (x, s) in enumerate(((xs, sx), (xs_far, sx_far)))
        ]
    ):
        td, bias_sum = td + td_part, bias_sum + bias_part

    def layer(left, here, there):
        n = here.shape[1]
        return dot_rows(left[:, 0:n], here[...]) + 0.5 * dot_rows(left[:, n:], there[...])

    grads[0:TWO, :] = layer(left1, here1, there1)[0:TWO]
    grads[TWO:THREE, :] = layer(left2, here2, there2)[0 : HID + 1]
    grads[THREE:BODY, :] = layer(left3, here3, there3)[0 : HID + 1]
    n = here3.shape[1]
    by_head = dot_rows(lefth[:, 0:n], righth[:, 0:n])
    grads[BODY : BODY + 1, :] = 2.0 * (by_head[0:1] + by_head[1:2]) + dot_rows(lefth[:, n:], righth[:, n:])[0:1]
    lane = lax.broadcasted_iota(jnp.int32, (1, HID), 1)
    grads[BODY + 1 : BODY + 2, :] = jnp.where(lane == 0, 2.0 * bias_sum, 0.0)
    grads[BODY + 2 :, :] = jnp.zeros((grads.shape[0] - BODY - 2, HID), F32)
    sums[...] = jnp.where(lax.broadcasted_iota(jnp.int32, (1, 128), 1) == 0, td, 0.0)


def deal_kernel(place, critic, keep, got, *out):
    n = len(out)
    part = critic.shape[0] // n
    policy = keep[...] + got[...]
    for k in range(n):
        to = jnp.bitwise_xor(place[2], k)
        out[k][0:part, :] = critic[pl.ds(pl.multiple_of(to * part, 8), part), :]
        out[k][part:, :] = policy


def reduce_kernel(part, place, one, two, *refs):
    ins, (out, critic_out, sums) = refs[:-3], refs[-3:]
    total = ins[0][...]
    for r in ins[1:]:
        total = total + r[...]
    out[...] = total
    critic, policy = total[:part], total[part:]
    critic_out[...] = critic
    square = jnp.sum(jnp.sum(critic * critic, axis=0, keepdims=True), axis=1, keepdims=True)
    once = (place[2] == 0).astype(F32)
    square = square + once * jnp.sum(jnp.sum(policy * policy, axis=0, keepdims=True), axis=1, keepdims=True)
    lane = lax.broadcasted_iota(jnp.int32, (1, 128), 1)
    row = one[...] + two[...] + jnp.where(lane == 5, square, 0.0)
    sums[...] = jnp.broadcast_to(row, sums.shape)


def adam(weights, moment, second, grads):
    moment_new = BETA_ONE * moment + (1.0 - BETA_ONE) * grads
    second_new = BETA_TWO * second + (1.0 - BETA_TWO) * grads * grads
    corrected = moment_new * (1.0 / (1.0 - BETA_ONE**STEPS_DONE))
    scale_sq = second_new * (1.0 / (1.0 - BETA_TWO**STEPS_DONE))
    step = corrected / (jnp.sqrt(scale_sq) + ADAM_EPSILON) + DECAY_RATE * weights
    return weights - LEARN_RATE * step, moment_new, second_new


def scalars_of(sums, log_temp):
    total = jnp.sum(sums[...], axis=0, keepdims=True)
    entropy, count = total[:, 3:4], total[:, 4:5]
    grad_temp = -entropy / count
    norm = jnp.sqrt(total[:, 5:6] / (count * count) + grad_temp * grad_temp)
    factor = CLIP_NORM / jnp.maximum(norm, CLIP_NORM)
    return total, entropy, count, grad_temp, norm, factor


def put(refs, at, got):
    for r, value in zip(refs, got):
        r[at] = value.astype(r.dtype)


def update_kernel(n_z, part, small, sources, places, place, log_temp, log_mom, log_sq, sums, *refs):
    refs = list(refs)
    take = lambda n: [refs.pop(0) for _ in range(n)]
    pieces, blocks = take(len(sources)), take(len(places))
    w, m, v, t, hw, hm, hv, ht, pw, pm, pv, phw, phm, phv = take(14)
    outs = take(23)
    total, policy = take(2)
    near, sem, body_sem = take(23), *take(2)
    row, entropy, count, grad_temp, norm, factor = scalars_of(sums, log_temp)
    scale = factor / count
    for piece, k in zip(pieces, sources):
        c = jnp.bitwise_xor(place[1], k // n_z)
        z = jnp.bitwise_xor(place[2], k % n_z)
        for side in range(2):
            at = pl.ds(4 * part * z + 2 * side + c, part, stride=4)
            total[at, :] = piece[0:part, side * 128 : (side + 1) * 128]
    copies = []

    def send(i, j):
        copies.extend(start_copies(near[i:j], outs[i:j], sem.at[pl.ds(i, j - i)]))

    rows = w.shape[0]
    step = 1088
    for i, start in enumerate(range(0, rows, step)):
        at = pl.ds(start, min(step, rows - start))
        new, mom, sq = adam(w[at, :], m[at, :], v[at, :], total[at, :] * scale)
        tgt = (1.0 - POLYAK_RATE) * t[at, :] + POLYAK_RATE * new
        put(near[2:7], (at, slice(None)), (new, mom, sq, tgt, new))
        copies += start_copies([r.at[at, :] for r in near[2:6]], [r.at[at, :] for r in outs[2:6]], body_sem.at[i])
    send(6, 7)
    for c in range(2):
        at = slice(c, c + 1)
        rows8 = [total[4 * (BODY + k) + 2 * side + c : 4 * (BODY + k) + 2 * side + c + 1, :] for k, side in ((0, 0), (0, 1), (1, 0))]
        grad = jnp.concatenate([rows8[0], rows8[1], rows8[2][:, 0:1]], axis=1)
        new, mom, sq = adam(hw[at, :], hm[at, :], hv[at, :], grad * scale)
        tgt = (1.0 - POLYAK_RATE) * ht[at, :] + POLYAK_RATE * new
        put(near[7:12], (at, slice(None)), (new, mom, sq, tgt, new))
    lane = lax.broadcasted_iota(jnp.int32, (1, 128), 1)
    near[0][...] = jnp.where(lane == 3, -log_temp[0] * entropy, row)[:, 0:5]
    near[1][...] = norm
    one = lambda v: jnp.full((1, 1), v[0])
    put(near[20:23], (slice(0, 1),), adam(one(log_temp), one(log_mom), one(log_sq), factor * grad_temp))
    send(0, 2)
    send(7, 12)
    send(20, 23)
    for block, dm in zip(blocks, places):
        for x in range(2):
            at = 2 * jnp.bitwise_xor(place[0], dm) + jnp.bitwise_xor(place[1], x)
            policy[pl.ds(pl.multiple_of(at * small, 8), small), :] = block[x * small : (x + 1) * small, :]
    n = S_DIM
    for mine, at in (
        (slice(0, n + 1), slice(0, n + 1)),
        (slice(P_TWO, P_TWO + HID + 1), slice(n + 1, n + 2 + HID)),
        (slice(P_THREE, P_THREE + HID + 1), slice(n + 2 + HID, n + 3 + 2 * HID)),
    ):
        new, mom, sq = adam(pw[at], pm[at], pv[at], policy[mine, :] * scale)
        put(near[12:16], (at,), (new, mom, sq, new))
    send(12, 16)
    by_head = policy[P_HEAD : P_HEAD + 16, :]
    last = jnp.broadcast_to(policy[P_LAST + 1 : P_LAST + 2, 0:16], (8, 16)).T[:, 0:1]
    for r, at in ((1, slice(0, A_DIM)), (9, slice(A_DIM, 2 * A_DIM))):
        grad = jnp.concatenate([by_head[r : r + A_DIM], last[r : r + A_DIM]], axis=1)
        new, mom, sq = adam(phw[at, :], phm[at, :], phv[at, :], grad * scale)
        put(near[16:20], (at, slice(None)), (new, mom, sq, new))
    send(16, 20)
    for copy in copies:
        copy.wait()


def blocks_kernel(part, own, other, out):
    half = out.shape[0] // 2
    out[0:half, :] = own[part:, :]
    out[half:, :] = other[part:, :]


def flat(v):
    return jnp.transpose(v.reshape(2, -1, 2, 128), (1, 2, 0, 3)).reshape(-1, 128)


def unflat(v):
    return jnp.transpose(v.reshape(-1, 2, 2, 128), (2, 0, 1, 3)).reshape(2, -1, HID)


def per_device(
    members,
    dp,
    states,
    actions,
    rewards,
    next_states,
    terminal,
    valid_rows,
    noise_seeds,
    member_live,
    critic_body,
    critic_body_mom,
    critic_body_sq,
    critic_body_tgt,
    critic_head,
    critic_head_mom,
    critic_head_sq,
    critic_head_tgt,
    policy_body,
    policy_body_mom,
    policy_body_sq,
    policy_head,
    policy_head_mom,
    policy_head_sq,
    log_temp,
    log_temp_mom,
    log_temp_sq,
):
    rows = states.shape[0]
    n_z = dp // 2
    part = -(-CRITIC_ROWS // (8 * n_z)) * 8
    small = -(-POLICY_ROWS // (16 * members)) * 8
    m, d = lax.axis_index("member"), lax.axis_index("dp")
    place = jnp.stack([m, d // n_z, d % n_z]).astype(jnp.int32)

    def across(value, axis, n, to):
        return lax.ppermute(value, axis, [(i, to(i)) for i in range(n)])

    def to_member(value, bit):
        return across(value, "member", members, lambda i: i ^ bit)

    def to_pair(value):
        return across(value, "dp", dp, lambda i: i ^ n_z)

    def along(value, offset):
        return across(value, "dp", dp, lambda i: i ^ offset)

    square = lambda v: v.reshape(rows // 128, 128)
    turned = [policy_head.T, policy_head_mom.T, policy_head_sq.T]
    body, mom, sq, body_tgt = flat(critic_body), flat(critic_body_mom), flat(critic_body_sq), flat(critic_body_tgt)
    like = lambda *arrays: [shape(*a.shape, dtype=a.dtype) for a in arrays]
    first = call(first_kernel, shape(8, 128), [SMEM], us=8.0, limit=1)(place)
    xs, xn, xp, aux = call(
        actor_kernel,
        [shape(24, rows), shape(24, rows), shape(24, rows), shape(32, rows)],
        [VMEM] * 10 + [SMEM],
        trunk_scratch(1, S_DIM),
        us=3.0,
    )(
        first, states.T, actions.T, next_states.T, noise_seeds.T, square(rewards), square(terminal), square(valid_rows),
        policy_body, turned[0], log_temp,
    )
    xs_far = to_pair(xs)
    scratch = trunk_scratch(4, X_DIM) + [pltpu.VMEM((4, HID, 128), F32)]
    ensemble = call(critic_kernel, shape(16, rows), [SMEM] + [VMEM] * 7, scratch, us=8.0)(
        member_live, xs, xn, xp, body, critic_head, body_tgt, critic_head_tgt
    )
    bit = 1
    while bit * 2 < members:
        other = to_member(ensemble, bit)
        k = lax.broadcasted_iota(jnp.int32, ensemble.shape, 0)
        ensemble = jnp.where(k == 7, jnp.minimum(ensemble, other), ensemble + other)
        bit *= 2
    sx, gx, sums_joint = call(
        joint_kernel, [shape(8, rows), shape(8, rows), shape(1, 128)], [VMEM, VMEM, VMEM, SMEM], us=0.7
    )(ensemble, to_member(ensemble, bit), aux, log_temp)
    sx_far = to_pair(sx)
    keep, give = call(
        policy_kernel,
        [shape(small, HID), shape(small, HID)],
        [SMEM] + [VMEM] * 5 + [SMEM],
        [pltpu.VMEM((2 * members * small, HID), F32)] + trunk_scratch(1, S_DIM),
        us=3.0,
    )(place, xs, aux, gx, policy_body, turned[0], log_temp)
    got = to_pair(give)
    both = 2 * rows
    left, side = pltpu.VMEM((HID + 16, 2 * both), BF16), pltpu.VMEM((HID, both), BF16)
    scratch = [left, side, side, left, side, side, pltpu.VMEM((32, 2 * both), BF16), side, side]
    scratch = scratch + [pltpu.VMEM((16, 2 * both), BF16), pltpu.VMEM((HID, 2 * both), BF16)]
    grads, sums_second = call(
        second_kernel,
        [shape(part * n_z, HID), shape(1, 128)],
        [SMEM, SMEM] + [VMEM] * 7,
        trunk_scratch(1, X_DIM) + scratch,
        us=9.0,
        limit=42,
    )(member_live, place, xs, xs_far, sx, sx_far, gx, body, critic_head)
    message = shape(part + small, HID)
    dealt = call(deal_kernel, [message] * n_z, [SMEM, VMEM, VMEM, VMEM], us=0.5)(place, grads, keep, got)
    arrived = [dealt[0]] + [along(dealt[k], k) for k in range(1, n_z)]
    whole, piece, sums = call(
        functools.partial(reduce_kernel, part),
        [message, shape(part, HID), shape(members * dp, 128)],
        [SMEM] + [VMEM] * (2 + n_z),
    )(place, sums_joint, sums_second, *arrived)
    sums = lax.all_to_all(sums, ("member", "dp"), 0, 0, tiled=True)
    pieces, bit = {0: piece, n_z: to_pair(whole)}, 1
    while bit < n_z:
        pieces[bit] = along(piece, bit)
        bit *= 2
    at_hand = sorted(pieces)
    *values, sums = lax.optimization_barrier((*[pieces[k] for k in at_hand], sums))
    pieces = dict(zip(at_hand, values))
    pieces[dp - 1] = along(pieces[0], dp - 1)
    for k in sorted(range(dp), key=lambda k: (bin(k).count("1"), -k)):
        if k not in pieces:
            pieces[k] = along(pieces[k & (k - 1)], k & -k)
    sources = sorted(pieces)
    block = call(functools.partial(blocks_kernel, part), shape(2 * small, HID), [VMEM] * 2, us=0.5)(whole, pieces[n_z])
    blocks, places, bit = [block], [0], members // 2
    while bit:
        if bit == 1:
            late = [k for k in sources if k not in at_hand]
            values = lax.optimization_barrier((*blocks, *[pieces[k] for k in late]))
            blocks = values[: len(blocks)]
            pieces.update(zip(late, values[len(blocks) :]))
        blocks = [*blocks] + [to_member(b, bit) for b in blocks]
        places = places + [k ^ bit for k in places]
        bit //= 2
    halved = lambda a: shape(*a.shape, dtype=BF16)
    heads = [critic_head, critic_head_mom, critic_head_sq, critic_head_tgt]
    single = shape(1, 1)
    outs = [shape(1, 5), single] + like(body, body, body, body) + [halved(body)] + like(*heads) + [halved(critic_head)]
    outs = outs + like(policy_body, policy_body, policy_body) + [halved(policy_body)] + like(*turned) + [halved(turned[0])]
    outs = outs + [single, single, single]
    new = call(
        functools.partial(update_kernel, n_z, part, small, sources, places),
        outs,
        [SMEM] * 4 + [VMEM] * (1 + len(sources) + len(blocks) + 14),
        [pltpu.VMEM((4 * n_z * part, 128), F32), pltpu.VMEM((2 * members * small, HID), F32)]
        + buffers(*outs)
        + [pltpu.SemaphoreType.DMA((-(-body.shape[0] // 1088), 4))],
        us=5.0,
        out_specs=[HBM] * len(outs),
    )(
        place, log_temp, log_temp_mom, log_temp_sq, sums, *[pieces[k] for k in sources], *blocks, body, mom, sq, body_tgt,
        *heads, policy_body, policy_body_mom, policy_body_sq, *turned,
    )
    new = list(new)
    new = [v[0] for v in new[:2]] + [unflat(v) for v in new[2:7]] + new[7:16] + [v.T for v in new[16:20]] + [v[0] for v in new[20:]]
    return tuple(new)


def solution(mesh):
    row, line = P("dp", None), P("dp")
    stack, flat = P("member", None, None), P("member", None)
    return jax.shard_map(
        functools.partial(per_device, mesh.shape["member"], mesh.shape["dp"]),
        mesh=mesh,
        in_specs=(row, row, line, row, line, line, row, P("member")) + (stack,) * 4 + (flat,) * 4 + (P(),) * 9,
        out_specs=(P(), P()) + (stack,) * 5 + (flat,) * 5 + (P(),) * 11,
        check_vma=False,
    )
```

```python
import functools

import jax
import jax.numpy as jnp
from jax import lax
from jax.experimental import pallas as pl
from jax.experimental.pallas import tpu as pltpu
from jax.sharding import PartitionSpec as P

STEPS_DONE = 5
DISCOUNT = 0.99
POLYAK_RATE = 0.005
ENTROPY_TARGET = -6.0
DIVERSITY_WEIGHT = 1.0
LEARN_RATE = 0.05
BETA_ONE = 0.5
BETA_TWO = 0.5
DECAY_RATE = 0.01
ADAM_EPSILON = 1e-08
GRAD_FLOOR = 0.0001
CLIP_NORM = 1.0
LOGSTD_LOW = -5.0
LOGSTD_HIGH = 2.0
LOG_TWO = 0.6931471805599453
HALF_LOG_TWOPI = 0.9189385332046727
FAR_VALUE = 1e30

F32 = jnp.float32
BF16 = jnp.bfloat16
HID = 256
S_DIM = 17
A_DIM = 6
X_DIM = S_DIM + A_DIM
TWO = X_DIM + 1
THREE = TWO + HID + 1
BODY = THREE + HID + 1
CRITIC_ROWS = 544
P_TWO = 24
P_THREE = 288
P_LAST = 544
P_HEAD = 552
POLICY_ROWS = 576
BLOCK = 272
VMEM = pl.BlockSpec(memory_space=pltpu.VMEM)
SMEM = pl.BlockSpec(memory_space=pltpu.SMEM)
HBM = pl.BlockSpec(memory_space=pltpu.HBM)


def call(kernel, outs, in_specs, scratch=(), us=1.0, out_specs=None, limit=32):
    return pl.pallas_call(
        kernel,
        out_shape=outs,
        in_specs=in_specs,
        out_specs=out_specs or jax.tree.map(lambda _: VMEM, outs),
        scratch_shapes=list(scratch),
        compiler_params=pltpu.CompilerParams(vmem_limit_bytes=limit * 2**20),
        cost_estimate=pl.CostEstimate(flops=int(us * 1.15e9), bytes_accessed=0, transcendentals=0),
    )


def buffers(*arrays):
    return [pltpu.VMEM(a.shape, a.dtype) for a in arrays] + [pltpu.SemaphoreType.DMA((len(arrays),))]


def start_copies(sources, targets, sem):
    copies = [pltpu.make_async_copy(a, b, sem.at[i]) for i, (a, b) in enumerate(zip(sources, targets))]
    for copy in copies:
        copy.start()
    return copies


def shape(*dims, dtype=F32):
    return jax.ShapeDtypeStruct(dims, dtype)


def dot(a, b):
    return lax.dot_general(a, b, (((1,), (0,)), ((), ())), preferred_element_type=F32)


def dot_rows(a, b):
    return lax.dot_general(a, b, (((1,), (1,)), ((), ())), preferred_element_type=F32)


def halves(w):
    high = w.astype(BF16)
    return high, (w - high.astype(F32)).astype(BF16)


def stack_weights(w):
    high = (0.5 * w).astype(BF16).astype(F32)
    return jnp.concatenate([high, high, 0.5 * w - high], axis=0).T.astype(BF16)


def stack_inputs(v):
    high = v.astype(BF16).astype(F32)
    return jnp.concatenate([high, v - high, high], axis=0).astype(BF16)


def act(z):
    t = jnp.tanh(z)
    return z + z * t, t


def slope(h, t):
    return (1.0 + h) + t * (1.0 - h)


def curve(z, t):
    return (1.0 - t * t) * (1.0 - z * t)


def wide(column):
    return jnp.broadcast_to(column, (column.shape[0], 128))


def spread(column, rows):
    return jnp.concatenate([column] * (rows // 128), axis=1)


def action_rows(v):
    k = lax.broadcasted_iota(jnp.int32, v.shape, 0)
    return jnp.where((k >= 1) & (k <= A_DIM), v, 0.0)


def row_at(v, k, like):
    return jnp.where(lax.broadcasted_iota(jnp.int32, like.shape, 0) == k, v, like)


def lane_row(block):
    return jnp.concatenate([block[i : i + 1] for i in range(block.shape[0])], axis=1)


def interleave(*streams):
    results, active = [None] * len(streams), list(enumerate(streams))
    while active:
        left = []
        for i, stream in active:
            try:
                next(stream)
                left.append((i, stream))
            except StopIteration as end:
                results[i] = end.value
        active = left
    return results


def critic_rows(ref, c):
    def read(a, b):
        return jnp.concatenate([ref[pl.ds(4 * a + 2 * t + c, b - a, stride=4), :] for t in range(2)], axis=1)

    return read


def load_trunk(body, n_in, one, mats, bias, i, backward=False):
    one[i] = stack_weights(body(0, n_in + 1))
    for k, start in enumerate((n_in + 1, n_in + 2 + HID)):
        high, low = halves(0.5 * body(start, start + HID))
        mats[i, 4 * k] = high.T
        mats[i, 4 * k + 1] = low.T
        if backward:
            mats[i, 4 * k + 2] = high
            mats[i, 4 * k + 3] = low
        bias[i, k] = wide(0.5 * body(start + HID, start + HID + 1).T)


def trunk_arrays(n, n_in):
    return [shape(n, HID, 3 * (n_in + 1), dtype=BF16), shape(n, 8, HID, HID, dtype=BF16), shape(n, 2, HID, 128)]


def trunk_scratch(n, n_in):
    return [pltpu.VMEM(a.shape, a.dtype) for a in trunk_arrays(n, n_in)]


def times(w, k, h):
    mats, i = w
    return dot(mats[i, k], h) + dot(mats[i, k + 1], h)


def times_exact(w, k, h):
    mats, i = w
    high, low = halves(h)
    return dot(mats[i, k], high) + dot(mats[i, k + 1], high) + dot(mats[i, k], low)


def policy_head_rows(turned):
    one = jnp.zeros((1, HID + 1), F32)
    return jnp.concatenate([one, turned[:A_DIM], one, one, turned[A_DIM:], one], axis=0)


def noise_of(seed_row):
    k = lax.broadcasted_iota(jnp.int32, (8, seed_row.shape[1]), 0).astype(F32) - 1.0
    return 1.7 * jnp.sin(0.618034 * seed_row + 2.39996 * k)


def actor_stream(one, mats, bias, head, head_bias, x, noise):
    rows = x.shape[1]
    z = dot(one[0], stack_inputs(x))
    yield
    z = times((mats, 0), 0, act(z)[0].astype(BF16))
    yield
    z = times((mats, 0), 4, act(z + spread(bias[0, 0], rows))[0].astype(BF16))
    yield
    high, low = halves(act(z + spread(bias[0, 1], rows))[0])
    out = dot(head, high)
    out = out[:16] + out[16:] + dot(head[:16], low) + spread(head_bias, rows)
    yield
    mean, raw = out[:8], out[8:]
    turned = jnp.tanh(raw)
    log_std = LOGSTD_LOW + 0.5 * (LOGSTD_HIGH - LOGSTD_LOW) * (turned + 1.0)
    deviation = jnp.exp(log_std) * noise
    u = mean + deviation
    soft = jnp.maximum(-2.0 * u, 0.0) + jnp.log(1.0 + jnp.exp(-jnp.abs(2.0 * u)))
    squash = 2.0 * (LOG_TWO - u - soft)
    terms = -0.5 * noise * noise - log_std - HALF_LOG_TWOPI - squash
    log_prob = jnp.sum(action_rows(terms), axis=0, keepdims=True)
    return jnp.tanh(u), turned, deviation, log_prob


def first_kernel(place, out):
    out[...] = jnp.full(out.shape, (place[0] == 0).astype(F32))


def actor_kernel(
    first, states, actions, next_states, seeds, rewards, terminal, valid, body, head, log_temp, xs, xn, xp, aux, one, mats, bias
):
    rows = states.shape[1]
    ones = jnp.ones((1, rows), F32)
    for x, source in ((xs, states), (xn, next_states), (xp, states)):
        x[0:S_DIM, :] = source[...]
        x[X_DIM : X_DIM + 1, :] = ones
    xs[S_DIM:X_DIM, :] = actions[...]
    seed = seeds[...].astype(F32)
    load_trunk(lambda a, b: body[a:b], S_DIM, one, mats, bias, 0, backward=True)
    head_rows = policy_head_rows(head[...])
    head_w, head_b = jnp.concatenate(halves(head_rows[:, :HID]), axis=0), wide(head_rows[:, HID:])
    carry = 1.0 - lane_row(terminal[...].astype(F32))
    temper = jnp.exp(log_temp[0])
    now_in = jnp.concatenate([states[...], ones], axis=0)
    later_in = jnp.concatenate([next_states[...], ones], axis=0)
    half = rows // 2
    done = interleave(
        *[
            actor_stream(one, mats, bias, head_w, head_b, x[:, i : i + half], noise_of(seed[k : k + 1, i : i + half]))
            for i in (0, half)
            for x, k in ((later_in, 1), (now_in, 0))
        ]
    )
    later = [jnp.concatenate(v, axis=1) for v in zip(*done[0::2])]
    now = [jnp.concatenate(v, axis=1) for v in zip(*done[1::2])]
    xn[S_DIM:X_DIM, :] = later[0][1 : 1 + A_DIM]
    aux[0:1, :] = lane_row(rewards[...]) - DISCOUNT * carry * temper * later[3]
    aux[1:2, :] = DISCOUNT * carry
    aux[2:3, :] = lane_row(valid[...].astype(F32))
    action, turned, deviation, log_prob = now
    xp[S_DIM:X_DIM, :] = action[1 : 1 + A_DIM]
    aux[3:4, :] = log_prob
    aux[4:5, :] = spread(first[0:1], rows)
    aux[5:8, :] = jnp.zeros((3, rows), F32)
    aux[8:16, :] = action_rows(action)
    aux[16:24, :] = action_rows(turned)
    aux[24:32, :] = action_rows(deviation)


def head_column(head, c):
    row = head[pl.ds(c, 1), :]
    return row[:, :HID].T, row[:, HID:]


def inner_rows(read):
    return jnp.concatenate(halves(0.5 * read(16, 24)), axis=0)


def action_gradient(inner, y):
    grad = dot(inner, y)
    return action_rows(grad[:8] + grad[8:])


def data_stream(one, mats, bias, i, column, inner, x, save):
    rows, w = x.shape[1], (mats, i)
    z = dot(one[i], x)
    save(0, z)
    yield
    h, t = act(z)
    d1 = slope(h, t)
    z = times_exact(w, 0, h)
    yield
    z = z + spread(bias[i, 0], rows)
    save(1, z)
    h, t = act(z)
    d2 = slope(h, t)
    z = times_exact(w, 4, h)
    yield
    z = z + spread(bias[i, 1], rows)
    save(2, z)
    h, t = act(z)
    c = times(w, 6, (spread(column, rows) * slope(h, t)).astype(BF16))
    yield
    save(3, c)
    c = times(w, 2, (c * d2).astype(BF16))
    yield
    save(4, c)
    grad = action_gradient(inner, (c * d1).astype(BF16))
    yield
    size = jnp.sum(grad * grad, axis=0, keepdims=True) + GRAD_FLOOR
    return grad * lax.rsqrt(size)


def target_stream(one, mats, bias, i, column, last, x):
    rows, w = x.shape[1], (mats, i)
    z = dot(one[i], x)
    yield
    z = times(w, 0, act(z)[0].astype(BF16))
    yield
    z = times(w, 4, act(z + spread(bias[i, 0], rows))[0].astype(BF16))
    yield
    h = act(z + spread(bias[i, 1], rows))[0]
    return jnp.sum(spread(column, rows) * h, axis=0, keepdims=True) + last


def chosen_stream(one, mats, bias, i, column, last, inner, x):
    rows = x.shape[1]
    z = dot(one[i], x)
    yield
    h, t = act(z)
    d1 = slope(h, t)
    z = dot(mats[i, 0], h.astype(BF16))
    yield
    h, t = act(z + spread(bias[i, 0], rows))
    d2 = slope(h, t)
    z = dot(mats[i, 4], h.astype(BF16))
    yield
    h, t = act(z + spread(bias[i, 1], rows))
    column = spread(column, rows)
    q = jnp.sum(column * h, axis=0, keepdims=True) + last
    c = dot(mats[i, 6], (column * slope(h, t)).astype(BF16))
    yield
    c = dot(mats[i, 2], (c * d2).astype(BF16))
    yield
    return q, action_gradient(inner, (c * d1).astype(BF16))


def critic_kernel(live, place, xs, xn, xp, body, head, body_tgt, head_tgt, out, saved, *refs):
    mine, scratch, columns = refs[:3], refs[3:6], refs[6]
    order = [place[1], 1 - place[1]]
    lasts, inners, trunks = [], [], []
    for i in range(4):
        c = order[i % 2]
        read = critic_rows((body, body_tgt)[i // 2], c)
        trunks.append((*mine, 0) if i == 0 else (*scratch, i - 1))
        load_trunk(read, X_DIM, *trunks[i], backward=i < 2)
        column, last = head_column((head, head_tgt)[i // 2], c)
        columns[i] = wide(column)
        lasts.append(last)
        if i < 2:
            inners.append(inner_rows(read))
    alive = [live[c].astype(F32) for c in order]
    rows = xs.shape[1]
    step = 256
    for start in range(0, rows, step):
        at = slice(start, start + step)
        data, later, chosen = stack_inputs(xs[:, at]), stack_inputs(xn[:, at]), stack_inputs(xp[:, at])

        def save(k, value, at=at):
            saved[k, :, at] = value

        done = interleave(
            data_stream(*trunks[0], columns[0], inners[0], data, save),
            data_stream(*trunks[1], columns[1], inners[1], data, lambda k, value: None),
            *[chosen_stream(*trunks[c], columns[c], lasts[c], inners[c], chosen) for c in range(2)],
            *[target_stream(*trunks[2 + c], columns[2 + c], lasts[2 + c], later) for c in range(2)],
        )
        unit, now, value = done[0:2], done[2:4], done[4:6]
        lowest = [jnp.where(alive[c] > 0, value[c], FAR_VALUE) for c in range(2)]
        total_n, total_q, total_g = [alive[0] * a + alive[1] * b for a, b in (unit, *zip(*now))]
        out[0:8, at] = row_at(jnp.minimum(lowest[0], lowest[1]), 7, row_at(alive[0] + alive[1], 0, total_n))
        out[8:16, at] = row_at(total_q, 0, total_g)


def merge(a, b):
    k = lax.broadcasted_iota(jnp.int32, a.shape, 0)
    return jnp.where(k == 7, jnp.minimum(a, b), a + b)


def joint_kernel(mine, other, aux, log_temp, sx, gx, sums):
    both = merge(mine[...], other[...])
    unit, grad = both[:8], both[8:]
    mask, log_prob = aux[2:3, :], aux[3:4, :]
    members = both[0:1]
    target = aux[0:1, :] + aux[1:2, :] * both[7:8]
    unit = action_rows(unit)
    sx[...] = row_at(target, 7, row_at(mask, 0, mask * unit))
    gx[...] = row_at(members, 7, grad)
    temper = jnp.exp(log_temp[0])
    spread = jnp.sum(mask * (jnp.sum(unit * unit, axis=0, keepdims=True) - members), axis=1, keepdims=True)
    actor = jnp.sum(mask * (temper * log_prob - both[8:9] / members), axis=1, keepdims=True)
    entropy = jnp.sum(mask * (log_prob + ENTROPY_TARGET), axis=1, keepdims=True)
    count = jnp.sum(mask, axis=1, keepdims=True)
    lane = lax.broadcasted_iota(jnp.int32, (1, 128), 1)
    row = jnp.where(lane == 1, spread, 0.0) + jnp.where(lane == 2, actor, 0.0)
    row = row + jnp.where(lane == 3, entropy, 0.0) + jnp.where(lane == 4, count, 0.0)
    sums[...] = row * aux[4:5, 0:128]


def policy_stream(one, mats, bias, head_back, x, rows8, by_log):
    rows, w = x.shape[1], (mats, 0)
    z = dot(one[0], stack_inputs(x))
    yield
    h, t = act(z)
    d1, h1 = slope(h, t), h.astype(BF16)
    z = times(w, 0, h1)
    yield
    h, t = act(z + spread(bias[0, 0], rows))
    d2, h2 = slope(h, t), h.astype(BF16)
    z = times(w, 4, h2)
    yield
    h, t = act(z + spread(bias[0, 1], rows))
    action, turned, deviation, by_action = rows8
    by_u = by_action * (1.0 - action * action) + by_log * 2.0 * action
    by_std = by_u * deviation - by_log
    by_raw = action_rows(by_std * (0.5 * (LOGSTD_HIGH - LOGSTD_LOW)) * (1.0 - turned * turned))
    by_out = jnp.concatenate([action_rows(by_u), by_raw], axis=0)
    high, low = halves(by_out)
    f3 = (dot(head_back, jnp.concatenate([high, low, high], axis=0)) * slope(h, t)).astype(BF16)
    yield
    f2 = (times(w, 6, f3) * d2).astype(BF16)
    yield
    f1 = (times(w, 2, f2) * d1).astype(BF16)
    yield
    return h1, h2, h.astype(BF16), f1, f2, f3, high, low, by_out


def policy_kernel(place, xs, aux, gx, one, mats, bias, head, log_temp, keep, give, full):
    rows = xs.shape[1]
    n = S_DIM
    head_high, head_low = halves(0.5 * policy_head_rows(head[...])[:, :HID])
    head_back = jnp.concatenate([head_high, head_high, head_low], axis=0).astype(F32).T.astype(BF16)
    x = row_at(1.0, n, xs[...])
    mask, members = aux[2:3, :], gx[7:8, :]
    by_action = -(mask / members) * action_rows(gx[...])
    by_log = jnp.exp(log_temp[0]) * mask
    rows8 = (aux[8:16, :], aux[16:24, :], aux[24:32, :], by_action)
    step = rows // 4
    cut = lambda v, i: v[:, i * step : (i + 1) * step]
    streams = [
        policy_stream(one, mats, bias, head_back, cut(x[: n + 1], i), [cut(v, i) for v in rows8], cut(by_log, i))
        for i in range(4)
    ]
    h1, h2, h3, f1, f2, f3, high, low, by_out = [jnp.concatenate(v, axis=1) for v in zip(*interleave(*streams))]
    ones = row_at(1.0, 0, jnp.zeros((16, rows), F32)).astype(BF16)
    start = jnp.where(lax.broadcasted_iota(jnp.int32, x.shape, 0) <= n, x, 0.0).astype(BF16)
    full[0:P_TWO, :] = dot_rows(start, f1)
    full[P_TWO:P_THREE, :] = dot_rows(jnp.concatenate([h1, ones], axis=0), f2)[: HID + 8]
    layer = dot_rows(jnp.concatenate([h2, ones], axis=0), f3)
    full[P_THREE : P_THREE + HID, :] = layer[:HID]
    last = wide(jnp.sum(by_out, axis=1, keepdims=True)).T[0:1]
    last = jnp.concatenate([last, jnp.zeros((1, HID - 16), F32)], axis=1)
    full[P_LAST:P_HEAD, :] = row_at(last, 1, layer[HID : HID + 8])
    by_head = dot_rows(jnp.concatenate([high, low], axis=0), h3)
    full[P_HEAD : P_HEAD + 16, :] = by_head[:16] + by_head[16:]
    full[P_HEAD + 16 :, :] = jnp.zeros((full.shape[0] - P_HEAD - 16, HID), F32)
    size = keep.shape[0]
    for out, x in ((keep, place[1]), (give, 1 - place[1])):
        out[...] = full[pl.ds(pl.multiple_of((2 * place[0] + x) * size, 8), size), :]


def second_stream(
    one, mats, bias, column, last, inner, inner_stack, alive, weight, x, s, saved, here, left3, here3, there3, left2, here2,
    there2, left1, here1, there1, lefth, righth,
):
    rows, w = x.shape[1], (mats, 0)
    total = left3.shape[1] // 2
    there = slice(total + here.start, total + here.stop)
    one_row = row_at(1.0, 0, jnp.zeros((16, rows), F32))
    none = jnp.zeros((16, rows), BF16)
    mask, target = s[0:1], s[7:8]
    left1[:, here] = jnp.concatenate([x, jnp.zeros((8, rows), F32)], axis=0).astype(BF16)
    for left in (left2, left3):
        left[HID : HID + 16, here] = one_row.astype(BF16)
        left[HID : HID + 16, there] = none
    lefth[:, there] = one_row.astype(BF16)
    z = dot(one[0], stack_inputs(x)) if saved is None else saved[0]
    yield
    h, t = act(z)
    d1, e1 = slope(h, t), curve(z, t)
    left2[0:HID, here] = h.astype(BF16)
    if saved is None:
        z = times_exact(w, 0, h)
        yield
        z = z + spread(bias[0, 0], rows)
    else:
        z = saved[1]
        yield
    h, t = act(z)
    d2, e2 = slope(h, t), curve(z, t)
    left3[0:HID, here] = h.astype(BF16)
    if saved is None:
        z = times_exact(w, 4, h)
        yield
        z = z + spread(bias[0, 1], rows)
    else:
        z = saved[2]
        yield
    h, t = act(z)
    d3, e3 = slope(h, t), curve(z, t)
    righth[:, here] = h.astype(BF16)
    column = spread(column, rows)
    q = jnp.sum(column * h, axis=0, keepdims=True) + last
    b3 = column * d3
    e3 = column * e3
    cut = b3.astype(BF16)
    there3[:, here] = cut
    c2 = times(w, 6, cut) if saved is None else saved[3]
    yield
    b2 = c2 * d2
    e2 = c2 * e2
    cut = b2.astype(BF16)
    there2[:, here] = cut
    c1 = times(w, 2, cut) if saved is None else saved[4]
    yield
    b1 = c1 * d1
    e1 = c1 * e1
    cut = b1.astype(BF16)
    there1[:, here] = cut
    grad = action_gradient(inner, cut)
    miss = q - target
    half_a = alive * mask * miss
    td = jnp.sum(half_a * miss, axis=1, keepdims=True)
    a_high = half_a.astype(BF16).astype(F32)
    lefth[:, here] = row_at(a_high, 0, row_at(half_a - a_high, 1, jnp.zeros((16, rows), F32))).astype(BF16)
    yield
    size = jnp.sum(grad * grad, axis=0, keepdims=True) + GRAD_FLOOR
    cot = action_rows(s) * weight
    along = jnp.sum(grad * cot, axis=0, keepdims=True)
    v = lax.rsqrt(size) * (cot - grad * (along / size))
    left1[:, there] = jnp.concatenate([jnp.zeros((16, rows), F32), v, jnp.zeros((8, rows), F32)], axis=0).astype(BF16)
    t1 = dot(inner_stack, stack_inputs(v))
    yield
    cut = (d1 * t1).astype(BF16)
    left2[0:HID, there] = cut
    t2 = times(w, 0, cut)
    yield
    cut = (d2 * t2).astype(BF16)
    left3[0:HID, there] = cut
    t3 = times(w, 4, cut)
    yield
    righth[:, there] = (d3 * t3).astype(BF16)
    r = e3 * t3
    here3[:, here] = (half_a * b3 + r).astype(BF16)
    r = dot(mats[0, 6], r.astype(BF16)) * d2 + e2 * t2
    yield
    here2[:, here] = (half_a * b2 + r).astype(BF16)
    r = dot(mats[0, 2], r.astype(BF16)) * d1 + e1 * t1
    yield
    here1[:, here] = (half_a * b1 + r).astype(BF16)
    return td, jnp.sum(half_a, axis=1, keepdims=True)


def second_kernel(live, place, xs, xs_far, sx, sx_far, gx, saved, one, mats, bias, body, head, *refs):
    (grads, sums), scratch = refs[:2], refs[2:]
    left3, here3, there3, left2, here2, there2, left1, here1, there1, lefth, righth = scratch
    rows = xs.shape[1]
    mine = place[1]
    alive = jnp.where(mine == 0, live[0], live[1]).astype(F32)
    read = critic_rows(body, mine)
    column, last = head_column(head, mine)
    column = wide(column)
    inner, inner_stack = inner_rows(read), stack_weights(read(16, 24))
    weight = 2.0 * DIVERSITY_WEIGHT * alive / (gx[7:8, :] - 1.0)
    td = bias_sum = jnp.zeros((1, 1), F32)
    step = rows // 2
    for td_part, bias_part in interleave(
        *[
            second_stream(
                one, mats, bias, column, last, inner, inner_stack, alive, weight[:, start : start + step],
                x[:, start : start + step], s[:, start : start + step],
                None if i else [saved[k, :, start : start + step] for k in range(5)],
                slice(i * rows + start, i * rows + start + step), *scratch,
            )
            for start in range(0, rows, step)
            for i, (x, s) in enumerate(((xs, sx), (xs_far, sx_far)))
        ]
    ):
        td, bias_sum = td + td_part, bias_sum + bias_part

    def layer(left, here, there):
        n = here.shape[1]
        return dot_rows(left[:, 0:n], here[...]) + 0.5 * dot_rows(left[:, n:], there[...])

    grads[0:TWO, :] = layer(left1, here1, there1)[0:TWO]
    grads[TWO:THREE, :] = layer(left2, here2, there2)[0 : HID + 1]
    grads[THREE:BODY, :] = layer(left3, here3, there3)[0 : HID + 1]
    n = here3.shape[1]
    by_head = dot_rows(lefth[:, 0:n], righth[:, 0:n])
    grads[BODY : BODY + 1, :] = 2.0 * (by_head[0:1] + by_head[1:2]) + dot_rows(lefth[:, n:], righth[:, n:])[0:1]
    lane = lax.broadcasted_iota(jnp.int32, (1, HID), 1)
    grads[BODY + 1 : BODY + 2, :] = jnp.where(lane == 0, 2.0 * bias_sum, 0.0)
    grads[BODY + 2 :, :] = jnp.zeros((grads.shape[0] - BODY - 2, HID), F32)
    sums[...] = jnp.where(lax.broadcasted_iota(jnp.int32, (1, 128), 1) == 0, td, 0.0)


def deal_kernel(place, critic, keep, got, *out):
    n = len(out)
    part = critic.shape[0] // n
    policy = keep[...] + got[...]
    for k in range(n):
        to = jnp.bitwise_xor(place[2], k)
        out[k][0:part, :] = critic[pl.ds(pl.multiple_of(to * part, 8), part), :]
        out[k][part:, :] = policy


def reduce_kernel(part, place, one, two, *refs):
    ins, (out, sums) = refs[:-2], refs[-2:]
    total = ins[0][...]
    for r in ins[1:]:
        total = total + r[...]
    out[...] = total
    critic, policy = total[:part], total[part:]
    square = jnp.sum(jnp.sum(critic * critic, axis=0, keepdims=True), axis=1, keepdims=True)
    once = (place[2] == 0).astype(F32)
    square = square + once * jnp.sum(jnp.sum(policy * policy, axis=0, keepdims=True), axis=1, keepdims=True)
    lane = lax.broadcasted_iota(jnp.int32, (1, 128), 1)
    row = one[...] + two[...] + jnp.where(lane == 5, square, 0.0)
    sums[...] = jnp.broadcast_to(row, sums.shape)


def piece_kernel(whole, out):
    out[...] = whole[0 : out.shape[0], :]


def adam(weights, moment, second, grads):
    moment_new = BETA_ONE * (moment + grads)
    second_new = BETA_TWO * (second + grads * grads)
    root = (1.0 / (1.0 - BETA_TWO**STEPS_DONE)) ** 0.5
    bottom = (root * second_new) * lax.rsqrt(second_new) + ADAM_EPSILON
    guess = pltpu.reciprocal(bottom, approx=True)
    inverse = guess * (2.0 - bottom * guess)
    step = ((LEARN_RATE / (1.0 - BETA_ONE**STEPS_DONE)) * moment_new) * inverse
    return (1.0 - LEARN_RATE * DECAY_RATE) * weights - step, moment_new, second_new


def scalars_of(sums):
    total = jnp.sum(sums[...], axis=0, keepdims=True)
    entropy, count = total[:, 3:4], total[:, 4:5]
    grad_temp = -entropy / count
    norm = jnp.sqrt(total[:, 5:6] / (count * count) + grad_temp * grad_temp)
    factor = CLIP_NORM / jnp.maximum(norm, CLIP_NORM)
    return total, entropy, count, grad_temp, norm, factor


def put(refs, at, got):
    for r, value in zip(refs, got):
        r[at] = value.astype(r.dtype)


def update_kernel(n_z, part, small, sources, n_pieces, n_blocks, place, log_temp, log_mom, log_sq, sums, *refs):
    refs = list(refs)
    take = lambda n: [refs.pop(0) for _ in range(n)]
    pieces, blocks = take(n_pieces), take(n_blocks)
    w, m, v, t, hw, hm, hv, ht, pw, pm, pv, phw, phm, phv = take(14)
    outs = take(23)
    total, policy = take(2)
    near, sem, body_sem = take(23), *take(2)
    row, entropy, count, grad_temp, norm, factor = scalars_of(sums)
    scale = factor / count
    for k, i, first, start, stop in sources:
        piece = pieces[i]
        c = jnp.bitwise_xor(place[1], k // n_z)
        z = jnp.bitwise_xor(place[2], k % n_z)
        for side in range(2):
            at = pl.ds(4 * (part * z + start) + 2 * side + c, stop - start, stride=4)
            total[at, :] = piece[first : first + stop - start, side * 128 : (side + 1) * 128]
    copies = []

    def send(i, j):
        copies.extend(start_copies(near[i:j], outs[i:j], sem.at[pl.ds(i, j - i)]))

    rows = w.shape[0]
    step = BLOCK
    for i, start in enumerate(range(0, rows, step)):
        at = pl.ds(start, min(step, rows - start))
        new, mom, sq = adam(w[at, :], m[at, :], v[at, :], total[at, :] * scale)
        tgt = t[at, :] + POLYAK_RATE * (new - t[at, :])
        put(near[2:7], (at, slice(None)), (new, mom, sq, tgt, new))
        copies += start_copies([r.at[at, :] for r in near[2:6]], [r.at[at, :] for r in outs[2:6]], body_sem.at[i])
    send(6, 7)
    for c in range(2):
        at = slice(c, c + 1)
        rows8 = [total[4 * (BODY + k) + 2 * side + c : 4 * (BODY + k) + 2 * side + c + 1, :] for k, side in ((0, 0), (0, 1), (1, 0))]
        grad = jnp.concatenate([rows8[0], rows8[1], rows8[2][:, 0:1]], axis=1)
        new, mom, sq = adam(hw[at, :], hm[at, :], hv[at, :], grad * scale)
        tgt = ht[at, :] + POLYAK_RATE * (new - ht[at, :])
        put(near[7:12], (at, slice(None)), (new, mom, sq, tgt, new))
    lane = lax.broadcasted_iota(jnp.int32, (1, 128), 1)
    near[0][...] = jnp.where(lane == 3, -log_temp[0] * entropy, row)[:, 0:5]
    near[1][...] = norm
    one = lambda v: jnp.full((1, 1), v[0])
    put(near[20:23], (slice(0, 1),), adam(one(log_temp), one(log_mom), one(log_sq), factor * grad_temp))
    send(0, 2)
    send(7, 12)
    send(20, 23)
    first = 0
    for block in blocks:
        for k in range(block.shape[0] // small):
            at = 2 * jnp.bitwise_xor(place[0], first + k // 2) + jnp.bitwise_xor(place[1], k % 2)
            policy[pl.ds(pl.multiple_of(at * small, 8), small), :] = block[k * small : (k + 1) * small, :]
        first += block.shape[0] // (2 * small)
    n = S_DIM
    for mine, at in (
        (slice(0, n + 1), slice(0, n + 1)),
        (slice(P_TWO, P_TWO + HID + 1), slice(n + 1, n + 2 + HID)),
        (slice(P_THREE, P_THREE + HID + 1), slice(n + 2 + HID, n + 3 + 2 * HID)),
    ):
        new, mom, sq = adam(pw[at], pm[at], pv[at], policy[mine, :] * scale)
        put(near[12:16], (at,), (new, mom, sq, new))
    send(12, 16)
    by_head = policy[P_HEAD : P_HEAD + 16, :]
    last = jnp.broadcast_to(policy[P_LAST + 1 : P_LAST + 2, 0:16], (8, 16)).T[:, 0:1]
    for r, at in ((1, slice(0, A_DIM)), (9, slice(A_DIM, 2 * A_DIM))):
        grad = jnp.concatenate([by_head[r : r + A_DIM], last[r : r + A_DIM]], axis=1)
        new, mom, sq = adam(phw[at, :], phm[at, :], phv[at, :], grad * scale)
        put(near[16:20], (at, slice(None)), (new, mom, sq, new))
    send(16, 20)
    for copy in copies:
        copy.wait()


def join_kernel(n, plan, *refs):
    for out, slices in zip(refs[n:], plan):
        at = 0
        for i, start, stop in slices:
            out[at : at + stop - start, :] = refs[i][start:stop, :]
            at += stop - start


def join(arrays, plan):
    outs = [shape(sum(stop - start for _, start, stop in slices), HID) for slices in plan]
    return call(functools.partial(join_kernel, len(arrays), plan), outs, [VMEM] * len(arrays), us=0.3)(*arrays)


def flat(v):
    return jnp.transpose(v.reshape(2, -1, 2, 128), (1, 2, 0, 3)).reshape(-1, 128)


def unflat(v):
    return jnp.transpose(v.reshape(-1, 2, 2, 128), (2, 0, 1, 3)).reshape(2, -1, HID)


def per_device(
    members,
    dp,
    states,
    actions,
    rewards,
    next_states,
    terminal,
    valid_rows,
    noise_seeds,
    member_live,
    critic_body,
    critic_body_mom,
    critic_body_sq,
    critic_body_tgt,
    critic_head,
    critic_head_mom,
    critic_head_sq,
    critic_head_tgt,
    policy_body,
    policy_body_mom,
    policy_body_sq,
    policy_head,
    policy_head_mom,
    policy_head_sq,
    log_temp,
    log_temp_mom,
    log_temp_sq,
):
    rows = states.shape[0]
    n_z = dp // 2
    part = -(-CRITIC_ROWS // (8 * n_z)) * 8
    small = -(-POLICY_ROWS // (16 * members)) * 8
    m, d = lax.axis_index("member"), lax.axis_index("dp")
    place = jnp.stack([m, d // n_z, d % n_z]).astype(jnp.int32)

    def across(value, axis, n, to):
        return lax.ppermute(value, axis, [(i, to(i)) for i in range(n)])

    def to_member(value, bit):
        return across(value, "member", members, lambda i: i ^ bit)

    def to_pair(value):
        return across(value, "dp", dp, lambda i: i ^ n_z)

    def along(value, offset):
        return across(value, "dp", dp, lambda i: i ^ offset)

    square = lambda v: v.reshape(rows // 128, 128)
    turned = [policy_head.T, policy_head_mom.T, policy_head_sq.T]
    body, mom, sq, body_tgt = flat(critic_body), flat(critic_body_mom), flat(critic_body_sq), flat(critic_body_tgt)
    like = lambda *arrays: [shape(*a.shape, dtype=a.dtype) for a in arrays]
    first = call(first_kernel, shape(8, 128), [SMEM], us=8.0, limit=1)(place)
    xs, xn, xp, aux, *actor_weights = call(
        actor_kernel,
        [shape(24, rows), shape(24, rows), shape(24, rows), shape(32, rows)] + trunk_arrays(1, S_DIM),
        [VMEM] * 10 + [SMEM],
        us=3.0,
    )(
        first, states.T, actions.T, next_states.T, noise_seeds.T, square(rewards), square(terminal), square(valid_rows),
        policy_body, turned[0], log_temp,
    )
    xs_far = to_pair(xs)
    ensemble, saved, *weights = call(
        critic_kernel,
        [shape(16, rows), shape(5, HID, rows)] + trunk_arrays(1, X_DIM),
        [SMEM, SMEM] + [VMEM] * 7,
        trunk_scratch(3, X_DIM) + [pltpu.VMEM((4, HID, 128), F32)],
        us=8.0,
    )(
        member_live, place, xs, xn, xp, body, critic_head, body_tgt, critic_head_tgt
    )
    bit = 1
    while bit * 2 < members:
        other = to_member(ensemble, bit)
        k = lax.broadcasted_iota(jnp.int32, ensemble.shape, 0)
        ensemble = jnp.where(k == 7, jnp.minimum(ensemble, other), ensemble + other)
        bit *= 2
    sx, gx, sums_joint = call(
        joint_kernel, [shape(8, rows), shape(8, rows), shape(1, 128)], [VMEM, VMEM, VMEM, SMEM], us=0.7
    )(ensemble, to_member(ensemble, bit), aux, log_temp)
    sx_far = to_pair(sx)
    keep, give = call(
        policy_kernel,
        [shape(small, HID), shape(small, HID)],
        [SMEM] + [VMEM] * 7 + [SMEM],
        [pltpu.VMEM((2 * members * small, HID), F32)],
        us=3.0,
    )(place, xs, aux, gx, *actor_weights, turned[0], log_temp)
    got = to_pair(give)
    both = 2 * rows
    left, side = pltpu.VMEM((HID + 16, 2 * both), BF16), pltpu.VMEM((HID, both), BF16)
    scratch = [left, side, side, left, side, side, pltpu.VMEM((32, 2 * both), BF16), side, side]
    scratch = scratch + [pltpu.VMEM((16, 2 * both), BF16), pltpu.VMEM((HID, 2 * both), BF16)]
    grads, sums_second = call(
        second_kernel,
        [shape(part * n_z, HID), shape(1, 128)],
        [SMEM, SMEM] + [VMEM] * 11,
        scratch,
        us=8.0,
        limit=42,
    )(member_live, place, xs, xs_far, sx, sx_far, gx, saved, *weights, body, critic_head)
    message = shape(part + small, HID)
    dealt = call(deal_kernel, [message] * n_z, [SMEM, VMEM, VMEM, VMEM], us=0.5)(place, grads, keep, got)
    arrived = [dealt[0]] + [along(dealt[k], k) for k in range(1, n_z)]
    whole, sums = call(
        functools.partial(reduce_kernel, part),
        [message, shape(members * dp, 128)],
        [SMEM] + [VMEM] * (2 + n_z),
    )(place, sums_joint, sums_second, *arrived)
    sums = lax.all_to_all(sums, ("member", "dp"), 0, 0, tiled=True)
    piece = call(piece_kernel, shape(part, HID), [VMEM], us=8.0)(whole)
    pieces, bit = {0: piece, n_z: to_pair(whole)}, 1
    while bit < n_z:
        pieces[bit] = along(piece, bit)
        bit *= 2
    at_hand = sorted(pieces)
    *values, sums = lax.optimization_barrier((*[pieces[k] for k in at_hand], sums))
    pieces = dict(zip(at_hand, values))
    found = {k: [(pieces[k], 0, 0, part)] for k in at_hand}
    actor = [[(0, part, part + small), (1, part, part + small)]]
    (block,) = join([whole, pieces[n_z]], actor)
    if dp > 2:
        found[dp - 1] = [(along(pieces[0], dp - 1), 0, 0, part)]
    bits = dp.bit_length() - 1
    for level in range(2, bits):
        paths = {}
        for k in range(dp):
            if bin(k).count("1") == level:
                low, rest = k & -k, k & (k - 1)
                cut = part // 16 * 8 if k < n_z and level == 2 else 0
                paths.setdefault(low, []).append((k, cut, part))
                if cut:
                    paths.setdefault(rest, []).append((k, 0, cut))
        inputs = sorted({k & ~bit for bit, slices in paths.items() for k, _, _ in slices})
        plan = []
        for bit, slices in paths.items():
            plan.append([])
            for k, start, stop in slices:
                first = found[k & ~bit][0][1]
                plan[-1].append((inputs.index(k & ~bit), first + start, first + stop))
        sent = join([found[k][0][0] for k in inputs], plan)
        level_found = {}
        for (bit, slices), message in zip(paths.items(), sent):
            came, at = along(message, bit), 0
            for k, start, stop in slices:
                level_found.setdefault(k, []).append((came, at, start, stop))
                at += stop - start
        if level + 1 < bits:
            whole_ones = sorted(level_found)
            rows_of = [join([v[0] for v in sorted(level_found[k], key=lambda v: v[2])], [[(i, v[1], v[1] + v[3] - v[2]) for i, v in enumerate(sorted(level_found[k], key=lambda v: v[2]))]])[0] for k in whole_ones]
            level_found = {k: [(v, 0, 0, part)] for k, v in zip(whole_ones, rows_of)}
        found.update(level_found)
    blocks = [block] + [to_member(block, k) for k in range(1, members)]
    arrays, sources = [], []
    for k, places in sorted(found.items()):
        for array, at, start, stop in places:
            if not any(array is other for other in arrays):
                arrays.append(array)
            sources.append((k, [array is other for other in arrays].index(True), at, start, stop))
    halved = lambda a: shape(*a.shape, dtype=BF16)
    heads = [critic_head, critic_head_mom, critic_head_sq, critic_head_tgt]
    single = shape(1, 1)
    outs = [shape(1, 5), single] + like(body, body, body, body) + [halved(body)] + like(*heads) + [halved(critic_head)]
    outs = outs + like(policy_body, policy_body, policy_body) + [halved(policy_body)] + like(*turned) + [halved(turned[0])]
    outs = outs + [single, single, single]
    new = call(
        functools.partial(update_kernel, n_z, part, small, sources, len(arrays), len(blocks)),
        outs,
        [SMEM] * 4 + [VMEM] * (1 + len(arrays) + len(blocks) + 14),
        [pltpu.VMEM((4 * n_z * part, 128), F32), pltpu.VMEM((2 * members * small, HID), F32)]
        + buffers(*outs)
        + [pltpu.SemaphoreType.DMA((-(-body.shape[0] // BLOCK), 4))],
        us=5.0,
        out_specs=[HBM] * len(outs),
    )(
        place, log_temp, log_temp_mom, log_temp_sq, sums, *arrays, *blocks, body, mom, sq, body_tgt,
        *heads, policy_body, policy_body_mom, policy_body_sq, *turned,
    )
    new = list(new)
    new = [v[0] for v in new[:2]] + [unflat(v) for v in new[2:7]] + new[7:16] + [v.T for v in new[16:20]] + [v[0] for v in new[20:]]
    return tuple(new)


def solution(mesh):
    row, line = P("dp", None), P("dp")
    stack, flat = P("member", None, None), P("member", None)
    return jax.shard_map(
        functools.partial(per_device, mesh.shape["member"], mesh.shape["dp"]),
        mesh=mesh,
        in_specs=(row, row, line, row, line, line, row, P("member")) + (stack,) * 4 + (flat,) * 4 + (P(),) * 9,
        out_specs=(P(), P()) + (stack,) * 5 + (flat,) * 5 + (P(),) * 11,
        check_vma=False,
    )
```

```python
import functools

import jax
import jax.numpy as jnp
from jax import lax
from jax.experimental import pallas as pl
from jax.experimental.pallas import tpu as pltpu
from jax.sharding import PartitionSpec as P

STEPS_DONE = 5
DISCOUNT = 0.99
POLYAK_RATE = 0.005
ENTROPY_TARGET = -6.0
DIVERSITY_WEIGHT = 1.0
LEARN_RATE = 0.05
BETA_ONE = 0.5
BETA_TWO = 0.5
DECAY_RATE = 0.01
ADAM_EPSILON = 1e-08
GRAD_FLOOR = 0.0001
CLIP_NORM = 1.0
LOGSTD_LOW = -5.0
LOGSTD_HIGH = 2.0
LOG_TWO = 0.6931471805599453
HALF_LOG_TWOPI = 0.9189385332046727
FAR_VALUE = 1e30

F32 = jnp.float32
BF16 = jnp.bfloat16
HID = 256
S_DIM = 17
A_DIM = 6
X_DIM = S_DIM + A_DIM
TWO = X_DIM + 1
THREE = TWO + HID + 1
BODY = THREE + HID + 1
CRITIC_ROWS = 544
P_TWO = 24
P_THREE = 288
P_LAST = 544
P_HEAD = 552
POLICY_ROWS = 576
BLOCK = 272
VMEM = pl.BlockSpec(memory_space=pltpu.VMEM)
SMEM = pl.BlockSpec(memory_space=pltpu.SMEM)
HBM = pl.BlockSpec(memory_space=pltpu.HBM)


def call(kernel, outs, in_specs, scratch=(), us=1.0, out_specs=None, limit=32):
    return pl.pallas_call(
        kernel,
        out_shape=outs,
        in_specs=in_specs,
        out_specs=out_specs or jax.tree.map(lambda _: VMEM, outs),
        scratch_shapes=list(scratch),
        compiler_params=pltpu.CompilerParams(vmem_limit_bytes=limit * 2**20),
        cost_estimate=pl.CostEstimate(flops=int(us * 1.15e9), bytes_accessed=0, transcendentals=0),
    )


def buffers(*arrays):
    return [pltpu.VMEM(a.shape, a.dtype) for a in arrays] + [pltpu.SemaphoreType.DMA((len(arrays),))]


def start_copies(sources, targets, sem):
    copies = [pltpu.make_async_copy(a, b, sem.at[i]) for i, (a, b) in enumerate(zip(sources, targets))]
    for copy in copies:
        copy.start()
    return copies


def shape(*dims, dtype=F32):
    return jax.ShapeDtypeStruct(dims, dtype)


def dot(a, b):
    return lax.dot_general(a, b, (((1,), (0,)), ((), ())), preferred_element_type=F32)


def dot_rows(a, b):
    return lax.dot_general(a, b, (((1,), (1,)), ((), ())), preferred_element_type=F32)


def halves(w):
    high = w.astype(BF16)
    return high, (w - high.astype(F32)).astype(BF16)


def stack_weights(w):
    high = (0.5 * w).astype(BF16).astype(F32)
    return jnp.concatenate([high, high, 0.5 * w - high], axis=0).T.astype(BF16)


def stack_inputs(v):
    high = v.astype(BF16).astype(F32)
    return jnp.concatenate([high, v - high, high], axis=0).astype(BF16)


def act(z):
    t = jnp.tanh(z)
    return z + z * t, t


def slope(h, t):
    return (1.0 + h) + t * (1.0 - h)


def curve(z, t):
    return (1.0 - t * t) * (1.0 - z * t)


def wide(column):
    return jnp.broadcast_to(column, (column.shape[0], 128))


def spread(column, rows):
    return jnp.concatenate([column] * (rows // 128), axis=1)


def action_rows(v):
    k = lax.broadcasted_iota(jnp.int32, v.shape, 0)
    return jnp.where((k >= 1) & (k <= A_DIM), v, 0.0)


def row_at(v, k, like):
    return jnp.where(lax.broadcasted_iota(jnp.int32, like.shape, 0) == k, v, like)


def lane_row(block):
    return jnp.concatenate([block[i : i + 1] for i in range(block.shape[0])], axis=1)


def interleave(*streams):
    results, active = [None] * len(streams), list(enumerate(streams))
    while active:
        left = []
        for i, stream in active:
            try:
                next(stream)
                left.append((i, stream))
            except StopIteration as end:
                results[i] = end.value
        active = left
    return results


def critic_rows(ref, c):
    def read(a, b):
        return jnp.concatenate([ref[pl.ds(4 * a + 2 * t + c, b - a, stride=4), :] for t in range(2)], axis=1)

    return read


def load_trunk(body, n_in, one, mats, bias, i, backward=False):
    one[i] = stack_weights(body(0, n_in + 1))
    yield
    for k, start in enumerate((n_in + 1, n_in + 2 + HID)):
        high, low = halves(0.5 * body(start, start + HID))
        mats[i, 4 * k] = high.T
        mats[i, 4 * k + 1] = low.T
        if backward:
            mats[i, 4 * k + 2] = high
            mats[i, 4 * k + 3] = low
        bias[i, k] = wide(0.5 * body(start + HID, start + HID + 1).T)
        yield


def trunk_arrays(n, n_in):
    return [shape(n, HID, 3 * (n_in + 1), dtype=BF16), shape(n, 8, HID, HID, dtype=BF16), shape(n, 2, HID, 128)]


def trunk_scratch(n, n_in):
    return [pltpu.VMEM(a.shape, a.dtype) for a in trunk_arrays(n, n_in)]


def times(w, k, h):
    mats, i = w
    return dot(mats[i, k], h) + dot(mats[i, k + 1], h)


def times_exact(w, k, h):
    mats, i = w
    high, low = halves(h)
    return dot(mats[i, k], high) + dot(mats[i, k + 1], high) + dot(mats[i, k], low)


def policy_head_rows(turned):
    one = jnp.zeros((1, HID + 1), F32)
    return jnp.concatenate([one, turned[:A_DIM], one, one, turned[A_DIM:], one], axis=0)


def noise_of(seed_row):
    k = lax.broadcasted_iota(jnp.int32, (8, seed_row.shape[1]), 0).astype(F32) - 1.0
    return 1.7 * jnp.sin(0.618034 * seed_row + 2.39996 * k)


def actor_stream(one, mats, bias, head, head_bias, x, noise):
    rows = x.shape[1]
    z = dot(one[0], stack_inputs(x))
    yield
    z = times((mats, 0), 0, act(z)[0].astype(BF16))
    yield
    z = times((mats, 0), 4, act(z + spread(bias[0, 0], rows))[0].astype(BF16))
    yield
    high, low = halves(act(z + spread(bias[0, 1], rows))[0])
    out = dot(head, high)
    out = out[:16] + out[16:] + dot(head[:16], low) + spread(head_bias, rows)
    yield
    mean, raw = out[:8], out[8:]
    turned = jnp.tanh(raw)
    log_std = LOGSTD_LOW + 0.5 * (LOGSTD_HIGH - LOGSTD_LOW) * (turned + 1.0)
    deviation = jnp.exp(log_std) * noise
    u = mean + deviation
    soft = jnp.maximum(-2.0 * u, 0.0) + jnp.log(1.0 + jnp.exp(-jnp.abs(2.0 * u)))
    squash = 2.0 * (LOG_TWO - u - soft)
    terms = -0.5 * noise * noise - log_std - HALF_LOG_TWOPI - squash
    log_prob = jnp.sum(action_rows(terms), axis=0, keepdims=True)
    return jnp.tanh(u), turned, deviation, log_prob


def first_kernel(place, out):
    out[...] = jnp.full(out.shape, (place[0] == 0).astype(F32))


def actor_kernel(
    first, states, actions, next_states, seeds, rewards, terminal, valid, body, head, log_temp, xs, xn, xp, aux, one, mats, bias
):
    rows = states.shape[1]
    ones = jnp.ones((1, rows), F32)
    for x, source in ((xs, states), (xn, next_states), (xp, states)):
        x[0:S_DIM, :] = source[...]
        x[X_DIM : X_DIM + 1, :] = ones
    xs[S_DIM:X_DIM, :] = actions[...]
    seed = seeds[...].astype(F32)
    loading = load_trunk(lambda a, b: body[a:b], S_DIM, one, mats, bias, 0, backward=True)
    next(loading)
    head_rows = policy_head_rows(head[...])
    head_w, head_b = jnp.concatenate(halves(head_rows[:, :HID]), axis=0), wide(head_rows[:, HID:])
    carry = 1.0 - lane_row(terminal[...].astype(F32))
    temper = jnp.exp(log_temp[0])
    now_in = jnp.concatenate([states[...], ones], axis=0)
    later_in = jnp.concatenate([next_states[...], ones], axis=0)
    half = rows // 2
    done = interleave(
        *[
            actor_stream(one, mats, bias, head_w, head_b, x[:, i : i + half], noise_of(seed[k : k + 1, i : i + half]))
            for i in (0, half)
            for x, k in ((later_in, 1), (now_in, 0))
        ],
        loading,
    )[:-1]
    later = [jnp.concatenate(v, axis=1) for v in zip(*done[0::2])]
    now = [jnp.concatenate(v, axis=1) for v in zip(*done[1::2])]
    xn[S_DIM:X_DIM, :] = later[0][1 : 1 + A_DIM]
    aux[0:1, :] = lane_row(rewards[...]) - DISCOUNT * carry * temper * later[3]
    aux[1:2, :] = DISCOUNT * carry
    aux[2:3, :] = lane_row(valid[...].astype(F32))
    action, turned, deviation, log_prob = now
    xp[S_DIM:X_DIM, :] = action[1 : 1 + A_DIM]
    aux[3:4, :] = log_prob
    aux[4:5, :] = spread(first[0:1], rows)
    aux[5:8, :] = jnp.zeros((3, rows), F32)
    aux[8:16, :] = action_rows(action)
    aux[16:24, :] = action_rows(turned)
    aux[24:32, :] = action_rows(deviation)


def head_column(head, c):
    row = head[pl.ds(c, 1), :]
    return row[:, :HID].T, row[:, HID:]


def inner_rows(read):
    return jnp.concatenate(halves(0.5 * read(16, 24)), axis=0)


def action_gradient(inner, y):
    grad = dot(inner, y)
    return action_rows(grad[:8] + grad[8:])


def data_stream(one, mats, bias, i, column, inner, x, save):
    rows, w = x.shape[1], (mats, i)
    z = dot(one[i], x)
    save(0, z)
    yield
    h, t = act(z)
    d1 = slope(h, t)
    z = times_exact(w, 0, h)
    yield
    z = z + spread(bias[i, 0], rows)
    save(1, z)
    h, t = act(z)
    d2 = slope(h, t)
    z = times_exact(w, 4, h)
    yield
    z = z + spread(bias[i, 1], rows)
    save(2, z)
    h, t = act(z)
    c = times(w, 6, (spread(column, rows) * slope(h, t)).astype(BF16))
    yield
    save(3, c)
    c = times(w, 2, (c * d2).astype(BF16))
    yield
    save(4, c)
    grad = action_gradient(inner, (c * d1).astype(BF16))
    yield
    size = jnp.sum(grad * grad, axis=0, keepdims=True) + GRAD_FLOOR
    return grad * lax.rsqrt(size)


def target_stream(one, mats, bias, i, column, last, x):
    rows, w = x.shape[1], (mats, i)
    z = dot(one[i], x)
    yield
    z = times(w, 0, act(z)[0].astype(BF16))
    yield
    z = times(w, 4, act(z + spread(bias[i, 0], rows))[0].astype(BF16))
    yield
    h = act(z + spread(bias[i, 1], rows))[0]
    return jnp.sum(spread(column, rows) * h, axis=0, keepdims=True) + last


def chosen_stream(one, mats, bias, i, column, last, inner, x):
    rows = x.shape[1]
    z = dot(one[i], x)
    yield
    h, t = act(z)
    d1 = slope(h, t)
    z = dot(mats[i, 0], h.astype(BF16))
    yield
    h, t = act(z + spread(bias[i, 0], rows))
    d2 = slope(h, t)
    z = dot(mats[i, 4], h.astype(BF16))
    yield
    h, t = act(z + spread(bias[i, 1], rows))
    column = spread(column, rows)
    q = jnp.sum(column * h, axis=0, keepdims=True) + last
    c = dot(mats[i, 6], (column * slope(h, t)).astype(BF16))
    yield
    c = dot(mats[i, 2], (c * d2).astype(BF16))
    yield
    return q, action_gradient(inner, (c * d1).astype(BF16))


def critic_kernel(live, place, xs, xn, xp, body, head, body_tgt, head_tgt, out, saved, *refs):
    mine, scratch, columns = refs[:3], refs[3:6], refs[6]
    order = [place[1], 1 - place[1]]
    lasts, inners, trunks, loading = [], [], [], []
    for i in range(4):
        c = order[i % 2]
        read = critic_rows((body, body_tgt)[i // 2], c)
        trunks.append((*mine, 0) if i == 0 else (*scratch, i - 1))
        loading.append(load_trunk(read, X_DIM, *trunks[i], backward=i < 2))
        next(loading[-1])
        column, last = head_column((head, head_tgt)[i // 2], c)
        columns[i] = wide(column)
        lasts.append(last)
        if i < 2:
            inners.append(inner_rows(read))
    alive = [live[c].astype(F32) for c in order]
    rows = xs.shape[1]
    step = 256
    for start in range(0, rows, step):
        at = slice(start, start + step)
        data, later, chosen = stack_inputs(xs[:, at]), stack_inputs(xn[:, at]), stack_inputs(xp[:, at])

        def save(k, value, at=at):
            saved[k, :, at] = value

        done = interleave(
            data_stream(*trunks[0], columns[0], inners[0], data, save),
            data_stream(*trunks[1], columns[1], inners[1], data, lambda k, value: None),
            *[chosen_stream(*trunks[c], columns[c], lasts[c], inners[c], chosen) for c in range(2)],
            *[target_stream(*trunks[2 + c], columns[2 + c], lasts[2 + c], later) for c in range(2)],
            *loading,
        )
        loading = []
        unit, now, value = done[0:2], done[2:4], done[4:6]
        lowest = [jnp.where(alive[c] > 0, value[c], FAR_VALUE) for c in range(2)]
        total_n, total_q, total_g = [alive[0] * a + alive[1] * b for a, b in (unit, *zip(*now))]
        out[0:8, at] = row_at(jnp.minimum(lowest[0], lowest[1]), 7, row_at(alive[0] + alive[1], 0, total_n))
        out[8:16, at] = row_at(total_q, 0, total_g)


def merge(a, b):
    k = lax.broadcasted_iota(jnp.int32, a.shape, 0)
    return jnp.where(k == 7, jnp.minimum(a, b), a + b)


def joint_kernel(mine, other, aux, log_temp, sx, gx, sums):
    both = merge(mine[...], other[...])
    unit, grad = both[:8], both[8:]
    mask, log_prob = aux[2:3, :], aux[3:4, :]
    members = both[0:1]
    target = aux[0:1, :] + aux[1:2, :] * both[7:8]
    unit = action_rows(unit)
    sx[...] = row_at(target, 7, row_at(mask, 0, mask * unit))
    gx[...] = row_at(members, 7, grad)
    temper = jnp.exp(log_temp[0])
    spread = jnp.sum(mask * (jnp.sum(unit * unit, axis=0, keepdims=True) - members), axis=1, keepdims=True)
    actor = jnp.sum(mask * (temper * log_prob - both[8:9] / members), axis=1, keepdims=True)
    entropy = jnp.sum(mask * (log_prob + ENTROPY_TARGET), axis=1, keepdims=True)
    count = jnp.sum(mask, axis=1, keepdims=True)
    lane = lax.broadcasted_iota(jnp.int32, (1, 128), 1)
    row = jnp.where(lane == 1, spread, 0.0) + jnp.where(lane == 2, actor, 0.0)
    row = row + jnp.where(lane == 3, entropy, 0.0) + jnp.where(lane == 4, count, 0.0)
    sums[...] = row * aux[4:5, 0:128]


def policy_stream(one, mats, bias, head_back, x, rows8, by_log):
    rows, w = x.shape[1], (mats, 0)
    z = dot(one[0], stack_inputs(x))
    yield
    h, t = act(z)
    d1, h1 = slope(h, t), h.astype(BF16)
    z = times(w, 0, h1)
    yield
    h, t = act(z + spread(bias[0, 0], rows))
    d2, h2 = slope(h, t), h.astype(BF16)
    z = times(w, 4, h2)
    yield
    h, t = act(z + spread(bias[0, 1], rows))
    action, turned, deviation, by_action = rows8
    by_u = by_action * (1.0 - action * action) + by_log * 2.0 * action
    by_std = by_u * deviation - by_log
    by_raw = action_rows(by_std * (0.5 * (LOGSTD_HIGH - LOGSTD_LOW)) * (1.0 - turned * turned))
    by_out = jnp.concatenate([action_rows(by_u), by_raw], axis=0)
    high, low = halves(by_out)
    f3 = (dot(head_back, jnp.concatenate([high, low, high], axis=0)) * slope(h, t)).astype(BF16)
    yield
    f2 = (times(w, 6, f3) * d2).astype(BF16)
    yield
    f1 = (times(w, 2, f2) * d1).astype(BF16)
    yield
    return h1, h2, h.astype(BF16), f1, f2, f3, high, low, by_out


def policy_kernel(place, xs, aux, gx, one, mats, bias, head, log_temp, keep, give, full):
    rows = xs.shape[1]
    n = S_DIM
    head_high, head_low = halves(0.5 * policy_head_rows(head[...])[:, :HID])
    head_back = jnp.concatenate([head_high, head_high, head_low], axis=0).astype(F32).T.astype(BF16)
    x = row_at(1.0, n, xs[...])
    mask, members = aux[2:3, :], gx[7:8, :]
    by_action = -(mask / members) * action_rows(gx[...])
    by_log = jnp.exp(log_temp[0]) * mask
    rows8 = (aux[8:16, :], aux[16:24, :], aux[24:32, :], by_action)
    step = rows // 4
    cut = lambda v, i: v[:, i * step : (i + 1) * step]
    streams = [
        policy_stream(one, mats, bias, head_back, cut(x[: n + 1], i), [cut(v, i) for v in rows8], cut(by_log, i))
        for i in range(4)
    ]
    h1, h2, h3, f1, f2, f3, high, low, by_out = [jnp.concatenate(v, axis=1) for v in zip(*interleave(*streams))]
    ones = row_at(1.0, 0, jnp.zeros((16, rows), F32)).astype(BF16)
    start = jnp.where(lax.broadcasted_iota(jnp.int32, x.shape, 0) <= n, x, 0.0).astype(BF16)
    full[0:P_TWO, :] = dot_rows(start, f1)
    full[P_TWO:P_THREE, :] = dot_rows(jnp.concatenate([h1, ones], axis=0), f2)[: HID + 8]
    layer = dot_rows(jnp.concatenate([h2, ones], axis=0), f3)
    full[P_THREE : P_THREE + HID, :] = layer[:HID]
    last = wide(jnp.sum(by_out, axis=1, keepdims=True)).T[0:1]
    last = jnp.concatenate([last, jnp.zeros((1, HID - 16), F32)], axis=1)
    full[P_LAST:P_HEAD, :] = row_at(last, 1, layer[HID : HID + 8])
    by_head = dot_rows(jnp.concatenate([high, low], axis=0), h3)
    full[P_HEAD : P_HEAD + 16, :] = by_head[:16] + by_head[16:]
    full[P_HEAD + 16 :, :] = jnp.zeros((full.shape[0] - P_HEAD - 16, HID), F32)
    size = keep.shape[0]
    for out, x in ((keep, place[1]), (give, 1 - place[1])):
        out[...] = full[pl.ds(pl.multiple_of((2 * place[0] + x) * size, 8), size), :]


def second_stream(
    one, mats, bias, column, last, inner, inner_stack, alive, weight, x, s, saved, here, left3, here3, there3, left2, here2,
    there2, left1, right1,
):
    rows, w = x.shape[1], (mats, 0)
    total = left3.shape[1] // 2
    there = slice(total + here.start, total + here.stop)
    one_row = row_at(1.0, 0, jnp.zeros((16, rows), F32))
    none = jnp.zeros((16, rows), BF16)
    mask, target = s[0:1], s[7:8]
    left1[:, here] = jnp.concatenate([x, jnp.zeros((8, rows), F32)], axis=0).astype(BF16)
    for left in (left2, left3):
        left[HID : HID + 16, here] = one_row.astype(BF16)
        left[HID : HID + 16, there] = none
    z = dot(one[0], stack_inputs(x)) if saved is None else saved[0]
    yield
    h, t = act(z)
    d1, e1 = slope(h, t), curve(z, t)
    left2[0:HID, here] = h.astype(BF16)
    if saved is None:
        z = times_exact(w, 0, h)
        yield
        z = z + spread(bias[0, 0], rows)
    else:
        z = saved[1]
        yield
    h, t = act(z)
    d2, e2 = slope(h, t), curve(z, t)
    left3[0:HID, here] = h.astype(BF16)
    if saved is None:
        z = times_exact(w, 4, h)
        yield
        z = z + spread(bias[0, 1], rows)
    else:
        z = saved[2]
        yield
    h, t = act(z)
    d3, e3 = slope(h, t), curve(z, t)
    column = spread(column, rows)
    q = jnp.sum(column * h, axis=0, keepdims=True) + last
    miss = q - target
    half_a = alive * mask * miss
    td = jnp.sum(half_a * miss, axis=1, keepdims=True)
    head = (2.0 * half_a) * h
    b3 = column * d3
    e3 = column * e3
    cut = b3.astype(BF16)
    there3[:, here] = cut
    c2 = times(w, 6, cut) if saved is None else saved[3]
    yield
    b2 = c2 * d2
    e2 = c2 * e2
    cut = b2.astype(BF16)
    there2[:, here] = cut
    c1 = times(w, 2, cut) if saved is None else saved[4]
    yield
    b1 = c1 * d1
    e1 = c1 * e1
    cut = b1.astype(BF16)
    right1[:, there] = cut
    grad = action_gradient(inner, cut)
    yield
    size = jnp.sum(grad * grad, axis=0, keepdims=True) + GRAD_FLOOR
    cot = action_rows(s) * weight
    along = jnp.sum(grad * cot, axis=0, keepdims=True)
    v = lax.rsqrt(size) * (cot - grad * (along / size))
    left1[:, there] = jnp.concatenate(
        [jnp.zeros((16, rows), F32), 0.5 * v, jnp.zeros((8, rows), F32)], axis=0
    ).astype(BF16)
    t1 = dot(inner_stack, stack_inputs(v))
    yield
    cut = (d1 * t1).astype(BF16)
    left2[0:HID, there] = cut
    t2 = times(w, 0, cut)
    yield
    cut = (d2 * t2).astype(BF16)
    left3[0:HID, there] = cut
    t3 = times(w, 4, cut)
    yield
    head = head + d3 * t3
    head = sum(head[:, i : i + 128] for i in range(0, rows, 128))
    r = e3 * t3
    here3[:, here] = (half_a * b3 + r).astype(BF16)
    r = dot(mats[0, 6], r.astype(BF16)) * d2 + e2 * t2
    yield
    here2[:, here] = (half_a * b2 + r).astype(BF16)
    r = dot(mats[0, 2], r.astype(BF16)) * d1 + e1 * t1
    yield
    right1[:, here] = (half_a * b1 + r).astype(BF16)
    return td, jnp.sum(half_a, axis=1, keepdims=True), head


def second_kernel(live, place, xs, xs_far, sx, sx_far, gx, saved, one, mats, bias, body, head, *refs):
    (grads, sums), scratch = refs[:2], refs[2:]
    left3, here3, there3, left2, here2, there2, left1, right1 = scratch
    rows = xs.shape[1]
    mine = place[1]
    alive = jnp.where(mine == 0, live[0], live[1]).astype(F32)
    read = critic_rows(body, mine)
    column, last = head_column(head, mine)
    column = wide(column)
    inner, inner_stack = inner_rows(read), stack_weights(read(16, 24))
    weight = 2.0 * DIVERSITY_WEIGHT * alive / (gx[7:8, :] - 1.0)
    td = bias_sum = jnp.zeros((1, 1), F32)
    step = rows // 2
    by_head = jnp.zeros((HID, 128), F32)
    for td_part, bias_part, head_part in interleave(
        *[
            second_stream(
                one, mats, bias, column, last, inner, inner_stack, alive, weight[:, start : start + step],
                x[:, start : start + step], s[:, start : start + step],
                None if i else [saved[k, :, start : start + step] for k in range(5)],
                slice(i * rows + start, i * rows + start + step), *scratch,
            )
            for start in range(0, rows, step)
            for i, (x, s) in enumerate(((xs, sx), (xs_far, sx_far)))
        ]
    ):
        td, bias_sum, by_head = td + td_part, bias_sum + bias_part, by_head + head_part

    def layer(left, here, there):
        n = here.shape[1]
        return dot_rows(left[:, 0:n], here[...]) + 0.5 * dot_rows(left[:, n:], there[...])

    grads[0:TWO, :] = dot_rows(right1[...], left1[...]).T[0:TWO]
    grads[TWO:THREE, :] = layer(left2, here2, there2)[0 : HID + 1]
    grads[THREE:BODY, :] = layer(left3, here3, there3)[0 : HID + 1]
    grads[BODY : BODY + 1, :] = jnp.sum(by_head.T, axis=0, keepdims=True)
    lane = lax.broadcasted_iota(jnp.int32, (1, HID), 1)
    grads[BODY + 1 : BODY + 2, :] = jnp.where(lane == 0, 2.0 * bias_sum, 0.0)
    grads[BODY + 2 :, :] = jnp.zeros((grads.shape[0] - BODY - 2, HID), F32)
    sums[...] = jnp.where(lax.broadcasted_iota(jnp.int32, (1, 128), 1) == 0, td, 0.0)


def deal_kernel(place, critic, keep, got, *out):
    n = len(out)
    part = critic.shape[0] // n
    policy = keep[...] + got[...]
    for k in range(n):
        to = jnp.bitwise_xor(place[2], k)
        out[k][0:part, :] = critic[pl.ds(pl.multiple_of(to * part, 8), part), :]
        out[k][part:, :] = policy


def reduce_kernel(part, place, one, two, *refs):
    ins, (out, sums) = refs[:-2], refs[-2:]
    total = ins[0][...]
    for r in ins[1:]:
        total = total + r[...]
    out[...] = total
    critic, policy = total[:part], total[part:]
    square = jnp.sum(jnp.sum(critic * critic, axis=0, keepdims=True), axis=1, keepdims=True)
    once = (place[2] == 0).astype(F32)
    square = square + once * jnp.sum(jnp.sum(policy * policy, axis=0, keepdims=True), axis=1, keepdims=True)
    lane = lax.broadcasted_iota(jnp.int32, (1, 128), 1)
    row = one[...] + two[...] + jnp.where(lane == 5, square, 0.0)
    sums[...] = jnp.broadcast_to(row, sums.shape)


def piece_kernel(whole, out):
    out[...] = whole[0 : out.shape[0], :]


def adam(weights, moment, second, grads):
    moment_new = BETA_ONE * (moment + grads)
    second_new = BETA_TWO * (second + grads * grads)
    root = (1.0 / (1.0 - BETA_TWO**STEPS_DONE)) ** 0.5
    bottom = (root * second_new) * lax.rsqrt(second_new) + ADAM_EPSILON
    guess = pltpu.reciprocal(bottom, approx=True)
    inverse = guess * (2.0 - bottom * guess)
    step = ((LEARN_RATE / (1.0 - BETA_ONE**STEPS_DONE)) * moment_new) * inverse
    return (1.0 - LEARN_RATE * DECAY_RATE) * weights - step, moment_new, second_new


def scalars_kernel(log_temp, log_mom, log_sq, sums, loss, norm_out, lt, lm, ls, scale):
    total = jnp.sum(sums[...], axis=0, keepdims=True)
    entropy, count = total[:, 3:4], total[:, 4:5]
    grad_temp = -entropy / count
    norm = jnp.sqrt(total[:, 5:6] / (count * count) + grad_temp * grad_temp)
    factor = CLIP_NORM / jnp.maximum(norm, CLIP_NORM)
    lane = lax.broadcasted_iota(jnp.int32, (1, 128), 1)
    loss[...] = jnp.where(lane == 3, -log_temp[0] * entropy, total)[:, 0:5]
    norm_out[...] = norm
    one = lambda v: jnp.full((1, 1), v[0])
    put((lt, lm, ls), (slice(0, 1),), adam(one(log_temp), one(log_mom), one(log_sq), factor * grad_temp))
    scale[...] = jnp.broadcast_to(factor / count, (8, 128))


def put(refs, at, got):
    for r, value in zip(refs, got):
        r[at] = value.astype(r.dtype)


def update_kernel(n_z, part, small, sources, n_pieces, n_blocks, place, scale, *refs):
    refs = list(refs)
    take = lambda n: [refs.pop(0) for _ in range(n)]
    pieces, blocks = take(n_pieces), take(n_blocks)
    w, m, v, t, hw, hm, hv, ht, pw, pm, pv, phw, phm, phv = take(14)
    outs = take(18)
    total, policy = take(2)
    near, sem, body_sem = take(18), *take(2)
    scale = scale[0:1, 0:1]
    for k, i, first, start, stop in sources:
        piece = pieces[i]
        c = jnp.bitwise_xor(place[1], k // n_z)
        z = jnp.bitwise_xor(place[2], k % n_z)
        for side in range(2):
            at = pl.ds(4 * (part * z + start) + 2 * side + c, stop - start, stride=4)
            total[at, :] = piece[first : first + stop - start, side * 128 : (side + 1) * 128]
    copies = []

    def send(i, j):
        copies.extend(start_copies(near[i:j], outs[i:j], sem.at[pl.ds(i, j - i)]))

    rows = w.shape[0]
    step = BLOCK
    for i, start in enumerate(range(0, rows, step)):
        at = pl.ds(start, min(step, rows - start))
        new, mom, sq = adam(w[at, :], m[at, :], v[at, :], total[at, :] * scale)
        tgt = t[at, :] + POLYAK_RATE * (new - t[at, :])
        put(near[0:5], (at, slice(None)), (new, mom, sq, tgt, new))
        copies += start_copies([r.at[at, :] for r in near[0:4]], [r.at[at, :] for r in outs[0:4]], body_sem.at[i])
    send(4, 5)
    for c in range(2):
        at = slice(c, c + 1)
        rows8 = [total[4 * (BODY + k) + 2 * side + c : 4 * (BODY + k) + 2 * side + c + 1, :] for k, side in ((0, 0), (0, 1), (1, 0))]
        grad = jnp.concatenate([rows8[0], rows8[1], rows8[2][:, 0:1]], axis=1)
        new, mom, sq = adam(hw[at, :], hm[at, :], hv[at, :], grad * scale)
        tgt = ht[at, :] + POLYAK_RATE * (new - ht[at, :])
        put(near[5:10], (at, slice(None)), (new, mom, sq, tgt, new))
    send(5, 10)
    first = 0
    for block in blocks:
        for k in range(block.shape[0] // small):
            at = 2 * jnp.bitwise_xor(place[0], first + k // 2) + jnp.bitwise_xor(place[1], k % 2)
            policy[pl.ds(pl.multiple_of(at * small, 8), small), :] = block[k * small : (k + 1) * small, :]
        first += block.shape[0] // (2 * small)
    n = S_DIM
    for mine, at in (
        (slice(0, n + 1), slice(0, n + 1)),
        (slice(P_TWO, P_TWO + HID + 1), slice(n + 1, n + 2 + HID)),
        (slice(P_THREE, P_THREE + HID + 1), slice(n + 2 + HID, n + 3 + 2 * HID)),
    ):
        new, mom, sq = adam(pw[at], pm[at], pv[at], policy[mine, :] * scale)
        put(near[10:14], (at,), (new, mom, sq, new))
    send(10, 14)
    by_head = policy[P_HEAD : P_HEAD + 16, :]
    last = jnp.broadcast_to(policy[P_LAST + 1 : P_LAST + 2, 0:16], (8, 16)).T[:, 0:1]
    for r, at in ((1, slice(0, A_DIM)), (9, slice(A_DIM, 2 * A_DIM))):
        grad = jnp.concatenate([by_head[r : r + A_DIM], last[r : r + A_DIM]], axis=1)
        new, mom, sq = adam(phw[at, :], phm[at, :], phv[at, :], grad * scale)
        put(near[14:18], (at, slice(None)), (new, mom, sq, new))
    send(14, 18)
    for copy in copies:
        copy.wait()


def join_kernel(n, plan, *refs):
    for out, slices in zip(refs[n:], plan):
        at = 0
        for i, start, stop in slices:
            out[at : at + stop - start, :] = refs[i][start:stop, :]
            at += stop - start


def join(arrays, plan):
    outs = [shape(sum(stop - start for _, start, stop in slices), HID) for slices in plan]
    return call(functools.partial(join_kernel, len(arrays), plan), outs, [VMEM] * len(arrays), us=0.3)(*arrays)


def flat(v):
    return jnp.transpose(v.reshape(2, -1, 2, 128), (1, 2, 0, 3)).reshape(-1, 128)


def unflat(v):
    return jnp.transpose(v.reshape(-1, 2, 2, 128), (2, 0, 1, 3)).reshape(2, -1, HID)


def per_device(
    members,
    dp,
    states,
    actions,
    rewards,
    next_states,
    terminal,
    valid_rows,
    noise_seeds,
    member_live,
    critic_body,
    critic_body_mom,
    critic_body_sq,
    critic_body_tgt,
    critic_head,
    critic_head_mom,
    critic_head_sq,
    critic_head_tgt,
    policy_body,
    policy_body_mom,
    policy_body_sq,
    policy_head,
    policy_head_mom,
    policy_head_sq,
    log_temp,
    log_temp_mom,
    log_temp_sq,
):
    rows = states.shape[0]
    n_z = dp // 2
    part = -(-CRITIC_ROWS // (8 * n_z)) * 8
    small = -(-POLICY_ROWS // (16 * members)) * 8
    m, d = lax.axis_index("member"), lax.axis_index("dp")
    place = jnp.stack([m, d // n_z, d % n_z]).astype(jnp.int32)

    def across(value, axis, n, to):
        return lax.ppermute(value, axis, [(i, to(i)) for i in range(n)])

    def to_member(value, bit):
        return across(value, "member", members, lambda i: i ^ bit)

    def to_pair(value):
        return across(value, "dp", dp, lambda i: i ^ n_z)

    def along(value, offset):
        return across(value, "dp", dp, lambda i: i ^ offset)

    square = lambda v: v.reshape(rows // 128, 128)
    turned = [policy_head.T, policy_head_mom.T, policy_head_sq.T]
    body, mom, sq, body_tgt = flat(critic_body), flat(critic_body_mom), flat(critic_body_sq), flat(critic_body_tgt)
    like = lambda *arrays: [shape(*a.shape, dtype=a.dtype) for a in arrays]
    first = call(first_kernel, shape(8, 128), [SMEM], us=8.0, limit=1)(place)
    xs, xn, xp, aux, *actor_weights = call(
        actor_kernel,
        [shape(24, rows), shape(24, rows), shape(24, rows), shape(32, rows)] + trunk_arrays(1, S_DIM),
        [VMEM] * 10 + [SMEM],
        us=3.0,
    )(
        first, states.T, actions.T, next_states.T, noise_seeds.T, square(rewards), square(terminal), square(valid_rows),
        policy_body, turned[0], log_temp,
    )
    xs_far = to_pair(xs)
    ensemble, saved, *weights = call(
        critic_kernel,
        [shape(16, rows), shape(5, HID, rows)] + trunk_arrays(1, X_DIM),
        [SMEM, SMEM] + [VMEM] * 7,
        trunk_scratch(3, X_DIM) + [pltpu.VMEM((4, HID, 128), F32)],
        us=8.0,
    )(
        member_live, place, xs, xn, xp, body, critic_head, body_tgt, critic_head_tgt
    )
    bit = 1
    while bit * 2 < members:
        other = to_member(ensemble, bit)
        k = lax.broadcasted_iota(jnp.int32, ensemble.shape, 0)
        ensemble = jnp.where(k == 7, jnp.minimum(ensemble, other), ensemble + other)
        bit *= 2
    sx, gx, sums_joint = call(
        joint_kernel, [shape(8, rows), shape(8, rows), shape(1, 128)], [VMEM, VMEM, VMEM, SMEM], us=0.7
    )(ensemble, to_member(ensemble, bit), aux, log_temp)
    sx_far = to_pair(sx)
    keep, give = call(
        policy_kernel,
        [shape(small, HID), shape(small, HID)],
        [SMEM] + [VMEM] * 7 + [SMEM],
        [pltpu.VMEM((2 * members * small, HID), F32)],
        us=3.0,
    )(place, xs, aux, gx, *actor_weights, turned[0], log_temp)
    got = to_pair(give)
    both = 2 * rows
    left, side = pltpu.VMEM((HID + 16, 2 * both), BF16), pltpu.VMEM((HID, both), BF16)
    scratch = [left, side, side, left, side, side]
    scratch = scratch + [pltpu.VMEM((32, 2 * both), BF16), pltpu.VMEM((HID, 2 * both), BF16)]
    grads, sums_second = call(
        second_kernel,
        [shape(part * n_z, HID), shape(1, 128)],
        [SMEM, SMEM] + [VMEM] * 11,
        scratch,
        us=8.0,
        limit=42,
    )(member_live, place, xs, xs_far, sx, sx_far, gx, saved, *weights, body, critic_head)
    message = shape(part + small, HID)
    dealt = call(deal_kernel, [message] * n_z, [SMEM, VMEM, VMEM, VMEM], us=0.5)(place, grads, keep, got)
    arrived = [dealt[0]] + [along(dealt[k], k) for k in range(1, n_z)]
    whole, sums = call(
        functools.partial(reduce_kernel, part),
        [message, shape(members * dp, 128)],
        [SMEM] + [VMEM] * (2 + n_z),
    )(place, sums_joint, sums_second, *arrived)
    sums = lax.all_to_all(sums, ("member", "dp"), 0, 0, tiled=True)
    piece = call(piece_kernel, shape(part, HID), [VMEM], us=8.0)(whole)
    pieces, bit = {0: piece, n_z: to_pair(whole)}, 1
    while bit < n_z:
        pieces[bit] = along(piece, bit)
        bit *= 2
    at_hand = sorted(pieces)
    *values, sums = lax.optimization_barrier((*[pieces[k] for k in at_hand], sums))
    pieces = dict(zip(at_hand, values))
    found = {k: [(pieces[k], 0, 0, part)] for k in at_hand}
    actor = [[(0, part, part + small), (1, part, part + small)]]
    (block,) = join([whole, pieces[n_z]], actor)
    if dp > 2:
        found[dp - 1] = [(along(pieces[0], dp - 1), 0, 0, part)]
    bits = dp.bit_length() - 1
    for level in range(2, bits):
        paths = {}
        for k in range(dp):
            if bin(k).count("1") == level:
                low, rest = k & -k, k & (k - 1)
                cut = part // 16 * 8 if k < n_z and level == 2 else 0
                paths.setdefault(low, []).append((k, cut, part))
                if cut:
                    paths.setdefault(rest, []).append((k, 0, cut))
        inputs = sorted({k & ~bit for bit, slices in paths.items() for k, _, _ in slices})
        plan = []
        for bit, slices in paths.items():
            plan.append([])
            for k, start, stop in slices:
                first = found[k & ~bit][0][1]
                plan[-1].append((inputs.index(k & ~bit), first + start, first + stop))
        sent = join([found[k][0][0] for k in inputs], plan)
        level_found = {}
        for (bit, slices), message in zip(paths.items(), sent):
            came, at = along(message, bit), 0
            for k, start, stop in slices:
                level_found.setdefault(k, []).append((came, at, start, stop))
                at += stop - start
        if level + 1 < bits:
            whole_ones = sorted(level_found)
            rows_of = [join([v[0] for v in sorted(level_found[k], key=lambda v: v[2])], [[(i, v[1], v[1] + v[3] - v[2]) for i, v in enumerate(sorted(level_found[k], key=lambda v: v[2]))]])[0] for k in whole_ones]
            level_found = {k: [(v, 0, 0, part)] for k, v in zip(whole_ones, rows_of)}
        found.update(level_found)
    blocks = [block] + [to_member(block, k) for k in range(1, members)]
    arrays, sources = [], []
    for k, places in sorted(found.items()):
        for array, at, start, stop in places:
            if not any(array is other for other in arrays):
                arrays.append(array)
            sources.append((k, [array is other for other in arrays].index(True), at, start, stop))
    halved = lambda a: shape(*a.shape, dtype=BF16)
    heads = [critic_head, critic_head_mom, critic_head_sq, critic_head_tgt]
    single = shape(1, 1)
    loss, norm, lt_new, lt_mom, lt_sq, scale = call(
        scalars_kernel, [shape(1, 5), single, single, single, single, shape(8, 128)], [SMEM] * 3 + [VMEM], us=0.5
    )(log_temp, log_temp_mom, log_temp_sq, sums)
    outs = like(body, body, body, body) + [halved(body)] + like(*heads) + [halved(critic_head)]
    outs = outs + like(policy_body, policy_body, policy_body) + [halved(policy_body)] + like(*turned) + [halved(turned[0])]
    new = call(
        functools.partial(update_kernel, n_z, part, small, sources, len(arrays), len(blocks)),
        outs,
        [SMEM] + [VMEM] * (1 + len(arrays) + len(blocks) + 14),
        [pltpu.VMEM((4 * n_z * part, 128), F32), pltpu.VMEM((2 * members * small, HID), F32)]
        + buffers(*outs)
        + [pltpu.SemaphoreType.DMA((-(-body.shape[0] // BLOCK), 4))],
        us=5.0,
        out_specs=[HBM] * len(outs),
    )(
        place, scale, *arrays, *blocks, body, mom, sq, body_tgt, *heads, policy_body, policy_body_mom, policy_body_sq, *turned,
    )
    new = list(new)
    new = [unflat(v) for v in new[:5]] + new[5:14] + [v.T for v in new[14:]]
    return (loss[0], norm[0], *new, lt_new[0], lt_mom[0], lt_sq[0])


def solution(mesh):
    row, line = P("dp", None), P("dp")
    stack, flat = P("member", None, None), P("member", None)
    return jax.shard_map(
        functools.partial(per_device, mesh.shape["member"], mesh.shape["dp"]),
        mesh=mesh,
        in_specs=(row, row, line, row, line, line, row, P("member")) + (stack,) * 4 + (flat,) * 4 + (P(),) * 9,
        out_specs=(P(), P()) + (stack,) * 5 + (flat,) * 5 + (P(),) * 11,
        check_vma=False,
    )
```

```python
import functools

import jax
import jax.numpy as jnp
from jax import lax
from jax.experimental import pallas as pl
from jax.experimental.pallas import tpu as pltpu
from jax.sharding import PartitionSpec as P

STEPS_DONE = 5
DISCOUNT = 0.99
POLYAK_RATE = 0.005
ENTROPY_TARGET = -6.0
DIVERSITY_WEIGHT = 1.0
LEARN_RATE = 0.05
BETA_ONE = 0.5
BETA_TWO = 0.5
DECAY_RATE = 0.01
ADAM_EPSILON = 1e-08
GRAD_FLOOR = 0.0001
CLIP_NORM = 1.0
LOGSTD_LOW = -5.0
LOGSTD_HIGH = 2.0
LOG_TWO = 0.6931471805599453
HALF_LOG_TWOPI = 0.9189385332046727
FAR_VALUE = 1e30

F32 = jnp.float32
BF16 = jnp.bfloat16
HID = 256
S_DIM = 17
A_DIM = 6
X_DIM = S_DIM + A_DIM
TWO = X_DIM + 1
THREE = TWO + HID + 1
BODY = THREE + HID + 1
CRITIC_ROWS = 544
P_TWO = 24
P_THREE = 288
P_LAST = 544
P_HEAD = 552
POLICY_ROWS = 576
BLOCK = 272
VMEM = pl.BlockSpec(memory_space=pltpu.VMEM)
SMEM = pl.BlockSpec(memory_space=pltpu.SMEM)
HBM = pl.BlockSpec(memory_space=pltpu.HBM)


def call(kernel, outs, in_specs, scratch=(), us=1.0, out_specs=None, limit=32):
    return pl.pallas_call(
        kernel,
        out_shape=outs,
        in_specs=in_specs,
        out_specs=out_specs or jax.tree.map(lambda _: VMEM, outs),
        scratch_shapes=list(scratch),
        compiler_params=pltpu.CompilerParams(vmem_limit_bytes=limit * 2**20),
        cost_estimate=pl.CostEstimate(flops=int(us * 1.15e9), bytes_accessed=0, transcendentals=0),
    )


def buffers(*arrays):
    return [pltpu.VMEM(a.shape, a.dtype) for a in arrays] + [pltpu.SemaphoreType.DMA((len(arrays),))]


def start_copies(sources, targets, sem):
    copies = [pltpu.make_async_copy(a, b, sem.at[i]) for i, (a, b) in enumerate(zip(sources, targets))]
    for copy in copies:
        copy.start()
    return copies


def shape(*dims, dtype=F32):
    return jax.ShapeDtypeStruct(dims, dtype)


def dot(a, b):
    return lax.dot_general(a, b, (((1,), (0,)), ((), ())), preferred_element_type=F32)


def dot_rows(a, b):
    return lax.dot_general(a, b, (((1,), (1,)), ((), ())), preferred_element_type=F32)


def halves(w):
    high = w.astype(BF16)
    return high, (w - high.astype(F32)).astype(BF16)


def stack_weights(w):
    high = (0.5 * w).astype(BF16).astype(F32)
    return jnp.concatenate([high, high, 0.5 * w - high], axis=0).T.astype(BF16)


def stack_inputs(v):
    high = v.astype(BF16).astype(F32)
    return jnp.concatenate([high, v - high, high], axis=0).astype(BF16)


def act(z):
    t = jnp.tanh(z)
    return z + z * t, t


def slope(h, t):
    return (1.0 + h) + t * (1.0 - h)


def curve(z, t):
    return (1.0 - t * t) * (1.0 - z * t)


def wide(column):
    return jnp.broadcast_to(column, (column.shape[0], 128))


def spread(column, rows):
    return jnp.concatenate([column] * (rows // 128), axis=1)


def action_rows(v):
    k = lax.broadcasted_iota(jnp.int32, v.shape, 0)
    return jnp.where((k >= 1) & (k <= A_DIM), v, 0.0)


def row_at(v, k, like):
    return jnp.where(lax.broadcasted_iota(jnp.int32, like.shape, 0) == k, v, like)


def lane_row(block):
    return jnp.concatenate([block[i : i + 1] for i in range(block.shape[0])], axis=1)


def interleave(*streams):
    results, active = [None] * len(streams), list(enumerate(streams))
    while active:
        left = []
        for i, stream in active:
            try:
                next(stream)
                left.append((i, stream))
            except StopIteration as end:
                results[i] = end.value
        active = left
    return results


def critic_rows(ref, c):
    def read(a, b):
        return jnp.concatenate([ref[pl.ds(4 * a + 2 * t + c, b - a, stride=4), :] for t in range(2)], axis=1)

    return read


def load_trunk(body, n_in, one, mats, bias, i, backward=False):
    one[i] = stack_weights(body(0, n_in + 1))
    yield
    for k, start in enumerate((n_in + 1, n_in + 2 + HID)):
        high, low = halves(0.5 * body(start, start + HID))
        mats[i, 4 * k] = high.T
        mats[i, 4 * k + 1] = low.T
        if backward:
            mats[i, 4 * k + 2] = high
            mats[i, 4 * k + 3] = low
        bias[i, k] = wide(0.5 * body(start + HID, start + HID + 1).T)
        yield


def trunk_arrays(n, n_in):
    return [shape(n, HID, 3 * (n_in + 1), dtype=BF16), shape(n, 8, HID, HID, dtype=BF16), shape(n, 2, HID, 128)]


def trunk_scratch(n, n_in):
    return [pltpu.VMEM(a.shape, a.dtype) for a in trunk_arrays(n, n_in)]


def times(w, k, h):
    mats, i = w
    return dot(mats[i, k], h) + dot(mats[i, k + 1], h)


def times_exact(w, k, h):
    mats, i = w
    high, low = halves(h)
    return dot(mats[i, k], high) + dot(mats[i, k + 1], high) + dot(mats[i, k], low)


def policy_head_rows(turned):
    one = jnp.zeros((1, HID + 1), F32)
    return jnp.concatenate([one, turned[:A_DIM], one, one, turned[A_DIM:], one], axis=0)


def noise_of(seed_row):
    k = lax.broadcasted_iota(jnp.int32, (8, seed_row.shape[1]), 0).astype(F32) - 1.0
    return 1.7 * jnp.sin(0.618034 * seed_row + 2.39996 * k)


def actor_stream(one, mats, bias, head, head_bias, x, noise):
    rows = x.shape[1]
    z = dot(one[0], stack_inputs(x))
    yield
    z = times((mats, 0), 0, act(z)[0].astype(BF16))
    yield
    z = times((mats, 0), 4, act(z + spread(bias[0, 0], rows))[0].astype(BF16))
    yield
    high, low = halves(act(z + spread(bias[0, 1], rows))[0])
    out = dot(head, high)
    out = out[:16] + out[16:] + dot(head[:16], low) + spread(head_bias, rows)
    yield
    mean, raw = out[:8], out[8:]
    turned = jnp.tanh(raw)
    log_std = LOGSTD_LOW + 0.5 * (LOGSTD_HIGH - LOGSTD_LOW) * (turned + 1.0)
    deviation = jnp.exp(log_std) * noise
    u = mean + deviation
    soft = jnp.maximum(-2.0 * u, 0.0) + jnp.log(1.0 + jnp.exp(-jnp.abs(2.0 * u)))
    squash = 2.0 * (LOG_TWO - u - soft)
    terms = -0.5 * noise * noise - log_std - HALF_LOG_TWOPI - squash
    log_prob = jnp.sum(action_rows(terms), axis=0, keepdims=True)
    return jnp.tanh(u), turned, deviation, log_prob


def first_kernel(place, out):
    out[...] = jnp.full(out.shape, (place[0] == 0).astype(F32))


def actor_kernel(
    first, states, actions, next_states, seeds, rewards, terminal, valid, body, head, log_temp, xs, xn, xp, aux, one, mats, bias
):
    rows = states.shape[1]
    ones = jnp.ones((1, rows), F32)
    for x, source in ((xs, states), (xn, next_states), (xp, states)):
        x[0:S_DIM, :] = source[...]
        x[X_DIM : X_DIM + 1, :] = ones
    xs[S_DIM:X_DIM, :] = actions[...]
    seed = seeds[...].astype(F32)
    loading = load_trunk(lambda a, b: body[a:b], S_DIM, one, mats, bias, 0, backward=True)
    next(loading)
    head_rows = policy_head_rows(head[...])
    head_w, head_b = jnp.concatenate(halves(head_rows[:, :HID]), axis=0), wide(head_rows[:, HID:])
    carry = 1.0 - lane_row(terminal[...].astype(F32))
    temper = jnp.exp(log_temp[0])
    now_in = jnp.concatenate([states[...], ones], axis=0)
    later_in = jnp.concatenate([next_states[...], ones], axis=0)
    half = rows // 2
    done = interleave(
        *[
            actor_stream(one, mats, bias, head_w, head_b, x[:, i : i + half], noise_of(seed[k : k + 1, i : i + half]))
            for i in (0, half)
            for x, k in ((later_in, 1), (now_in, 0))
        ],
        loading,
    )[:-1]
    later = [jnp.concatenate(v, axis=1) for v in zip(*done[0::2])]
    now = [jnp.concatenate(v, axis=1) for v in zip(*done[1::2])]
    xn[S_DIM:X_DIM, :] = later[0][1 : 1 + A_DIM]
    aux[0:1, :] = lane_row(rewards[...]) - DISCOUNT * carry * temper * later[3]
    aux[1:2, :] = DISCOUNT * carry
    aux[2:3, :] = lane_row(valid[...].astype(F32))
    action, turned, deviation, log_prob = now
    xp[S_DIM:X_DIM, :] = action[1 : 1 + A_DIM]
    aux[3:4, :] = log_prob
    aux[4:5, :] = spread(first[0:1], rows)
    aux[5:8, :] = jnp.zeros((3, rows), F32)
    aux[8:16, :] = action_rows(action)
    aux[16:24, :] = action_rows(turned)
    aux[24:32, :] = action_rows(deviation)


def head_column(head, c):
    row = head[pl.ds(c, 1), :]
    return row[:, :HID].T, row[:, HID:]


def inner_rows(read):
    return jnp.concatenate(halves(0.5 * read(16, 24)), axis=0)


def action_gradient(inner, y):
    grad = dot(inner, y)
    return action_rows(grad[:8] + grad[8:])


def data_stream(one, mats, bias, i, column, inner, x, save):
    rows, w = x.shape[1], (mats, i)
    z = dot(one[i], x)
    save(0, z)
    yield
    h, t = act(z)
    d1 = slope(h, t)
    z = times_exact(w, 0, h)
    yield
    z = z + spread(bias[i, 0], rows)
    save(1, z)
    h, t = act(z)
    d2 = slope(h, t)
    z = times_exact(w, 4, h)
    yield
    z = z + spread(bias[i, 1], rows)
    save(2, z)
    h, t = act(z)
    c = times(w, 6, (spread(column, rows) * slope(h, t)).astype(BF16))
    yield
    save(3, c)
    c = times(w, 2, (c * d2).astype(BF16))
    yield
    save(4, c)
    grad = action_gradient(inner, (c * d1).astype(BF16))
    yield
    size = jnp.sum(grad * grad, axis=0, keepdims=True) + GRAD_FLOOR
    return grad * lax.rsqrt(size)


def target_stream(one, mats, bias, i, column, last, x):
    rows, w = x.shape[1], (mats, i)
    z = dot(one[i], x)
    yield
    z = times(w, 0, act(z)[0].astype(BF16))
    yield
    z = times(w, 4, act(z + spread(bias[i, 0], rows))[0].astype(BF16))
    yield
    h = act(z + spread(bias[i, 1], rows))[0]
    return jnp.sum(spread(column, rows) * h, axis=0, keepdims=True) + last


def chosen_stream(one, mats, bias, i, column, last, inner, x):
    rows = x.shape[1]
    z = dot(one[i], x)
    yield
    h, t = act(z)
    d1 = slope(h, t)
    z = dot(mats[i, 0], h.astype(BF16))
    yield
    h, t = act(z + spread(bias[i, 0], rows))
    d2 = slope(h, t)
    z = dot(mats[i, 4], h.astype(BF16))
    yield
    h, t = act(z + spread(bias[i, 1], rows))
    column = spread(column, rows)
    q = jnp.sum(column * h, axis=0, keepdims=True) + last
    c = dot(mats[i, 6], (column * slope(h, t)).astype(BF16))
    yield
    c = dot(mats[i, 2], (c * d2).astype(BF16))
    yield
    return q, action_gradient(inner, (c * d1).astype(BF16))


def critic_kernel(live, place, xs, xn, xp, body, head, body_tgt, head_tgt, out, saved, *refs):
    mine, scratch, columns = refs[:3], refs[3:6], refs[6]
    order = [place[1], 1 - place[1]]
    lasts, inners, trunks, loading = [], [], [], []
    for i in range(4):
        c = order[i % 2]
        read = critic_rows((body, body_tgt)[i // 2], c)
        trunks.append((*mine, 0) if i == 0 else (*scratch, i - 1))
        loading.append(load_trunk(read, X_DIM, *trunks[i], backward=i < 2))
        next(loading[-1])
        column, last = head_column((head, head_tgt)[i // 2], c)
        columns[i] = wide(column)
        lasts.append(last)
        if i < 2:
            inners.append(inner_rows(read))
    alive = [live[c].astype(F32) for c in order]
    rows = xs.shape[1]
    step = 256
    for start in range(0, rows, step):
        at = slice(start, start + step)
        data, later, chosen = stack_inputs(xs[:, at]), stack_inputs(xn[:, at]), stack_inputs(xp[:, at])

        def save(k, value, at=at):
            saved[k, :, at] = value

        done = interleave(
            data_stream(*trunks[0], columns[0], inners[0], data, save),
            data_stream(*trunks[1], columns[1], inners[1], data, lambda k, value: None),
            *[chosen_stream(*trunks[c], columns[c], lasts[c], inners[c], chosen) for c in range(2)],
            *[target_stream(*trunks[2 + c], columns[2 + c], lasts[2 + c], later) for c in range(2)],
            *loading,
        )
        loading = []
        unit, now, value = done[0:2], done[2:4], done[4:6]
        lowest = [jnp.where(alive[c] > 0, value[c], FAR_VALUE) for c in range(2)]
        total_n, total_q, total_g = [alive[0] * a + alive[1] * b for a, b in (unit, *zip(*now))]
        out[0:8, at] = row_at(jnp.minimum(lowest[0], lowest[1]), 7, row_at(alive[0] + alive[1], 0, total_n))
        out[8:16, at] = row_at(total_q, 0, total_g)


def merge(a, b):
    k = lax.broadcasted_iota(jnp.int32, a.shape, 0)
    return jnp.where(k == 7, jnp.minimum(a, b), a + b)


def joint_kernel(mine, other, aux, log_temp, sx, gx, sums):
    both = merge(mine[...], other[...])
    unit, grad = both[:8], both[8:]
    mask, log_prob = aux[2:3, :], aux[3:4, :]
    members = both[0:1]
    target = aux[0:1, :] + aux[1:2, :] * both[7:8]
    unit = action_rows(unit)
    sx[...] = row_at(target, 7, row_at(mask, 0, mask * unit))
    gx[...] = row_at(members, 7, grad)
    temper = jnp.exp(log_temp[0])
    spread = jnp.sum(mask * (jnp.sum(unit * unit, axis=0, keepdims=True) - members), axis=1, keepdims=True)
    actor = jnp.sum(mask * (temper * log_prob - both[8:9] / members), axis=1, keepdims=True)
    entropy = jnp.sum(mask * (log_prob + ENTROPY_TARGET), axis=1, keepdims=True)
    count = jnp.sum(mask, axis=1, keepdims=True)
    lane = lax.broadcasted_iota(jnp.int32, (1, 128), 1)
    row = jnp.where(lane == 1, spread, 0.0) + jnp.where(lane == 2, actor, 0.0)
    row = row + jnp.where(lane == 3, entropy, 0.0) + jnp.where(lane == 4, count, 0.0)
    sums[...] = row * aux[4:5, 0:128]


def policy_stream(one, mats, bias, head_back, x, rows8, by_log):
    rows, w = x.shape[1], (mats, 0)
    z = dot(one[0], stack_inputs(x))
    yield
    h, t = act(z)
    d1, h1 = slope(h, t), h.astype(BF16)
    z = times(w, 0, h1)
    yield
    h, t = act(z + spread(bias[0, 0], rows))
    d2, h2 = slope(h, t), h.astype(BF16)
    z = times(w, 4, h2)
    yield
    h, t = act(z + spread(bias[0, 1], rows))
    action, turned, deviation, by_action = rows8
    by_u = by_action * (1.0 - action * action) + by_log * 2.0 * action
    by_std = by_u * deviation - by_log
    by_raw = action_rows(by_std * (0.5 * (LOGSTD_HIGH - LOGSTD_LOW)) * (1.0 - turned * turned))
    by_out = jnp.concatenate([action_rows(by_u), by_raw], axis=0)
    high, low = halves(by_out)
    f3 = (dot(head_back, jnp.concatenate([high, low, high], axis=0)) * slope(h, t)).astype(BF16)
    yield
    f2 = (times(w, 6, f3) * d2).astype(BF16)
    yield
    f1 = (times(w, 2, f2) * d1).astype(BF16)
    yield
    return h1, h2, h.astype(BF16), f1, f2, f3, high, low, by_out


def policy_kernel(place, xs, aux, gx, one, mats, bias, head, log_temp, keep, give, full):
    rows = xs.shape[1]
    n = S_DIM
    head_high, head_low = halves(0.5 * policy_head_rows(head[...])[:, :HID])
    head_back = jnp.concatenate([head_high, head_high, head_low], axis=0).astype(F32).T.astype(BF16)
    x = row_at(1.0, n, xs[...])
    mask, members = aux[2:3, :], gx[7:8, :]
    by_action = -(mask / members) * action_rows(gx[...])
    by_log = jnp.exp(log_temp[0]) * mask
    rows8 = (aux[8:16, :], aux[16:24, :], aux[24:32, :], by_action)
    step = rows // 4
    cut = lambda v, i: v[:, i * step : (i + 1) * step]
    streams = [
        policy_stream(one, mats, bias, head_back, cut(x[: n + 1], i), [cut(v, i) for v in rows8], cut(by_log, i))
        for i in range(4)
    ]
    h1, h2, h3, f1, f2, f3, high, low, by_out = [jnp.concatenate(v, axis=1) for v in zip(*interleave(*streams))]
    ones = row_at(1.0, 0, jnp.zeros((16, rows), F32)).astype(BF16)
    start = jnp.where(lax.broadcasted_iota(jnp.int32, x.shape, 0) <= n, x, 0.0).astype(BF16)
    full[0:P_TWO, :] = dot_rows(start, f1)
    full[P_TWO:P_THREE, :] = dot_rows(jnp.concatenate([h1, ones], axis=0), f2)[: HID + 8]
    layer = dot_rows(jnp.concatenate([h2, ones], axis=0), f3)
    full[P_THREE : P_THREE + HID, :] = layer[:HID]
    last = wide(jnp.sum(by_out, axis=1, keepdims=True)).T[0:1]
    last = jnp.concatenate([last, jnp.zeros((1, HID - 16), F32)], axis=1)
    full[P_LAST:P_HEAD, :] = row_at(last, 1, layer[HID : HID + 8])
    by_head = dot_rows(jnp.concatenate([high, low], axis=0), h3)
    full[P_HEAD : P_HEAD + 16, :] = by_head[:16] + by_head[16:]
    full[P_HEAD + 16 :, :] = jnp.zeros((full.shape[0] - P_HEAD - 16, HID), F32)
    size = keep.shape[0]
    for out, x in ((keep, place[1]), (give, 1 - place[1])):
        out[...] = full[pl.ds(pl.multiple_of((2 * place[0] + x) * size, 8), size), :]


def padded(parts, rows):
    return jnp.concatenate([v if n == 0 else jnp.zeros((n, rows), F32) for n, v in parts], axis=0).astype(BF16)


def second_stream(
    one, mats, bias, column, last, inner, inner_stack, alive, weight, x, s, saved, here, left3, here3, there3, left2, here2,
    there2,
):
    rows, w = x.shape[1], (mats, 0)
    total = left3.shape[1] // 2
    there = slice(total + here.start, total + here.stop)
    one_row = row_at(1.0, 0, jnp.zeros((16, rows), F32))
    none = jnp.zeros((16, rows), BF16)
    mask, target = s[0:1], s[7:8]
    for left in (left2, left3):
        left[HID : HID + 16, here] = one_row.astype(BF16)
        left[HID : HID + 16, there] = none
    z = dot(one[0], stack_inputs(x)) if saved is None else saved[0]
    yield
    h, t = act(z)
    d1, e1 = slope(h, t), curve(z, t)
    left2[0:HID, here] = h.astype(BF16)
    if saved is None:
        z = times_exact(w, 0, h)
        yield
        z = z + spread(bias[0, 0], rows)
    else:
        z = saved[1]
        yield
    h, t = act(z)
    d2, e2 = slope(h, t), curve(z, t)
    left3[0:HID, here] = h.astype(BF16)
    if saved is None:
        z = times_exact(w, 4, h)
        yield
        z = z + spread(bias[0, 1], rows)
    else:
        z = saved[2]
        yield
    h, t = act(z)
    d3, e3 = slope(h, t), curve(z, t)
    column = spread(column, rows)
    q = jnp.sum(column * h, axis=0, keepdims=True) + last
    miss = q - target
    half_a = alive * mask * miss
    td = jnp.sum(half_a * miss, axis=1, keepdims=True)
    head = (2.0 * half_a) * h
    b3 = column * d3
    e3 = column * e3
    cut = b3.astype(BF16)
    there3[:, here] = cut
    c2 = times(w, 6, cut) if saved is None else saved[3]
    yield
    b2 = c2 * d2
    e2 = c2 * e2
    cut = b2.astype(BF16)
    there2[:, here] = cut
    c1 = times(w, 2, cut) if saved is None else saved[4]
    yield
    b1 = c1 * d1
    e1 = c1 * e1
    cut = b1.astype(BF16)
    there1 = cut
    grad = action_gradient(inner, cut)
    yield
    size = jnp.sum(grad * grad, axis=0, keepdims=True) + GRAD_FLOOR
    cot = action_rows(s) * weight
    along = jnp.sum(grad * cot, axis=0, keepdims=True)
    v = lax.rsqrt(size) * (cot - grad * (along / size))
    first = dot_rows(there1, padded([(16, 0), (0, 0.5 * v), (8, 0)], rows))
    t1 = dot(inner_stack, stack_inputs(v))
    yield
    cut = (d1 * t1).astype(BF16)
    left2[0:HID, there] = cut
    t2 = times(w, 0, cut)
    yield
    cut = (d2 * t2).astype(BF16)
    left3[0:HID, there] = cut
    t3 = times(w, 4, cut)
    yield
    head = head + d3 * t3
    head = sum(head[:, i : i + 128] for i in range(0, rows, 128))
    r = e3 * t3
    here3[:, here] = (half_a * b3 + r).astype(BF16)
    r = dot(mats[0, 6], r.astype(BF16)) * d2 + e2 * t2
    yield
    here2[:, here] = (half_a * b2 + r).astype(BF16)
    r = dot(mats[0, 2], r.astype(BF16)) * d1 + e1 * t1
    yield
    first = first + dot_rows((half_a * b1 + r).astype(BF16), padded([(0, x), (8, 0)], rows))
    return td, jnp.sum(half_a, axis=1, keepdims=True), head, first


def second_kernel(live, place, xs, xs_far, sx, sx_far, gx, saved, one, mats, bias, body, head, *refs):
    (grads, sums), scratch = refs[:2], refs[2:]
    left3, here3, there3, left2, here2, there2 = scratch
    rows = xs.shape[1]
    mine = place[1]
    alive = jnp.where(mine == 0, live[0], live[1]).astype(F32)
    read = critic_rows(body, mine)
    column, last = head_column(head, mine)
    column = wide(column)
    inner, inner_stack = inner_rows(read), stack_weights(read(16, 24))
    weight = 2.0 * DIVERSITY_WEIGHT * alive / (gx[7:8, :] - 1.0)
    td = bias_sum = jnp.zeros((1, 1), F32)
    step = rows // 2
    by_head, first = jnp.zeros((HID, 128), F32), jnp.zeros((HID, 32), F32)
    for td_part, bias_part, head_part, first_part in interleave(
        *[
            second_stream(
                one, mats, bias, column, last, inner, inner_stack, alive, weight[:, start : start + step],
                x[:, start : start + step], s[:, start : start + step],
                None if i else [saved[k, :, start : start + step] for k in range(5)],
                slice(i * rows + start, i * rows + start + step), *scratch,
            )
            for start in range(0, rows, step)
            for i, (x, s) in enumerate(((xs, sx), (xs_far, sx_far)))
        ]
    ):
        td, bias_sum, by_head, first = td + td_part, bias_sum + bias_part, by_head + head_part, first + first_part

    def layer(left, here, there):
        n = here.shape[1]
        return dot_rows(left[:, 0:n], here[...]) + 0.5 * dot_rows(left[:, n:], there[...])

    grads[0:TWO, :] = first.T[0:TWO]
    grads[TWO:THREE, :] = layer(left2, here2, there2)[0 : HID + 1]
    grads[THREE:BODY, :] = layer(left3, here3, there3)[0 : HID + 1]
    grads[BODY : BODY + 1, :] = jnp.sum(by_head.T, axis=0, keepdims=True)
    lane = lax.broadcasted_iota(jnp.int32, (1, HID), 1)
    grads[BODY + 1 : BODY + 2, :] = jnp.where(lane == 0, 2.0 * bias_sum, 0.0)
    grads[BODY + 2 :, :] = jnp.zeros((grads.shape[0] - BODY - 2, HID), F32)
    sums[...] = jnp.where(lax.broadcasted_iota(jnp.int32, (1, 128), 1) == 0, td, 0.0)


def deal_kernel(place, critic, keep, got, *out):
    n = len(out)
    part = critic.shape[0] // n
    policy = keep[...] + got[...]
    for k in range(n):
        to = jnp.bitwise_xor(place[2], k)
        out[k][0:part, :] = critic[pl.ds(pl.multiple_of(to * part, 8), part), :]
        out[k][part:, :] = policy


def reduce_kernel(part, place, one, two, *refs):
    ins, (out, sums) = refs[:-2], refs[-2:]
    total = ins[0][...]
    for r in ins[1:]:
        total = total + r[...]
    out[...] = total
    critic, policy = total[:part], total[part:]
    square = jnp.sum(jnp.sum(critic * critic, axis=0, keepdims=True), axis=1, keepdims=True)
    once = (place[2] == 0).astype(F32)
    square = square + once * jnp.sum(jnp.sum(policy * policy, axis=0, keepdims=True), axis=1, keepdims=True)
    lane = lax.broadcasted_iota(jnp.int32, (1, 128), 1)
    row = one[...] + two[...] + jnp.where(lane == 5, square, 0.0)
    sums[...] = jnp.broadcast_to(row, sums.shape)


def piece_kernel(whole, out):
    out[...] = whole[0 : out.shape[0], :]


def adam(weights, moment, second, grads):
    moment_new = BETA_ONE * (moment + grads)
    second_new = BETA_TWO * (second + grads * grads)
    root = (1.0 / (1.0 - BETA_TWO**STEPS_DONE)) ** 0.5
    bottom = (root * second_new) * lax.rsqrt(second_new) + ADAM_EPSILON
    guess = pltpu.reciprocal(bottom, approx=True)
    inverse = guess * (2.0 - bottom * guess)
    step = ((LEARN_RATE / (1.0 - BETA_ONE**STEPS_DONE)) * moment_new) * inverse
    return (1.0 - LEARN_RATE * DECAY_RATE) * weights - step, moment_new, second_new


def scalars_kernel(log_temp, log_mom, log_sq, sums, loss, norm_out, lt, lm, ls, scale):
    total = jnp.sum(sums[...], axis=0, keepdims=True)
    entropy, count = total[:, 3:4], total[:, 4:5]
    grad_temp = -entropy / count
    norm = jnp.sqrt(total[:, 5:6] / (count * count) + grad_temp * grad_temp)
    factor = CLIP_NORM / jnp.maximum(norm, CLIP_NORM)
    lane = lax.broadcasted_iota(jnp.int32, (1, 128), 1)
    loss[...] = jnp.where(lane == 3, -log_temp[0] * entropy, total)[:, 0:5]
    norm_out[...] = norm
    one = lambda v: jnp.full((1, 1), v[0])
    put((lt, lm, ls), (slice(0, 1),), adam(one(log_temp), one(log_mom), one(log_sq), factor * grad_temp))
    scale[...] = jnp.broadcast_to(factor / count, (8, 128))


def put(refs, at, got):
    for r, value in zip(refs, got):
        r[at] = value.astype(r.dtype)


def critic_update_kernel(n_z, part, sources, n_pieces, place, scale, *refs):
    refs = list(refs)
    take = lambda n: [refs.pop(0) for _ in range(n)]
    pieces = take(n_pieces)
    w, m, v, t, hw, hm, hv, ht = take(8)
    outs, (total,), near, (sem, body_sem) = take(10), take(1), take(10), take(2)
    scale = scale[0:1, 0:1]
    for k, i, first, start, stop in sources:
        piece = pieces[i]
        c = jnp.bitwise_xor(place[1], k // n_z)
        z = jnp.bitwise_xor(place[2], k % n_z)
        for side in range(2):
            at = pl.ds(4 * (part * z + start) + 2 * side + c, stop - start, stride=4)
            total[at, :] = piece[first : first + stop - start, side * 128 : (side + 1) * 128]
    copies = []
    rows = w.shape[0]
    for i, start in enumerate(range(0, rows, BLOCK)):
        at = pl.ds(start, min(BLOCK, rows - start))
        new, mom, sq = adam(w[at, :], m[at, :], v[at, :], total[at, :] * scale)
        tgt = t[at, :] + POLYAK_RATE * (new - t[at, :])
        put(near[0:5], (at, slice(None)), (new, mom, sq, tgt, new))
        copies += start_copies([r.at[at, :] for r in near[0:4]], [r.at[at, :] for r in outs[0:4]], body_sem.at[i])
    copies += start_copies(near[4:5], outs[4:5], sem)
    for c in range(2):
        at = slice(c, c + 1)
        rows8 = [total[4 * (BODY + k) + 2 * side + c : 4 * (BODY + k) + 2 * side + c + 1, :] for k, side in ((0, 0), (0, 1), (1, 0))]
        grad = jnp.concatenate([rows8[0], rows8[1], rows8[2][:, 0:1]], axis=1)
        new, mom, sq = adam(hw[at, :], hm[at, :], hv[at, :], grad * scale)
        tgt = ht[at, :] + POLYAK_RATE * (new - ht[at, :])
        put(near[5:10], (at, slice(None)), (new, mom, sq, tgt, new))
    copies += start_copies(near[5:], outs[5:], sem.at[pl.ds(5, 5)])
    for copy in copies:
        copy.wait()


def policy_update_kernel(small, n_blocks, place, scale, *refs):
    refs = list(refs)
    take = lambda n: [refs.pop(0) for _ in range(n)]
    blocks, (w, m, v, hw, hm, hv), outs, (policy,), near, (sem,) = take(n_blocks), take(6), take(8), take(1), take(8), take(1)
    scale = scale[0:1, 0:1]
    for owner, block in enumerate(blocks):
        for x in range(2):
            at = 2 * jnp.bitwise_xor(place[0], owner) + jnp.bitwise_xor(place[1], x)
            policy[pl.ds(pl.multiple_of(at * small, 8), small), :] = block[x * small : (x + 1) * small, :]
    n = S_DIM
    for mine, at in (
        (slice(0, n + 1), slice(0, n + 1)),
        (slice(P_TWO, P_TWO + HID + 1), slice(n + 1, n + 2 + HID)),
        (slice(P_THREE, P_THREE + HID + 1), slice(n + 2 + HID, n + 3 + 2 * HID)),
    ):
        new, mom, sq = adam(w[at], m[at], v[at], policy[mine, :] * scale)
        put(near[0:4], (at,), (new, mom, sq, new))
    copies = start_copies(near[:4], outs[:4], sem)
    by_head = policy[P_HEAD : P_HEAD + 16, :]
    last = jnp.broadcast_to(policy[P_LAST + 1 : P_LAST + 2, 0:16], (8, 16)).T[:, 0:1]
    for r, at in ((1, slice(0, A_DIM)), (9, slice(A_DIM, 2 * A_DIM))):
        grad = jnp.concatenate([by_head[r : r + A_DIM], last[r : r + A_DIM]], axis=1)
        new, mom, sq = adam(hw[at, :], hm[at, :], hv[at, :], grad * scale)
        put(near[4:8], (at, slice(None)), (new, mom, sq, new))
    copies += start_copies(near[4:], outs[4:], sem.at[pl.ds(4, 4)])
    for copy in copies:
        copy.wait()


def join_kernel(n, plan, *refs):
    for out, slices in zip(refs[n:], plan):
        at = 0
        for i, start, stop in slices:
            out[at : at + stop - start, :] = refs[i][start:stop, :]
            at += stop - start


def join(arrays, plan):
    outs = [shape(sum(stop - start for _, start, stop in slices), HID) for slices in plan]
    return call(functools.partial(join_kernel, len(arrays), plan), outs, [VMEM] * len(arrays), us=0.3)(*arrays)


def flat(v):
    return jnp.transpose(v.reshape(2, -1, 2, 128), (1, 2, 0, 3)).reshape(-1, 128)


def unflat(v):
    return jnp.transpose(v.reshape(-1, 2, 2, 128), (2, 0, 1, 3)).reshape(2, -1, HID)


def per_device(
    members,
    dp,
    states,
    actions,
    rewards,
    next_states,
    terminal,
    valid_rows,
    noise_seeds,
    member_live,
    critic_body,
    critic_body_mom,
    critic_body_sq,
    critic_body_tgt,
    critic_head,
    critic_head_mom,
    critic_head_sq,
    critic_head_tgt,
    policy_body,
    policy_body_mom,
    policy_body_sq,
    policy_head,
    policy_head_mom,
    policy_head_sq,
    log_temp,
    log_temp_mom,
    log_temp_sq,
):
    rows = states.shape[0]
    n_z = dp // 2
    part = -(-CRITIC_ROWS // (8 * n_z)) * 8
    small = -(-POLICY_ROWS // (16 * members)) * 8
    m, d = lax.axis_index("member"), lax.axis_index("dp")
    place = jnp.stack([m, d // n_z, d % n_z]).astype(jnp.int32)

    def across(value, axis, n, to):
        return lax.ppermute(value, axis, [(i, to(i)) for i in range(n)])

    def to_member(value, bit):
        return across(value, "member", members, lambda i: i ^ bit)

    def to_pair(value):
        return across(value, "dp", dp, lambda i: i ^ n_z)

    def along(value, offset):
        return across(value, "dp", dp, lambda i: i ^ offset)

    square = lambda v: v.reshape(rows // 128, 128)
    turned = [policy_head.T, policy_head_mom.T, policy_head_sq.T]
    body, mom, sq, body_tgt = flat(critic_body), flat(critic_body_mom), flat(critic_body_sq), flat(critic_body_tgt)
    like = lambda *arrays: [shape(*a.shape, dtype=a.dtype) for a in arrays]
    first = call(first_kernel, shape(8, 128), [SMEM], us=8.0, limit=1)(place)
    xs, xn, xp, aux, *actor_weights = call(
        actor_kernel,
        [shape(24, rows), shape(24, rows), shape(24, rows), shape(32, rows)] + trunk_arrays(1, S_DIM),
        [VMEM] * 10 + [SMEM],
        us=3.0,
    )(
        first, states.T, actions.T, next_states.T, noise_seeds.T, square(rewards), square(terminal), square(valid_rows),
        policy_body, turned[0], log_temp,
    )
    xs_far = to_pair(xs)
    ensemble, saved, *weights = call(
        critic_kernel,
        [shape(16, rows), shape(5, HID, rows)] + trunk_arrays(1, X_DIM),
        [SMEM, SMEM] + [VMEM] * 7,
        trunk_scratch(3, X_DIM) + [pltpu.VMEM((4, HID, 128), F32)],
        us=8.0,
    )(
        member_live, place, xs, xn, xp, body, critic_head, body_tgt, critic_head_tgt
    )
    bit = 1
    while bit * 2 < members:
        other = to_member(ensemble, bit)
        k = lax.broadcasted_iota(jnp.int32, ensemble.shape, 0)
        ensemble = jnp.where(k == 7, jnp.minimum(ensemble, other), ensemble + other)
        bit *= 2
    sx, gx, sums_joint = call(
        joint_kernel, [shape(8, rows), shape(8, rows), shape(1, 128)], [VMEM, VMEM, VMEM, SMEM], us=0.7
    )(ensemble, to_member(ensemble, bit), aux, log_temp)
    sx_far = to_pair(sx)
    keep, give = call(
        policy_kernel,
        [shape(small, HID), shape(small, HID)],
        [SMEM] + [VMEM] * 7 + [SMEM],
        [pltpu.VMEM((2 * members * small, HID), F32)],
        us=3.0,
    )(place, xs, aux, gx, *actor_weights, turned[0], log_temp)
    got = to_pair(give)
    both = 2 * rows
    left, side = pltpu.VMEM((HID + 16, 2 * both), BF16), pltpu.VMEM((HID, both), BF16)
    scratch = [left, side, side, left, side, side]
    grads, sums_second = call(
        second_kernel,
        [shape(part * n_z, HID), shape(1, 128)],
        [SMEM, SMEM] + [VMEM] * 11,
        scratch,
        us=8.0,
        limit=42,
    )(member_live, place, xs, xs_far, sx, sx_far, gx, saved, *weights, body, critic_head)
    message = shape(part + small, HID)
    dealt = call(deal_kernel, [message] * n_z, [SMEM, VMEM, VMEM, VMEM], us=0.5)(place, grads, keep, got)
    arrived = [dealt[0]] + [along(dealt[k], k) for k in range(1, n_z)]
    whole, sums = call(
        functools.partial(reduce_kernel, part),
        [message, shape(members * dp, 128)],
        [SMEM] + [VMEM] * (2 + n_z),
    )(place, sums_joint, sums_second, *arrived)
    sums = lax.all_to_all(sums, ("member", "dp"), 0, 0, tiled=True)
    piece = call(piece_kernel, shape(part, HID), [VMEM], us=8.0)(whole)
    pieces, bit = {0: piece, n_z: to_pair(whole)}, 1
    while bit < n_z:
        pieces[bit] = along(piece, bit)
        bit *= 2
    at_hand = sorted(pieces)
    *values, sums = lax.optimization_barrier((*[pieces[k] for k in at_hand], sums))
    pieces = dict(zip(at_hand, values))
    found = {k: [(pieces[k], 0, 0, part)] for k in at_hand}
    actor = [[(0, part, part + small), (1, part, part + small)]]
    (block,) = join([whole, pieces[n_z]], actor)
    if dp > 2:
        found[dp - 1] = [(along(pieces[0], dp - 1), 0, 0, part)]
    bits = dp.bit_length() - 1
    for level in range(2, bits):
        paths = {}
        for k in range(dp):
            if bin(k).count("1") == level:
                low, rest = k & -k, k & (k - 1)
                cut = part // 16 * 8 if k < n_z and level == 2 else 0
                paths.setdefault(low, []).append((k, cut, part))
                if cut:
                    paths.setdefault(rest, []).append((k, 0, cut))
        inputs = sorted({k & ~bit for bit, slices in paths.items() for k, _, _ in slices})
        plan = []
        for bit, slices in paths.items():
            plan.append([])
            for k, start, stop in slices:
                first = found[k & ~bit][0][1]
                plan[-1].append((inputs.index(k & ~bit), first + start, first + stop))
        sent = join([found[k][0][0] for k in inputs], plan)
        level_found = {}
        for (bit, slices), message in zip(paths.items(), sent):
            came, at = along(message, bit), 0
            for k, start, stop in slices:
                level_found.setdefault(k, []).append((came, at, start, stop))
                at += stop - start
        if level + 1 < bits:
            whole_ones = sorted(level_found)
            rows_of = [join([v[0] for v in sorted(level_found[k], key=lambda v: v[2])], [[(i, v[1], v[1] + v[3] - v[2]) for i, v in enumerate(sorted(level_found[k], key=lambda v: v[2]))]])[0] for k in whole_ones]
            level_found = {k: [(v, 0, 0, part)] for k, v in zip(whole_ones, rows_of)}
        found.update(level_found)
    blocks = [block] + [to_member(block, k) for k in range(1, members)]
    arrays, sources = [], []
    for k, places in sorted(found.items()):
        for array, at, start, stop in places:
            if not any(array is other for other in arrays):
                arrays.append(array)
            sources.append((k, [array is other for other in arrays].index(True), at, start, stop))
    halved = lambda a: shape(*a.shape, dtype=BF16)
    heads = [critic_head, critic_head_mom, critic_head_sq, critic_head_tgt]
    single = shape(1, 1)
    loss, norm, lt_new, lt_mom, lt_sq, scale = call(
        scalars_kernel, [shape(1, 5), single, single, single, single, shape(8, 128)], [SMEM] * 3 + [VMEM], us=0.5
    )(log_temp, log_temp_mom, log_temp_sq, sums)
    outs = like(body, body, body, body) + [halved(body)] + like(*heads) + [halved(critic_head)]
    critic = call(
        functools.partial(critic_update_kernel, n_z, part, sources, len(arrays)),
        outs,
        [SMEM] + [VMEM] * (1 + len(arrays) + 8),
        [pltpu.VMEM((4 * n_z * part, 128), F32)]
        + buffers(*outs)
        + [pltpu.SemaphoreType.DMA((-(-body.shape[0] // BLOCK), 4))],
        us=6.0,
        out_specs=[HBM] * len(outs),
    )(place, scale, *arrays, body, mom, sq, body_tgt, *heads)
    outs = like(policy_body, policy_body, policy_body) + [halved(policy_body)] + like(*turned) + [halved(turned[0])]
    policy = call(
        functools.partial(policy_update_kernel, small, len(blocks)),
        outs,
        [SMEM] + [VMEM] * (1 + len(blocks) + 6),
        [pltpu.VMEM((2 * members * small, HID), F32)] + buffers(*outs),
        us=0.2,
        out_specs=[HBM] * len(outs),
    )(place, scale, *blocks, policy_body, policy_body_mom, policy_body_sq, *turned)
    new = [unflat(v) for v in critic[:5]] + list(critic[5:]) + list(policy[:4]) + [v.T for v in policy[4:]]
    return (loss[0], norm[0], *new, lt_new[0], lt_mom[0], lt_sq[0])


def solution(mesh):
    row, line = P("dp", None), P("dp")
    stack, flat = P("member", None, None), P("member", None)
    return jax.shard_map(
        functools.partial(per_device, mesh.shape["member"], mesh.shape["dp"]),
        mesh=mesh,
        in_specs=(row, row, line, row, line, line, row, P("member")) + (stack,) * 4 + (flat,) * 4 + (P(),) * 9,
        out_specs=(P(), P()) + (stack,) * 5 + (flat,) * 5 + (P(),) * 11,
        check_vma=False,
    )
```

```python
import functools

import jax
import jax.numpy as jnp
from jax import lax
from jax.experimental import pallas as pl
from jax.experimental.pallas import tpu as pltpu
from jax.sharding import PartitionSpec as P

STEPS_DONE = 5
DISCOUNT = 0.99
POLYAK_RATE = 0.005
ENTROPY_TARGET = -6.0
DIVERSITY_WEIGHT = 1.0
LEARN_RATE = 0.05
BETA_ONE = 0.5
BETA_TWO = 0.5
DECAY_RATE = 0.01
ADAM_EPSILON = 1e-08
GRAD_FLOOR = 0.0001
CLIP_NORM = 1.0
LOGSTD_LOW = -5.0
LOGSTD_HIGH = 2.0
LOG_TWO = 0.6931471805599453
HALF_LOG_TWOPI = 0.9189385332046727
FAR_VALUE = 1e30

F32 = jnp.float32
BF16 = jnp.bfloat16
HID = 256
S_DIM = 17
A_DIM = 6
X_DIM = S_DIM + A_DIM
TWO = X_DIM + 1
THREE = TWO + HID + 1
BODY = THREE + HID + 1
CRITIC_ROWS = 544
P_TWO = 24
P_THREE = 288
P_LAST = 544
P_HEAD = 552
POLICY_ROWS = 576
BLOCK = 272
VMEM = pl.BlockSpec(memory_space=pltpu.VMEM)
SMEM = pl.BlockSpec(memory_space=pltpu.SMEM)
HBM = pl.BlockSpec(memory_space=pltpu.HBM)


def call(kernel, outs, in_specs, scratch=(), us=1.0, out_specs=None, limit=32):
    return pl.pallas_call(
        kernel,
        out_shape=outs,
        in_specs=in_specs,
        out_specs=out_specs or jax.tree.map(lambda _: VMEM, outs),
        scratch_shapes=list(scratch),
        compiler_params=pltpu.CompilerParams(vmem_limit_bytes=limit * 2**20),
        cost_estimate=pl.CostEstimate(flops=int(us * 1.15e9), bytes_accessed=0, transcendentals=0),
    )


def buffers(*arrays):
    return [pltpu.VMEM(a.shape, a.dtype) for a in arrays] + [pltpu.SemaphoreType.DMA((len(arrays),))]


def start_copies(sources, targets, sem):
    copies = [pltpu.make_async_copy(a, b, sem.at[i]) for i, (a, b) in enumerate(zip(sources, targets))]
    for copy in copies:
        copy.start()
    return copies


def shape(*dims, dtype=F32):
    return jax.ShapeDtypeStruct(dims, dtype)


def dot(a, b):
    return lax.dot_general(a, b, (((1,), (0,)), ((), ())), preferred_element_type=F32)


def dot_rows(a, b):
    return lax.dot_general(a, b, (((1,), (1,)), ((), ())), preferred_element_type=F32)


def halves(w):
    high = w.astype(BF16)
    return high, (w - high.astype(F32)).astype(BF16)


def stack_weights(w):
    high = (0.5 * w).astype(BF16).astype(F32)
    return jnp.concatenate([high, high, 0.5 * w - high], axis=0).T.astype(BF16)


def stack_inputs(v):
    high = v.astype(BF16).astype(F32)
    return jnp.concatenate([high, v - high, high], axis=0).astype(BF16)


def act(z):
    t = jnp.tanh(z)
    return z + z * t, t


def slope(h, t):
    return (1.0 + h) + t * (1.0 - h)


def curve(z, t):
    return (1.0 - t * t) * (1.0 - z * t)


def wide(column):
    return jnp.broadcast_to(column, (column.shape[0], 128))


def spread(column, rows):
    return jnp.concatenate([column] * (rows // 128), axis=1)


def action_rows(v):
    k = lax.broadcasted_iota(jnp.int32, v.shape, 0)
    return jnp.where((k >= 1) & (k <= A_DIM), v, 0.0)


def row_at(v, k, like):
    return jnp.where(lax.broadcasted_iota(jnp.int32, like.shape, 0) == k, v, like)


def lane_row(block):
    return jnp.concatenate([block[i : i + 1] for i in range(block.shape[0])], axis=1)


def interleave(*streams):
    results, active = [None] * len(streams), list(enumerate(streams))
    while active:
        left = []
        for i, stream in active:
            try:
                next(stream)
                left.append((i, stream))
            except StopIteration as end:
                results[i] = end.value
        active = left
    return results


def critic_rows(ref, c):
    def read(a, b):
        if b - a == 1:
            base = 4 * a // 8 * 8
            window = ref[base : base + 8, :]
            k = lax.broadcasted_iota(jnp.int32, window.shape, 0)
            picked = [jnp.where(k == 4 * a - base + 2 * t + c, window, 0.0) for t in range(2)]
            return jnp.concatenate([jnp.sum(v, axis=0, keepdims=True) for v in picked], axis=1)
        return jnp.concatenate([ref[pl.ds(4 * a + 2 * t + c, b - a, stride=4), :] for t in range(2)], axis=1)

    return read


def load_trunk(body, n_in, one, mats, bias, i, backward=False):
    one[i] = stack_weights(body(0, n_in + 1))
    yield
    for k, start in enumerate((n_in + 1, n_in + 2 + HID)):
        high, low = halves(0.5 * body(start, start + HID))
        mats[i, 4 * k] = high.T
        mats[i, 4 * k + 1] = low.T
        if backward:
            mats[i, 4 * k + 2] = high
            mats[i, 4 * k + 3] = low
        bias[i, k] = wide(0.5 * body(start + HID, start + HID + 1).T)
        yield


def trunk_arrays(n, n_in):
    return [shape(n, HID, 3 * (n_in + 1), dtype=BF16), shape(n, 8, HID, HID, dtype=BF16), shape(n, 2, HID, 128)]


def trunk_scratch(n, n_in):
    return [pltpu.VMEM(a.shape, a.dtype) for a in trunk_arrays(n, n_in)]


def times(w, k, h):
    mats, i = w
    return dot(mats[i, k], h) + dot(mats[i, k + 1], h)


def times_exact(w, k, h):
    mats, i = w
    high, low = halves(h)
    return dot(mats[i, k], high) + dot(mats[i, k + 1], high) + dot(mats[i, k], low)


def policy_head_rows(turned):
    one = jnp.zeros((1, HID + 1), F32)
    return jnp.concatenate([one, turned[:A_DIM], one, one, turned[A_DIM:], one], axis=0)


def noise_of(seed_row):
    k = lax.broadcasted_iota(jnp.int32, (8, seed_row.shape[1]), 0).astype(F32) - 1.0
    return 1.7 * jnp.sin(0.618034 * seed_row + 2.39996 * k)


def actor_stream(one, mats, bias, head, head_bias, x, noise):
    rows = x.shape[1]
    z = dot(one[0], stack_inputs(x))
    yield
    z = times((mats, 0), 0, act(z)[0].astype(BF16))
    yield
    z = times((mats, 0), 4, act(z + spread(bias[0, 0], rows))[0].astype(BF16))
    yield
    high, low = halves(act(z + spread(bias[0, 1], rows))[0])
    out = dot(head, high)
    out = out[:16] + out[16:] + dot(head[:16], low) + spread(head_bias, rows)
    yield
    mean, raw = out[:8], out[8:]
    turned = jnp.tanh(raw)
    log_std = LOGSTD_LOW + 0.5 * (LOGSTD_HIGH - LOGSTD_LOW) * (turned + 1.0)
    deviation = jnp.exp(log_std) * noise
    u = mean + deviation
    soft = jnp.maximum(-2.0 * u, 0.0) + jnp.log(1.0 + jnp.exp(-jnp.abs(2.0 * u)))
    squash = 2.0 * (LOG_TWO - u - soft)
    terms = -0.5 * noise * noise - log_std - HALF_LOG_TWOPI - squash
    log_prob = jnp.sum(action_rows(terms), axis=0, keepdims=True)
    return jnp.tanh(u), turned, deviation, log_prob


def first_kernel(place, out):
    out[...] = jnp.full(out.shape, (place[0] == 0).astype(F32))


def actor_kernel(
    first, states, actions, next_states, seeds, rewards, terminal, valid, body, head, log_temp, xs, xn, xp, aux, one, mats, bias
):
    rows = states.shape[1]
    ones = jnp.ones((1, rows), F32)
    for x, source in ((xs, states), (xn, next_states), (xp, states)):
        x[0:S_DIM, :] = source[...]
        x[X_DIM : X_DIM + 1, :] = ones
    xs[S_DIM:X_DIM, :] = actions[...]
    seed = seeds[...].astype(F32)
    loading = load_trunk(lambda a, b: body[a:b], S_DIM, one, mats, bias, 0, backward=True)
    next(loading)
    head_rows = policy_head_rows(head[...])
    head_w, head_b = jnp.concatenate(halves(head_rows[:, :HID]), axis=0), wide(head_rows[:, HID:])
    carry = 1.0 - lane_row(terminal[...].astype(F32))
    temper = jnp.exp(log_temp[0])
    now_in = jnp.concatenate([states[...], ones], axis=0)
    later_in = jnp.concatenate([next_states[...], ones], axis=0)
    half = rows // 2
    done = interleave(
        *[
            actor_stream(one, mats, bias, head_w, head_b, x[:, i : i + half], noise_of(seed[k : k + 1, i : i + half]))
            for i in (0, half)
            for x, k in ((later_in, 1), (now_in, 0))
        ],
        loading,
    )[:-1]
    later = [jnp.concatenate(v, axis=1) for v in zip(*done[0::2])]
    now = [jnp.concatenate(v, axis=1) for v in zip(*done[1::2])]
    xn[S_DIM:X_DIM, :] = later[0][1 : 1 + A_DIM]
    aux[0:1, :] = lane_row(rewards[...]) - DISCOUNT * carry * temper * later[3]
    aux[1:2, :] = DISCOUNT * carry
    aux[2:3, :] = lane_row(valid[...].astype(F32))
    action, turned, deviation, log_prob = now
    xp[S_DIM:X_DIM, :] = action[1 : 1 + A_DIM]
    aux[3:4, :] = log_prob
    aux[4:5, :] = spread(first[0:1], rows)
    aux[5:8, :] = jnp.zeros((3, rows), F32)
    aux[8:16, :] = action_rows(action)
    aux[16:24, :] = action_rows(turned)
    aux[24:32, :] = action_rows(deviation)


def head_column(head, c):
    row = head[pl.ds(c, 1), :]
    return row[:, :HID].T, row[:, HID:]


def inner_rows(read):
    high, low = halves(0.5 * read(16, 24))
    return jnp.concatenate([high.astype(F32), low.astype(F32)], axis=0).astype(BF16)


def action_gradient(inner, y):
    grad = dot(inner, y)
    return action_rows(grad[:8] + grad[8:])


def data_stream(one, mats, bias, i, column, inner, x, save):
    rows, w = x.shape[1], (mats, i)
    z = dot(one[i], x)
    save(0, z)
    yield
    h, t = act(z)
    d1 = slope(h, t)
    z = times_exact(w, 0, h)
    yield
    z = z + spread(bias[i, 0], rows)
    save(1, z)
    h, t = act(z)
    d2 = slope(h, t)
    z = times_exact(w, 4, h)
    yield
    z = z + spread(bias[i, 1], rows)
    save(2, z)
    h, t = act(z)
    c = times(w, 6, (spread(column, rows) * slope(h, t)).astype(BF16))
    yield
    save(3, c)
    c = times(w, 2, (c * d2).astype(BF16))
    yield
    save(4, c)
    grad = action_gradient(inner, (c * d1).astype(BF16))
    yield
    size = jnp.sum(grad * grad, axis=0, keepdims=True) + GRAD_FLOOR
    return grad * lax.rsqrt(size)


def target_stream(one, mats, bias, i, column, last, x):
    rows, w = x.shape[1], (mats, i)
    z = dot(one[i], x)
    yield
    z = times(w, 0, act(z)[0].astype(BF16))
    yield
    z = times(w, 4, act(z + spread(bias[i, 0], rows))[0].astype(BF16))
    yield
    h = act(z + spread(bias[i, 1], rows))[0]
    return jnp.sum(spread(column, rows) * h, axis=0, keepdims=True) + last


def chosen_stream(one, mats, bias, i, column, last, inner, x):
    rows = x.shape[1]
    z = dot(one[i], x)
    yield
    h, t = act(z)
    d1 = slope(h, t)
    z = dot(mats[i, 0], h.astype(BF16))
    yield
    h, t = act(z + spread(bias[i, 0], rows))
    d2 = slope(h, t)
    z = dot(mats[i, 4], h.astype(BF16))
    yield
    h, t = act(z + spread(bias[i, 1], rows))
    column = spread(column, rows)
    q = jnp.sum(column * h, axis=0, keepdims=True) + last
    c = dot(mats[i, 6], (column * slope(h, t)).astype(BF16))
    yield
    c = dot(mats[i, 2], (c * d2).astype(BF16))
    yield
    return q, action_gradient(inner, (c * d1).astype(BF16))


def critic_kernel(live, place, xs, xn, xp, body, head, body_tgt, head_tgt, out, saved, *refs):
    mine, scratch, columns = refs[:3], refs[3:6], refs[6]
    order = [place[1], 1 - place[1]]
    lasts, inners, trunks, loading = [], [], [], []
    for i in range(4):
        c = order[i % 2]
        read = critic_rows((body, body_tgt)[i // 2], c)
        trunks.append((*mine, 0) if i == 0 else (*scratch, i - 1))
        loading.append(load_trunk(read, X_DIM, *trunks[i], backward=i < 2))
        next(loading[-1])
        column, last = head_column((head, head_tgt)[i // 2], c)
        columns[i] = wide(column)
        lasts.append(last)
        if i < 2:
            inners.append(inner_rows(read))
    alive = [live[c].astype(F32) for c in order]
    rows = xs.shape[1]
    step = 256
    for start in range(0, rows, step):
        at = slice(start, start + step)
        data, later, chosen = stack_inputs(xs[:, at]), stack_inputs(xn[:, at]), stack_inputs(xp[:, at])

        def save(k, value, at=at):
            saved[k, :, at] = value

        done = interleave(
            data_stream(*trunks[0], columns[0], inners[0], data, save),
            data_stream(*trunks[1], columns[1], inners[1], data, lambda k, value: None),
            *[chosen_stream(*trunks[c], columns[c], lasts[c], inners[c], chosen) for c in range(2)],
            *[target_stream(*trunks[2 + c], columns[2 + c], lasts[2 + c], later) for c in range(2)],
            *loading,
        )
        loading = []
        unit, now, value = done[0:2], done[2:4], done[4:6]
        lowest = [jnp.where(alive[c] > 0, value[c], FAR_VALUE) for c in range(2)]
        total_n, total_q, total_g = [alive[0] * a + alive[1] * b for a, b in (unit, *zip(*now))]
        out[0:8, at] = row_at(jnp.minimum(lowest[0], lowest[1]), 7, row_at(alive[0] + alive[1], 0, total_n))
        out[8:16, at] = row_at(total_q, 0, total_g)


def merge(a, b):
    k = lax.broadcasted_iota(jnp.int32, a.shape, 0)
    return jnp.where(k == 7, jnp.minimum(a, b), a + b)


def joint_kernel(mine, other, aux, log_temp, sx, gx, sums):
    both = merge(mine[...], other[...])
    unit, grad = both[:8], both[8:]
    mask, log_prob = aux[2:3, :], aux[3:4, :]
    members = both[0:1]
    target = aux[0:1, :] + aux[1:2, :] * both[7:8]
    unit = action_rows(unit)
    sx[...] = row_at(target, 7, row_at(mask, 0, mask * unit))
    gx[...] = row_at(members, 7, grad)
    temper = jnp.exp(log_temp[0])
    spread = jnp.sum(mask * (jnp.sum(unit * unit, axis=0, keepdims=True) - members), axis=1, keepdims=True)
    actor = jnp.sum(mask * (temper * log_prob - both[8:9] / members), axis=1, keepdims=True)
    entropy = jnp.sum(mask * (log_prob + ENTROPY_TARGET), axis=1, keepdims=True)
    count = jnp.sum(mask, axis=1, keepdims=True)
    lane = lax.broadcasted_iota(jnp.int32, (1, 128), 1)
    row = jnp.where(lane == 1, spread, 0.0) + jnp.where(lane == 2, actor, 0.0)
    row = row + jnp.where(lane == 3, entropy, 0.0) + jnp.where(lane == 4, count, 0.0)
    sums[...] = row * aux[4:5, 0:128]


def policy_stream(one, mats, bias, head_back, x, rows8, by_log):
    rows, w = x.shape[1], (mats, 0)
    z = dot(one[0], stack_inputs(x))
    yield
    h, t = act(z)
    d1, h1 = slope(h, t), h.astype(BF16)
    z = times(w, 0, h1)
    yield
    h, t = act(z + spread(bias[0, 0], rows))
    d2, h2 = slope(h, t), h.astype(BF16)
    z = times(w, 4, h2)
    yield
    h, t = act(z + spread(bias[0, 1], rows))
    action, turned, deviation, by_action = rows8
    by_u = by_action * (1.0 - action * action) + by_log * 2.0 * action
    by_std = by_u * deviation - by_log
    by_raw = action_rows(by_std * (0.5 * (LOGSTD_HIGH - LOGSTD_LOW)) * (1.0 - turned * turned))
    by_out = jnp.concatenate([action_rows(by_u), by_raw], axis=0)
    high, low = halves(by_out)
    f3 = (dot(head_back, jnp.concatenate([high, low, high], axis=0)) * slope(h, t)).astype(BF16)
    yield
    f2 = (times(w, 6, f3) * d2).astype(BF16)
    yield
    f1 = (times(w, 2, f2) * d1).astype(BF16)
    yield
    return h1, h2, h.astype(BF16), f1, f2, f3, high, low, by_out


def policy_kernel(place, xs, aux, gx, one, mats, bias, head, log_temp, keep, give, full):
    rows = xs.shape[1]
    n = S_DIM
    head_high, head_low = halves(0.5 * policy_head_rows(head[...])[:, :HID])
    head_back = jnp.concatenate([head_high, head_high, head_low], axis=0).astype(F32).T.astype(BF16)
    x = row_at(1.0, n, xs[...])
    mask, members = aux[2:3, :], gx[7:8, :]
    by_action = -(mask / members) * action_rows(gx[...])
    by_log = jnp.exp(log_temp[0]) * mask
    rows8 = (aux[8:16, :], aux[16:24, :], aux[24:32, :], by_action)
    step = rows // 4
    cut = lambda v, i: v[:, i * step : (i + 1) * step]
    streams = [
        policy_stream(one, mats, bias, head_back, cut(x[: n + 1], i), [cut(v, i) for v in rows8], cut(by_log, i))
        for i in range(4)
    ]
    h1, h2, h3, f1, f2, f3, high, low, by_out = [jnp.concatenate(v, axis=1) for v in zip(*interleave(*streams))]
    ones = row_at(1.0, 0, jnp.zeros((16, rows), F32)).astype(BF16)
    start = jnp.where(lax.broadcasted_iota(jnp.int32, x.shape, 0) <= n, x, 0.0).astype(BF16)
    full[0:P_TWO, :] = dot_rows(start, f1)
    full[P_TWO:P_THREE, :] = dot_rows(jnp.concatenate([h1, ones], axis=0), f2)[: HID + 8]
    layer = dot_rows(jnp.concatenate([h2, ones], axis=0), f3)
    full[P_THREE : P_THREE + HID, :] = layer[:HID]
    last = wide(jnp.sum(by_out, axis=1, keepdims=True)).T[0:1]
    last = jnp.concatenate([last, jnp.zeros((1, HID - 16), F32)], axis=1)
    full[P_LAST:P_HEAD, :] = row_at(last, 1, layer[HID : HID + 8])
    by_head = dot_rows(jnp.concatenate([high, low], axis=0), h3)
    full[P_HEAD : P_HEAD + 16, :] = by_head[:16] + by_head[16:]
    full[P_HEAD + 16 :, :] = jnp.zeros((full.shape[0] - P_HEAD - 16, HID), F32)
    size = keep.shape[0]
    for out, x in ((keep, place[1]), (give, 1 - place[1])):
        out[...] = full[pl.ds(pl.multiple_of((2 * place[0] + x) * size, 8), size), :]


def padded(parts, rows):
    return jnp.concatenate([v if n == 0 else jnp.zeros((n, rows), F32) for n, v in parts], axis=0).astype(BF16)


def second_stream(
    one, mats, bias, column, last, inner, inner_stack, alive, weight, x, s, saved, here, left3, here3, there3, left2, here2,
    there2,
):
    rows, w = x.shape[1], (mats, 0)
    total = left3.shape[1] // 2
    there = slice(total + here.start, total + here.stop)
    one_row = row_at(1.0, 0, jnp.zeros((16, rows), F32))
    none = jnp.zeros((16, rows), BF16)
    mask, target = s[0:1], s[7:8]
    for left in (left2, left3):
        left[HID : HID + 16, here] = one_row.astype(BF16)
        left[HID : HID + 16, there] = none
    z = dot(one[0], stack_inputs(x)) if saved is None else saved[0]
    yield
    h, t = act(z)
    d1, e1 = slope(h, t), curve(z, t)
    left2[0:HID, here] = h.astype(BF16)
    if saved is None:
        z = times_exact(w, 0, h)
        yield
        z = z + spread(bias[0, 0], rows)
    else:
        z = saved[1]
        yield
    h, t = act(z)
    d2, e2 = slope(h, t), curve(z, t)
    left3[0:HID, here] = h.astype(BF16)
    if saved is None:
        z = times_exact(w, 4, h)
        yield
        z = z + spread(bias[0, 1], rows)
    else:
        z = saved[2]
        yield
    h, t = act(z)
    d3, e3 = slope(h, t), curve(z, t)
    column = spread(column, rows)
    q = jnp.sum(column * h, axis=0, keepdims=True) + last
    miss = q - target
    half_a = alive * mask * miss
    td = jnp.sum(half_a * miss, axis=1, keepdims=True)
    head = (2.0 * half_a) * h
    b3 = column * d3
    e3 = column * e3
    cut = b3.astype(BF16)
    there3[:, here] = cut
    c2 = times(w, 6, cut) if saved is None else saved[3]
    yield
    b2 = c2 * d2
    e2 = c2 * e2
    cut = b2.astype(BF16)
    there2[:, here] = cut
    c1 = times(w, 2, cut) if saved is None else saved[4]
    yield
    b1 = c1 * d1
    e1 = c1 * e1
    cut = b1.astype(BF16)
    there1 = cut
    grad = action_gradient(inner, cut)
    yield
    size = jnp.sum(grad * grad, axis=0, keepdims=True) + GRAD_FLOOR
    cot = action_rows(s) * weight
    along = jnp.sum(grad * cot, axis=0, keepdims=True)
    v = lax.rsqrt(size) * (cot - grad * (along / size))
    first = dot_rows(there1, padded([(16, 0), (0, 0.5 * v), (8, 0)], rows))
    t1 = dot(inner_stack, stack_inputs(v))
    yield
    cut = (d1 * t1).astype(BF16)
    left2[0:HID, there] = cut
    t2 = times(w, 0, cut)
    yield
    cut = (d2 * t2).astype(BF16)
    left3[0:HID, there] = cut
    t3 = times(w, 4, cut)
    yield
    head = head + d3 * t3
    head = sum(head[:, i : i + 128] for i in range(0, rows, 128))
    r = e3 * t3
    here3[:, here] = (half_a * b3 + r).astype(BF16)
    r = dot(mats[0, 6], r.astype(BF16)) * d2 + e2 * t2
    yield
    here2[:, here] = (half_a * b2 + r).astype(BF16)
    r = dot(mats[0, 2], r.astype(BF16)) * d1 + e1 * t1
    yield
    first = first + dot_rows((half_a * b1 + r).astype(BF16), padded([(0, x), (8, 0)], rows))
    return td, jnp.sum(half_a, axis=1, keepdims=True), head, first


def second_kernel(live, place, xs, xs_far, sx, sx_far, gx, saved, one, mats, bias, body, head, *refs):
    (grads, sums), scratch = refs[:2], refs[2:]
    left3, here3, there3, left2, here2, there2 = scratch
    rows = xs.shape[1]
    mine = place[1]
    alive = jnp.where(mine == 0, live[0], live[1]).astype(F32)
    read = critic_rows(body, mine)
    column, last = head_column(head, mine)
    column = wide(column)
    inner, inner_stack = inner_rows(read), stack_weights(read(16, 24))
    weight = 2.0 * DIVERSITY_WEIGHT * alive / (gx[7:8, :] - 1.0)
    td = bias_sum = jnp.zeros((1, 1), F32)
    step = rows // 2
    by_head, first = jnp.zeros((HID, 128), F32), jnp.zeros((HID, 32), F32)
    for td_part, bias_part, head_part, first_part in interleave(
        *[
            second_stream(
                one, mats, bias, column, last, inner, inner_stack, alive, weight[:, start : start + step],
                x[:, start : start + step], s[:, start : start + step],
                None if i else [saved[k, :, start : start + step] for k in range(5)],
                slice(i * rows + start, i * rows + start + step), *scratch,
            )
            for start in range(0, rows, step)
            for i, (x, s) in enumerate(((xs, sx), (xs_far, sx_far)))
        ]
    ):
        td, bias_sum, by_head, first = td + td_part, bias_sum + bias_part, by_head + head_part, first + first_part

    def layer(left, here, there):
        n = here.shape[1]
        return dot_rows(left[:, 0:n], here[...]) + 0.5 * dot_rows(left[:, n:], there[...])

    grads[0:TWO, :] = first.T[0:TWO]
    grads[TWO:THREE, :] = layer(left2, here2, there2)[0 : HID + 1]
    grads[THREE:BODY, :] = layer(left3, here3, there3)[0 : HID + 1]
    grads[BODY : BODY + 1, :] = jnp.sum(by_head.T, axis=0, keepdims=True)
    lane = lax.broadcasted_iota(jnp.int32, (1, HID), 1)
    grads[BODY + 1 : BODY + 2, :] = jnp.where(lane == 0, 2.0 * bias_sum, 0.0)
    grads[BODY + 2 :, :] = jnp.zeros((grads.shape[0] - BODY - 2, HID), F32)
    sums[...] = jnp.where(lax.broadcasted_iota(jnp.int32, (1, 128), 1) == 0, td, 0.0)


def deal_kernel(place, critic, keep, got, *out):
    n = len(out)
    part = critic.shape[0] // n
    policy = keep[...] + got[...]
    for k in range(n):
        to = jnp.bitwise_xor(place[2], k)
        out[k][0:part, :] = critic[pl.ds(pl.multiple_of(to * part, 8), part), :]
        out[k][part:, :] = policy


def reduce_kernel(part, place, one, two, *refs):
    ins, (out, sums) = refs[:-2], refs[-2:]
    total = ins[0][...]
    for r in ins[1:]:
        total = total + r[...]
    out[...] = total
    critic, policy = total[:part], total[part:]
    square = jnp.sum(jnp.sum(critic * critic, axis=0, keepdims=True), axis=1, keepdims=True)
    once = (place[2] == 0).astype(F32)
    square = square + once * jnp.sum(jnp.sum(policy * policy, axis=0, keepdims=True), axis=1, keepdims=True)
    lane = lax.broadcasted_iota(jnp.int32, (1, 128), 1)
    row = one[...] + two[...] + jnp.where(lane == 5, square, 0.0)
    sums[...] = jnp.broadcast_to(row, sums.shape)


def piece_kernel(whole, out):
    out[...] = whole[0 : out.shape[0], :]


def adam(weights, moment, second, grads):
    moment_new = BETA_ONE * (moment + grads)
    second_new = BETA_TWO * (second + grads * grads)
    root = (1.0 / (1.0 - BETA_TWO**STEPS_DONE)) ** 0.5
    bottom = (root * second_new) * lax.rsqrt(second_new) + ADAM_EPSILON
    guess = pltpu.reciprocal(bottom, approx=True)
    inverse = guess * (2.0 - bottom * guess)
    step = ((LEARN_RATE / (1.0 - BETA_ONE**STEPS_DONE)) * moment_new) * inverse
    return (1.0 - LEARN_RATE * DECAY_RATE) * weights - step, moment_new, second_new


def scalars_kernel(log_temp, log_mom, log_sq, sums, loss, norm_out, lt, lm, ls, scale):
    total = jnp.sum(sums[...], axis=0, keepdims=True)
    entropy, count = total[:, 3:4], total[:, 4:5]
    grad_temp = -entropy / count
    norm = jnp.sqrt(total[:, 5:6] / (count * count) + grad_temp * grad_temp)
    factor = CLIP_NORM / jnp.maximum(norm, CLIP_NORM)
    lane = lax.broadcasted_iota(jnp.int32, (1, 128), 1)
    loss[...] = jnp.where(lane == 3, -log_temp[0] * entropy, total)[:, 0:5]
    norm_out[...] = norm
    one = lambda v: jnp.full((1, 1), v[0])
    put((lt, lm, ls), (slice(0, 1),), adam(one(log_temp), one(log_mom), one(log_sq), factor * grad_temp))
    scale[...] = jnp.broadcast_to(factor / count, (8, 128))


def put(refs, at, got):
    for r, value in zip(refs, got):
        r[at] = value.astype(r.dtype)


def critic_update_kernel(n_z, part, sources, n_pieces, place, scale, *refs):
    refs = list(refs)
    take = lambda n: [refs.pop(0) for _ in range(n)]
    pieces = take(n_pieces)
    w, m, v, t, hw, hm, hv, ht = take(8)
    outs, (total,), near, (sem, body_sem) = take(10), take(1), take(10), take(2)
    scale = scale[0:1, 0:1]
    for k, i, first, start, stop in sources:
        piece = pieces[i]
        c = jnp.bitwise_xor(place[1], k // n_z)
        z = jnp.bitwise_xor(place[2], k % n_z)
        for side in range(2):
            at = pl.ds(4 * (part * z + start) + 2 * side + c, stop - start, stride=4)
            total[at, :] = piece[first : first + stop - start, side * 128 : (side + 1) * 128]
    copies = []
    rows = w.shape[0]
    for i, start in enumerate(range(0, rows, BLOCK)):
        at = pl.ds(start, min(BLOCK, rows - start))
        new, mom, sq = adam(w[at, :], m[at, :], v[at, :], total[at, :] * scale)
        tgt = t[at, :] + POLYAK_RATE * (new - t[at, :])
        put(near[0:4], (at, slice(None)), (new, mom, sq, tgt))
        copies += start_copies([r.at[at, :] for r in near[0:4]], [r.at[at, :] for r in outs[0:4]], body_sem.at[i])
    near[4][...] = near[0][...].astype(BF16)
    copies += start_copies(near[4:5], outs[4:5], sem)
    grads = []
    for c in range(2):
        first = [4 * BODY + c, 4 * BODY + 2 + c, 4 * BODY + 4 + c]
        grads.append(jnp.concatenate([total[first[0] : first[0] + 1, :], total[first[1] : first[1] + 1, :], total[first[2] : first[2] + 1, 0:1]], axis=1))
    new, mom, sq = adam(hw[...], hm[...], hv[...], jnp.concatenate(grads, axis=0) * scale)
    tgt = ht[...] + POLYAK_RATE * (new - ht[...])
    put(near[5:10], (slice(None), slice(None)), (new, mom, sq, tgt, new))
    copies += start_copies(near[5:], outs[5:], sem.at[pl.ds(5, 5)])
    for copy in copies:
        copy.wait()


def policy_update_kernel(small, n_blocks, place, scale, *refs):
    refs = list(refs)
    take = lambda n: [refs.pop(0) for _ in range(n)]
    blocks, (w, m, v, hw, hm, hv), outs, (policy, natural), near, (sem,) = take(n_blocks), take(6), take(8), take(2), take(8), take(1)
    scale = scale[0:1, 0:1]
    for owner, block in enumerate(blocks):
        for x in range(2):
            at = 2 * jnp.bitwise_xor(place[0], owner) + jnp.bitwise_xor(place[1], x)
            policy[pl.ds(pl.multiple_of(at * small, 8), small), :] = block[x * small : (x + 1) * small, :]
    second, third = S_DIM + 1, S_DIM + 2 + HID
    natural[0:second, :] = policy[0:second, :]
    natural[second:third, :] = policy[P_TWO : P_TWO + HID + 1, :]
    natural[third:, :] = policy[P_THREE : P_THREE + HID + 1, :]
    new, mom, sq = adam(w[...], m[...], v[...], natural[...] * scale)
    put(near[0:4], (slice(None),), (new, mom, sq, new))
    copies = start_copies(near[:4], outs[:4], sem)
    by_head = policy[P_HEAD : P_HEAD + 16, :]
    last = jnp.broadcast_to(policy[P_LAST + 1 : P_LAST + 2, 0:16], (8, 16)).T[:, 0:1]
    grad = jnp.concatenate([by_head, last], axis=1)
    grad = jnp.concatenate([grad[1 : 1 + A_DIM], grad[9 : 9 + A_DIM]], axis=0)
    new, mom, sq = adam(hw[...], hm[...], hv[...], grad * scale)
    put(near[4:8], (slice(None), slice(None)), (new, mom, sq, new))
    copies += start_copies(near[4:], outs[4:], sem.at[pl.ds(4, 4)])
    for copy in copies:
        copy.wait()


def join_kernel(n, plan, *refs):
    for out, slices in zip(refs[n:], plan):
        at = 0
        for i, start, stop in slices:
            out[at : at + stop - start, :] = refs[i][start:stop, :]
            at += stop - start


def join(arrays, plan):
    outs = [shape(sum(stop - start for _, start, stop in slices), HID) for slices in plan]
    return call(functools.partial(join_kernel, len(arrays), plan), outs, [VMEM] * len(arrays), us=0.3)(*arrays)


def flat(v):
    return jnp.transpose(v.reshape(2, -1, 2, 128), (1, 2, 0, 3)).reshape(-1, 128)


def unflat(v):
    return jnp.transpose(v.reshape(-1, 2, 2, 128), (2, 0, 1, 3)).reshape(2, -1, HID)


def per_device(
    members,
    dp,
    states,
    actions,
    rewards,
    next_states,
    terminal,
    valid_rows,
    noise_seeds,
    member_live,
    critic_body,
    critic_body_mom,
    critic_body_sq,
    critic_body_tgt,
    critic_head,
    critic_head_mom,
    critic_head_sq,
    critic_head_tgt,
    policy_body,
    policy_body_mom,
    policy_body_sq,
    policy_head,
    policy_head_mom,
    policy_head_sq,
    log_temp,
    log_temp_mom,
    log_temp_sq,
):
    rows = states.shape[0]
    n_z = dp // 2
    part = -(-CRITIC_ROWS // (8 * n_z)) * 8
    small = -(-POLICY_ROWS // (16 * members)) * 8
    m, d = lax.axis_index("member"), lax.axis_index("dp")
    place = jnp.stack([m, d // n_z, d % n_z]).astype(jnp.int32)

    def across(value, axis, n, to):
        return lax.ppermute(value, axis, [(i, to(i)) for i in range(n)])

    def to_member(value, bit):
        return across(value, "member", members, lambda i: i ^ bit)

    def to_pair(value):
        return across(value, "dp", dp, lambda i: i ^ n_z)

    def along(value, offset):
        return across(value, "dp", dp, lambda i: i ^ offset)

    square = lambda v: v.reshape(rows // 128, 128)
    turned = [policy_head.T, policy_head_mom.T, policy_head_sq.T]
    body, mom, sq, body_tgt = flat(critic_body), flat(critic_body_mom), flat(critic_body_sq), flat(critic_body_tgt)
    like = lambda *arrays: [shape(*a.shape, dtype=a.dtype) for a in arrays]
    first = call(first_kernel, shape(8, 128), [SMEM], us=8.0, limit=1)(place)
    xs, xn, xp, aux, *actor_weights = call(
        actor_kernel,
        [shape(24, rows), shape(24, rows), shape(24, rows), shape(32, rows)] + trunk_arrays(1, S_DIM),
        [VMEM] * 10 + [SMEM],
        us=3.0,
    )(
        first, states.T, actions.T, next_states.T, noise_seeds.T, square(rewards), square(terminal), square(valid_rows),
        policy_body, turned[0], log_temp,
    )
    xs_far = to_pair(xs)
    ensemble, saved, *weights = call(
        critic_kernel,
        [shape(16, rows), shape(5, HID, rows)] + trunk_arrays(1, X_DIM),
        [SMEM, SMEM] + [VMEM] * 7,
        trunk_scratch(3, X_DIM) + [pltpu.VMEM((4, HID, 128), F32)],
        us=8.0,
    )(
        member_live, place, xs, xn, xp, body, critic_head, body_tgt, critic_head_tgt
    )
    bit = 1
    while bit * 2 < members:
        other = to_member(ensemble, bit)
        k = lax.broadcasted_iota(jnp.int32, ensemble.shape, 0)
        ensemble = jnp.where(k == 7, jnp.minimum(ensemble, other), ensemble + other)
        bit *= 2
    sx, gx, sums_joint = call(
        joint_kernel, [shape(8, rows), shape(8, rows), shape(1, 128)], [VMEM, VMEM, VMEM, SMEM], us=0.7
    )(ensemble, to_member(ensemble, bit), aux, log_temp)
    sx_far = to_pair(sx)
    keep, give = call(
        policy_kernel,
        [shape(small, HID), shape(small, HID)],
        [SMEM] + [VMEM] * 7 + [SMEM],
        [pltpu.VMEM((2 * members * small, HID), F32)],
        us=3.0,
    )(place, xs, aux, gx, *actor_weights, turned[0], log_temp)
    got = to_pair(give)
    both = 2 * rows
    left, side = pltpu.VMEM((HID + 16, 2 * both), BF16), pltpu.VMEM((HID, both), BF16)
    scratch = [left, side, side, left, side, side]
    grads, sums_second = call(
        second_kernel,
        [shape(part * n_z, HID), shape(1, 128)],
        [SMEM, SMEM] + [VMEM] * 11,
        scratch,
        us=8.0,
        limit=42,
    )(member_live, place, xs, xs_far, sx, sx_far, gx, saved, *weights, body, critic_head)
    message = shape(part + small, HID)
    dealt = call(deal_kernel, [message] * n_z, [SMEM, VMEM, VMEM, VMEM], us=0.5)(place, grads, keep, got)
    arrived = [dealt[0]] + [along(dealt[k], k) for k in range(1, n_z)]
    whole, sums = call(
        functools.partial(reduce_kernel, part),
        [message, shape(members * dp, 128)],
        [SMEM] + [VMEM] * (2 + n_z),
    )(place, sums_joint, sums_second, *arrived)
    sums = lax.all_to_all(sums, ("member", "dp"), 0, 0, tiled=True)
    piece = call(piece_kernel, shape(part, HID), [VMEM], us=8.0)(whole)
    pieces, bit = {0: piece, n_z: to_pair(whole)}, 1
    while bit < n_z:
        pieces[bit] = along(piece, bit)
        bit *= 2
    at_hand = sorted(pieces)
    *values, sums = lax.optimization_barrier((*[pieces[k] for k in at_hand], sums))
    pieces = dict(zip(at_hand, values))
    found = {k: [(pieces[k], 0, 0, part)] for k in at_hand}
    actor = [[(0, part, part + small), (1, part, part + small)]]
    (block,) = join([whole, pieces[n_z]], actor)
    if dp > 2:
        found[dp - 1] = [(along(pieces[0], dp - 1), 0, 0, part)]
    bits = dp.bit_length() - 1
    for level in range(2, bits):
        paths = {}
        for k in range(dp):
            if bin(k).count("1") == level:
                low, rest = k & -k, k & (k - 1)
                cut = part // 16 * 8 if k < n_z and level == 2 else 0
                paths.setdefault(low, []).append((k, cut, part))
                if cut:
                    paths.setdefault(rest, []).append((k, 0, cut))
        inputs = sorted({k & ~bit for bit, slices in paths.items() for k, _, _ in slices})
        plan = []
        for bit, slices in paths.items():
            plan.append([])
            for k, start, stop in slices:
                first = found[k & ~bit][0][1]
                plan[-1].append((inputs.index(k & ~bit), first + start, first + stop))
        sent = join([found[k][0][0] for k in inputs], plan)
        level_found = {}
        for (bit, slices), message in zip(paths.items(), sent):
            came, at = along(message, bit), 0
            for k, start, stop in slices:
                level_found.setdefault(k, []).append((came, at, start, stop))
                at += stop - start
        if level + 1 < bits:
            whole_ones = sorted(level_found)
            rows_of = [join([v[0] for v in sorted(level_found[k], key=lambda v: v[2])], [[(i, v[1], v[1] + v[3] - v[2]) for i, v in enumerate(sorted(level_found[k], key=lambda v: v[2]))]])[0] for k in whole_ones]
            level_found = {k: [(v, 0, 0, part)] for k, v in zip(whole_ones, rows_of)}
        found.update(level_found)
    blocks = [block] + [to_member(block, k) for k in range(1, members)]
    arrays, sources = [], []
    for k, places in sorted(found.items()):
        for array, at, start, stop in places:
            if not any(array is other for other in arrays):
                arrays.append(array)
            sources.append((k, [array is other for other in arrays].index(True), at, start, stop))
    halved = lambda a: shape(*a.shape, dtype=BF16)
    heads = [critic_head, critic_head_mom, critic_head_sq, critic_head_tgt]
    single = shape(1, 1)
    loss, norm, lt_new, lt_mom, lt_sq, scale = call(
        scalars_kernel, [shape(1, 5), single, single, single, single, shape(8, 128)], [SMEM] * 3 + [VMEM], us=0.5
    )(log_temp, log_temp_mom, log_temp_sq, sums)
    outs = like(body, body, body, body) + [halved(body)] + like(*heads) + [halved(critic_head)]
    critic = call(
        functools.partial(critic_update_kernel, n_z, part, sources, len(arrays)),
        outs,
        [SMEM] + [VMEM] * (1 + len(arrays) + 8),
        [pltpu.VMEM((4 * n_z * part + 8, 128), F32)]
        + buffers(*outs)
        + [pltpu.SemaphoreType.DMA((-(-body.shape[0] // BLOCK), 4))],
        us=6.0,
        out_specs=[HBM] * len(outs),
    )(place, scale, *arrays, body, mom, sq, body_tgt, *heads)
    outs = like(policy_body, policy_body, policy_body) + [halved(policy_body)] + like(*turned) + [halved(turned[0])]
    policy = call(
        functools.partial(policy_update_kernel, small, len(blocks)),
        outs,
        [SMEM] + [VMEM] * (1 + len(blocks) + 6),
        [pltpu.VMEM((2 * members * small, HID), F32), pltpu.VMEM(policy_body.shape, F32)] + buffers(*outs),
        us=0.2,
        out_specs=[HBM] * len(outs),
    )(place, scale, *blocks, policy_body, policy_body_mom, policy_body_sq, *turned)
    new = [unflat(v) for v in critic[:5]] + list(critic[5:]) + list(policy[:4]) + [v.T for v in policy[4:]]
    return (loss[0], norm[0], *new, lt_new[0], lt_mom[0], lt_sq[0])


def solution(mesh):
    row, line = P("dp", None), P("dp")
    stack, flat = P("member", None, None), P("member", None)
    return jax.shard_map(
        functools.partial(per_device, mesh.shape["member"], mesh.shape["dp"]),
        mesh=mesh,
        in_specs=(row, row, line, row, line, line, row, P("member")) + (stack,) * 4 + (flat,) * 4 + (P(),) * 9,
        out_specs=(P(), P()) + (stack,) * 5 + (flat,) * 5 + (P(),) * 11,
        check_vma=False,
    )
```

```python
import functools

import jax
import jax.numpy as jnp
from jax import lax
from jax.experimental import pallas as pl
from jax.experimental.pallas import tpu as pltpu
from jax.sharding import PartitionSpec as P

STEPS_DONE = 5
DISCOUNT = 0.99
POLYAK_RATE = 0.005
ENTROPY_TARGET = -6.0
DIVERSITY_WEIGHT = 1.0
LEARN_RATE = 0.05
BETA_ONE = 0.5
BETA_TWO = 0.5
DECAY_RATE = 0.01
ADAM_EPSILON = 1e-08
GRAD_FLOOR = 0.0001
CLIP_NORM = 1.0
LOGSTD_LOW = -5.0
LOGSTD_HIGH = 2.0
LOG_TWO = 0.6931471805599453
HALF_LOG_TWOPI = 0.9189385332046727
FAR_VALUE = 1e30

F32 = jnp.float32
BF16 = jnp.bfloat16
HID = 256
S_DIM = 17
A_DIM = 6
X_DIM = S_DIM + A_DIM
TWO = X_DIM + 1
THREE = TWO + HID + 1
BODY = THREE + HID + 1
CRITIC_ROWS = 544
P_TWO = 24
P_THREE = 288
P_LAST = 544
P_HEAD = 552
POLICY_ROWS = 576
BLOCK = 272
VMEM = pl.BlockSpec(memory_space=pltpu.VMEM)
SMEM = pl.BlockSpec(memory_space=pltpu.SMEM)
HBM = pl.BlockSpec(memory_space=pltpu.HBM)


def call(kernel, outs, in_specs, scratch=(), us=1.0, out_specs=None, limit=32):
    return pl.pallas_call(
        kernel,
        out_shape=outs,
        in_specs=in_specs,
        out_specs=out_specs or jax.tree.map(lambda _: VMEM, outs),
        scratch_shapes=list(scratch),
        compiler_params=pltpu.CompilerParams(vmem_limit_bytes=limit * 2**20),
        cost_estimate=pl.CostEstimate(flops=int(us * 1.15e9), bytes_accessed=0, transcendentals=0),
    )


def buffers(*arrays):
    return [pltpu.VMEM(a.shape, a.dtype) for a in arrays] + [pltpu.SemaphoreType.DMA((len(arrays),))]


def start_copies(sources, targets, sem):
    copies = [pltpu.make_async_copy(a, b, sem.at[i]) for i, (a, b) in enumerate(zip(sources, targets))]
    for copy in copies:
        copy.start()
    return copies


def shape(*dims, dtype=F32):
    return jax.ShapeDtypeStruct(dims, dtype)


def dot(a, b):
    return lax.dot_general(a, b, (((1,), (0,)), ((), ())), preferred_element_type=F32)


def dot_rows(a, b):
    return lax.dot_general(a, b, (((1,), (1,)), ((), ())), preferred_element_type=F32)


def halves(w):
    high = w.astype(BF16)
    return high, (w - high.astype(F32)).astype(BF16)


def stack_weights(w):
    high = (0.5 * w).astype(BF16).astype(F32)
    return jnp.concatenate([high, high, 0.5 * w - high], axis=0).T.astype(BF16)


def stack_inputs(v):
    high = v.astype(BF16).astype(F32)
    return jnp.concatenate([high, v - high, high], axis=0).astype(BF16)


def act(z):
    t = jnp.tanh(z)
    return z + z * t, t


def slope(h, t):
    return (1.0 + h) + t * (1.0 - h)


def curve(z, t):
    return (1.0 - t * t) * (1.0 - z * t)


def wide(column):
    return jnp.broadcast_to(column, (column.shape[0], 128))


def spread(column, rows):
    return jnp.concatenate([column] * (rows // 128), axis=1)


def action_rows(v):
    k = lax.broadcasted_iota(jnp.int32, v.shape, 0)
    return jnp.where((k >= 1) & (k <= A_DIM), v, 0.0)


def row_at(v, k, like):
    return jnp.where(lax.broadcasted_iota(jnp.int32, like.shape, 0) == k, v, like)


def lane_row(block):
    return jnp.concatenate([block[i : i + 1] for i in range(block.shape[0])], axis=1)


def interleave(*streams):
    results, active = [None] * len(streams), list(enumerate(streams))
    while active:
        left = []
        for i, stream in active:
            try:
                next(stream)
                left.append((i, stream))
            except StopIteration as end:
                results[i] = end.value
        active = left
    return results


def critic_rows(ref, c):
    def read(a, b):
        if b - a == 1:
            base = 4 * a // 8 * 8
            window = ref[base : base + 8, :]
            k = lax.broadcasted_iota(jnp.int32, window.shape, 0)
            picked = [jnp.where(k == 4 * a - base + 2 * t + c, window, 0.0) for t in range(2)]
            return jnp.concatenate([jnp.sum(v, axis=0, keepdims=True) for v in picked], axis=1)
        return jnp.concatenate([ref[pl.ds(4 * a + 2 * t + c, b - a, stride=4), :] for t in range(2)], axis=1)

    return read


def load_trunk(body, n_in, one, mats, bias, i, backward=False):
    one[i] = stack_weights(body(0, n_in + 1))
    yield
    for k, start in enumerate((n_in + 1, n_in + 2 + HID)):
        high, low = halves(0.5 * body(start, start + HID))
        mats[i, 4 * k] = high.T
        mats[i, 4 * k + 1] = low.T
        if backward:
            mats[i, 4 * k + 2] = high
            mats[i, 4 * k + 3] = low
        bias[i, k] = wide(0.5 * body(start + HID, start + HID + 1).T)
        yield


def trunk_arrays(n, n_in):
    return [shape(n, HID, 3 * (n_in + 1), dtype=BF16), shape(n, 8, HID, HID, dtype=BF16), shape(n, 2, HID, 128)]


def trunk_scratch(n, n_in):
    return [pltpu.VMEM(a.shape, a.dtype) for a in trunk_arrays(n, n_in)]


def times(w, k, h):
    mats, i = w
    return dot(mats[i, k], h) + dot(mats[i, k + 1], h)


def times_exact(w, k, h):
    mats, i = w
    high, low = halves(h)
    return dot(mats[i, k], high) + dot(mats[i, k + 1], high) + dot(mats[i, k], low)


def policy_head_rows(turned):
    one = jnp.zeros((1, HID + 1), F32)
    return jnp.concatenate([one, turned[:A_DIM], one, one, turned[A_DIM:], one], axis=0)


def noise_of(seed_row):
    k = lax.broadcasted_iota(jnp.int32, (8, seed_row.shape[1]), 0).astype(F32) - 1.0
    return 1.7 * jnp.sin(0.618034 * seed_row + 2.39996 * k)


def actor_stream(one, mats, bias, head, head_bias, x, noise):
    rows = x.shape[1]
    z = dot(one[0], stack_inputs(x))
    yield
    z = times((mats, 0), 0, act(z)[0].astype(BF16))
    yield
    z = times((mats, 0), 4, act(z + spread(bias[0, 0], rows))[0].astype(BF16))
    yield
    high, low = halves(act(z + spread(bias[0, 1], rows))[0])
    out = dot(head, high)
    out = out[:16] + out[16:] + dot(head[:16], low) + spread(head_bias, rows)
    yield
    mean, raw = out[:8], out[8:]
    turned = jnp.tanh(raw)
    log_std = LOGSTD_LOW + 0.5 * (LOGSTD_HIGH - LOGSTD_LOW) * (turned + 1.0)
    deviation = jnp.exp(log_std) * noise
    u = mean + deviation
    soft = jnp.maximum(-2.0 * u, 0.0) + jnp.log(1.0 + jnp.exp(-jnp.abs(2.0 * u)))
    squash = 2.0 * (LOG_TWO - u - soft)
    terms = -0.5 * noise * noise - log_std - HALF_LOG_TWOPI - squash
    log_prob = jnp.sum(action_rows(terms), axis=0, keepdims=True)
    return jnp.tanh(u), turned, deviation, log_prob


def first_kernel(place, out):
    out[...] = jnp.full(out.shape, (place[0] == 0).astype(F32))


def actor_kernel(
    first, states, actions, next_states, seeds, rewards, terminal, valid, body, head, log_temp, xs, xn, xp, aux, one, mats, bias
):
    rows = states.shape[1]
    ones = jnp.ones((1, rows), F32)
    for x, source in ((xs, states), (xn, next_states), (xp, states)):
        x[0:S_DIM, :] = source[...]
        x[X_DIM : X_DIM + 1, :] = ones
    xs[S_DIM:X_DIM, :] = actions[...]
    seed = seeds[...].astype(F32)
    loading = load_trunk(lambda a, b: body[a:b], S_DIM, one, mats, bias, 0, backward=True)
    next(loading)
    head_rows = policy_head_rows(head[...])
    head_w, head_b = jnp.concatenate(halves(head_rows[:, :HID]), axis=0), wide(head_rows[:, HID:])
    carry = 1.0 - lane_row(terminal[...].astype(F32))
    temper = jnp.exp(log_temp[0])
    now_in = jnp.concatenate([states[...], ones], axis=0)
    later_in = jnp.concatenate([next_states[...], ones], axis=0)
    half = rows // 2
    done = interleave(
        *[
            actor_stream(one, mats, bias, head_w, head_b, x[:, i : i + half], noise_of(seed[k : k + 1, i : i + half]))
            for i in (0, half)
            for x, k in ((later_in, 1), (now_in, 0))
        ],
        loading,
    )[:-1]
    later = [jnp.concatenate(v, axis=1) for v in zip(*done[0::2])]
    now = [jnp.concatenate(v, axis=1) for v in zip(*done[1::2])]
    xn[S_DIM:X_DIM, :] = later[0][1 : 1 + A_DIM]
    aux[0:1, :] = lane_row(rewards[...]) - DISCOUNT * carry * temper * later[3]
    aux[1:2, :] = DISCOUNT * carry
    aux[2:3, :] = lane_row(valid[...].astype(F32))
    action, turned, deviation, log_prob = now
    xp[S_DIM:X_DIM, :] = action[1 : 1 + A_DIM]
    aux[3:4, :] = log_prob
    aux[4:5, :] = spread(first[0:1], rows)
    aux[5:8, :] = jnp.zeros((3, rows), F32)
    aux[8:16, :] = action_rows(action)
    aux[16:24, :] = action_rows(turned)
    aux[24:32, :] = action_rows(deviation)


def head_column(head, c):
    row = head[pl.ds(c, 1), :]
    return row[:, :HID].T, row[:, HID:]


def inner_rows(read):
    high, low = halves(0.5 * read(16, 24))
    return jnp.concatenate([high.astype(F32), low.astype(F32)], axis=0).astype(BF16)


def action_gradient(inner, y):
    grad = dot(inner, y)
    return action_rows(grad[:8] + grad[8:])


def data_stream(one, mats, bias, i, column, inner, x, save):
    rows, w = x.shape[1], (mats, i)
    z = dot(one[i], x)
    save(0, z)
    yield
    h, t = act(z)
    d1 = slope(h, t)
    z = times_exact(w, 0, h)
    yield
    z = z + spread(bias[i, 0], rows)
    save(1, z)
    h, t = act(z)
    d2 = slope(h, t)
    z = times_exact(w, 4, h)
    yield
    z = z + spread(bias[i, 1], rows)
    save(2, z)
    h, t = act(z)
    c = times(w, 6, (spread(column, rows) * slope(h, t)).astype(BF16))
    yield
    save(3, c)
    c = times(w, 2, (c * d2).astype(BF16))
    yield
    save(4, c)
    grad = action_gradient(inner, (c * d1).astype(BF16))
    yield
    size = jnp.sum(grad * grad, axis=0, keepdims=True) + GRAD_FLOOR
    return grad * lax.rsqrt(size)


def target_stream(one, mats, bias, i, column, last, x):
    rows, w = x.shape[1], (mats, i)
    z = dot(one[i], x)
    yield
    z = times(w, 0, act(z)[0].astype(BF16))
    yield
    z = times(w, 4, act(z + spread(bias[i, 0], rows))[0].astype(BF16))
    yield
    h = act(z + spread(bias[i, 1], rows))[0]
    return jnp.sum(spread(column, rows) * h, axis=0, keepdims=True) + last


def chosen_stream(one, mats, bias, i, column, last, inner, x):
    rows = x.shape[1]
    z = dot(one[i], x)
    yield
    h, t = act(z)
    d1 = slope(h, t)
    z = dot(mats[i, 0], h.astype(BF16))
    yield
    h, t = act(z + spread(bias[i, 0], rows))
    d2 = slope(h, t)
    z = dot(mats[i, 4], h.astype(BF16))
    yield
    h, t = act(z + spread(bias[i, 1], rows))
    column = spread(column, rows)
    q = jnp.sum(column * h, axis=0, keepdims=True) + last
    c = dot(mats[i, 6], (column * slope(h, t)).astype(BF16))
    yield
    c = dot(mats[i, 2], (c * d2).astype(BF16))
    yield
    return q, action_gradient(inner, (c * d1).astype(BF16))


def critic_kernel(live, place, xs, xn, xp, body, head, body_tgt, head_tgt, out, saved, *refs):
    mine, scratch, columns = refs[:3], refs[3:6], refs[6]
    order = [place[1], 1 - place[1]]
    lasts, inners, trunks, loading = [], [], [], []
    for i in range(4):
        c = order[i % 2]
        read = critic_rows((body, body_tgt)[i // 2], c)
        trunks.append((*mine, 0) if i == 0 else (*scratch, i - 1))
        loading.append(load_trunk(read, X_DIM, *trunks[i], backward=i < 2))
        next(loading[-1])
        column, last = head_column((head, head_tgt)[i // 2], c)
        columns[i] = wide(column)
        lasts.append(last)
        if i < 2:
            inners.append(inner_rows(read))
    alive = [live[c].astype(F32) for c in order]
    rows = xs.shape[1]
    step = 256
    for start in range(0, rows, step):
        at = slice(start, start + step)
        data, later, chosen = stack_inputs(xs[:, at]), stack_inputs(xn[:, at]), stack_inputs(xp[:, at])

        def save(k, value, at=at):
            saved[k, :, at] = value

        done = interleave(
            data_stream(*trunks[0], columns[0], inners[0], data, save),
            data_stream(*trunks[1], columns[1], inners[1], data, lambda k, value: None),
            *[chosen_stream(*trunks[c], columns[c], lasts[c], inners[c], chosen) for c in range(2)],
            *[target_stream(*trunks[2 + c], columns[2 + c], lasts[2 + c], later) for c in range(2)],
            *loading,
        )
        loading = []
        unit, now, value = done[0:2], done[2:4], done[4:6]
        lowest = [jnp.where(alive[c] > 0, value[c], FAR_VALUE) for c in range(2)]
        total_n, total_q, total_g = [alive[0] * a + alive[1] * b for a, b in (unit, *zip(*now))]
        out[0:8, at] = row_at(jnp.minimum(lowest[0], lowest[1]), 7, row_at(alive[0] + alive[1], 0, total_n))
        out[8:16, at] = row_at(total_q, 0, total_g)


def merge(a, b):
    k = lax.broadcasted_iota(jnp.int32, a.shape, 0)
    return jnp.where(k == 7, jnp.minimum(a, b), a + b)


def joint_kernel(mine, other, aux, log_temp, sx, gx, sums):
    both = merge(mine[...], other[...])
    unit, grad = both[:8], both[8:]
    mask, log_prob = aux[2:3, :], aux[3:4, :]
    members = both[0:1]
    target = aux[0:1, :] + aux[1:2, :] * both[7:8]
    unit = action_rows(unit)
    sx[...] = row_at(target, 7, row_at(mask, 0, mask * unit))
    gx[...] = row_at(members, 7, grad)
    temper = jnp.exp(log_temp[0])
    spread = jnp.sum(mask * (jnp.sum(unit * unit, axis=0, keepdims=True) - members), axis=1, keepdims=True)
    actor = jnp.sum(mask * (temper * log_prob - both[8:9] / members), axis=1, keepdims=True)
    entropy = jnp.sum(mask * (log_prob + ENTROPY_TARGET), axis=1, keepdims=True)
    count = jnp.sum(mask, axis=1, keepdims=True)
    lane = lax.broadcasted_iota(jnp.int32, (1, 128), 1)
    row = jnp.where(lane == 1, spread, 0.0) + jnp.where(lane == 2, actor, 0.0)
    row = row + jnp.where(lane == 3, entropy, 0.0) + jnp.where(lane == 4, count, 0.0)
    sums[...] = row * aux[4:5, 0:128]


def policy_stream(one, mats, bias, head_back, x, rows8, by_log):
    rows, w = x.shape[1], (mats, 0)
    z = dot(one[0], stack_inputs(x))
    yield
    h, t = act(z)
    d1, h1 = slope(h, t), h.astype(BF16)
    z = times(w, 0, h1)
    yield
    h, t = act(z + spread(bias[0, 0], rows))
    d2, h2 = slope(h, t), h.astype(BF16)
    z = times(w, 4, h2)
    yield
    h, t = act(z + spread(bias[0, 1], rows))
    action, turned, deviation, by_action = rows8
    by_u = by_action * (1.0 - action * action) + by_log * 2.0 * action
    by_std = by_u * deviation - by_log
    by_raw = action_rows(by_std * (0.5 * (LOGSTD_HIGH - LOGSTD_LOW)) * (1.0 - turned * turned))
    by_out = jnp.concatenate([action_rows(by_u), by_raw], axis=0)
    high, low = halves(by_out)
    f3 = (dot(head_back, jnp.concatenate([high, low, high], axis=0)) * slope(h, t)).astype(BF16)
    yield
    f2 = (times(w, 6, f3) * d2).astype(BF16)
    yield
    f1 = (times(w, 2, f2) * d1).astype(BF16)
    yield
    return h1, h2, h.astype(BF16), f1, f2, f3, high, low, by_out


def policy_kernel(place, xs, aux, gx, one, mats, bias, head, log_temp, keep, give, full):
    rows = xs.shape[1]
    n = S_DIM
    head_high, head_low = halves(0.5 * policy_head_rows(head[...])[:, :HID])
    head_back = jnp.concatenate([head_high, head_high, head_low], axis=0).astype(F32).T.astype(BF16)
    x = row_at(1.0, n, xs[...])
    mask, members = aux[2:3, :], gx[7:8, :]
    by_action = -(mask / members) * action_rows(gx[...])
    by_log = jnp.exp(log_temp[0]) * mask
    rows8 = (aux[8:16, :], aux[16:24, :], aux[24:32, :], by_action)
    step = rows // 4
    cut = lambda v, i: v[:, i * step : (i + 1) * step]
    streams = [
        policy_stream(one, mats, bias, head_back, cut(x[: n + 1], i), [cut(v, i) for v in rows8], cut(by_log, i))
        for i in range(4)
    ]
    h1, h2, h3, f1, f2, f3, high, low, by_out = [jnp.concatenate(v, axis=1) for v in zip(*interleave(*streams))]
    ones = row_at(1.0, 0, jnp.zeros((16, rows), F32)).astype(BF16)
    start = jnp.where(lax.broadcasted_iota(jnp.int32, x.shape, 0) <= n, x, 0.0).astype(BF16)
    full[0:P_TWO, :] = dot_rows(start, f1)
    full[P_TWO:P_THREE, :] = dot_rows(jnp.concatenate([h1, ones], axis=0), f2)[: HID + 8]
    layer = dot_rows(jnp.concatenate([h2, ones], axis=0), f3)
    full[P_THREE : P_THREE + HID, :] = layer[:HID]
    last = wide(jnp.sum(by_out, axis=1, keepdims=True)).T[0:1]
    last = jnp.concatenate([last, jnp.zeros((1, HID - 16), F32)], axis=1)
    full[P_LAST:P_HEAD, :] = row_at(last, 1, layer[HID : HID + 8])
    by_head = dot_rows(jnp.concatenate([high, low], axis=0), h3)
    full[P_HEAD : P_HEAD + 16, :] = by_head[:16] + by_head[16:]
    full[P_HEAD + 16 :, :] = jnp.zeros((full.shape[0] - P_HEAD - 16, HID), F32)
    size = keep.shape[0]
    for out, x in ((keep, place[1]), (give, 1 - place[1])):
        out[...] = full[pl.ds(pl.multiple_of((2 * place[0] + x) * size, 8), size), :]


def padded(parts, rows):
    return jnp.concatenate([v if n == 0 else jnp.zeros((n, rows), F32) for n, v in parts], axis=0).astype(BF16)


def second_stream(
    one, mats, bias, column, last, inner, inner_stack, alive, weight, x, s, saved, here, left3, here3, there3, left2, here2,
    there2,
):
    rows, w = x.shape[1], (mats, 0)
    total = left3.shape[1] // 2
    there = slice(total + here.start, total + here.stop)
    one_row = row_at(1.0, 0, jnp.zeros((16, rows), F32))
    none = jnp.zeros((16, rows), BF16)
    mask, target = s[0:1], s[7:8]
    for left in (left2, left3):
        left[HID : HID + 16, here] = one_row.astype(BF16)
        left[HID : HID + 16, there] = none
    z = dot(one[0], stack_inputs(x)) if saved is None else saved[0]
    yield
    h, t = act(z)
    d1, e1 = slope(h, t), curve(z, t)
    left2[0:HID, here] = h.astype(BF16)
    if saved is None:
        z = times_exact(w, 0, h)
        yield
        z = z + spread(bias[0, 0], rows)
    else:
        z = saved[1]
        yield
    h, t = act(z)
    d2, e2 = slope(h, t), curve(z, t)
    left3[0:HID, here] = h.astype(BF16)
    if saved is None:
        z = times_exact(w, 4, h)
        yield
        z = z + spread(bias[0, 1], rows)
    else:
        z = saved[2]
        yield
    h, t = act(z)
    d3, e3 = slope(h, t), curve(z, t)
    column = spread(column, rows)
    q = jnp.sum(column * h, axis=0, keepdims=True) + last
    miss = q - target
    half_a = alive * mask * miss
    td = jnp.sum(half_a * miss, axis=1, keepdims=True)
    head = (2.0 * half_a) * h
    b3 = column * d3
    e3 = column * e3
    cut = b3.astype(BF16)
    there3[:, here] = cut
    c2 = times(w, 6, cut) if saved is None else saved[3]
    yield
    b2 = c2 * d2
    e2 = c2 * e2
    cut = b2.astype(BF16)
    there2[:, here] = cut
    c1 = times(w, 2, cut) if saved is None else saved[4]
    yield
    b1 = c1 * d1
    e1 = c1 * e1
    cut = b1.astype(BF16)
    there1 = cut
    grad = action_gradient(inner, cut)
    yield
    size = jnp.sum(grad * grad, axis=0, keepdims=True) + GRAD_FLOOR
    cot = action_rows(s) * weight
    along = jnp.sum(grad * cot, axis=0, keepdims=True)
    v = lax.rsqrt(size) * (cot - grad * (along / size))
    first = dot_rows(there1, padded([(16, 0), (0, 0.5 * v), (8, 0)], rows))
    t1 = dot(inner_stack, stack_inputs(v))
    yield
    cut = (d1 * t1).astype(BF16)
    left2[0:HID, there] = cut
    t2 = times(w, 0, cut)
    yield
    cut = (d2 * t2).astype(BF16)
    left3[0:HID, there] = cut
    t3 = times(w, 4, cut)
    yield
    head = head + d3 * t3
    head = sum(head[:, i : i + 128] for i in range(0, rows, 128))
    r = e3 * t3
    here3[:, here] = (half_a * b3 + r).astype(BF16)
    r = dot(mats[0, 6], r.astype(BF16)) * d2 + e2 * t2
    yield
    here2[:, here] = (half_a * b2 + r).astype(BF16)
    r = dot(mats[0, 2], r.astype(BF16)) * d1 + e1 * t1
    yield
    first = first + dot_rows((half_a * b1 + r).astype(BF16), padded([(0, x), (8, 0)], rows))
    return td, jnp.sum(half_a, axis=1, keepdims=True), head, first


def second_kernel(live, place, xs, xs_far, sx, sx_far, gx, saved, one, mats, bias, body, head, *refs):
    (grads, sums), scratch = refs[:2], refs[2:]
    left3, here3, there3, left2, here2, there2 = scratch
    rows = xs.shape[1]
    mine = place[1]
    alive = jnp.where(mine == 0, live[0], live[1]).astype(F32)
    read = critic_rows(body, mine)
    column, last = head_column(head, mine)
    column = wide(column)
    inner, inner_stack = inner_rows(read), stack_weights(read(16, 24))
    weight = 2.0 * DIVERSITY_WEIGHT * alive / (gx[7:8, :] - 1.0)
    td = bias_sum = jnp.zeros((1, 1), F32)
    step = rows // 2
    by_head, first = jnp.zeros((HID, 128), F32), jnp.zeros((HID, 32), F32)
    for td_part, bias_part, head_part, first_part in interleave(
        *[
            second_stream(
                one, mats, bias, column, last, inner, inner_stack, alive, weight[:, start : start + step],
                x[:, start : start + step], s[:, start : start + step],
                None if i else [saved[k, :, start : start + step] for k in range(5)],
                slice(i * rows + start, i * rows + start + step), *scratch,
            )
            for start in range(0, rows, step)
            for i, (x, s) in enumerate(((xs, sx), (xs_far, sx_far)))
        ]
    ):
        td, bias_sum, by_head, first = td + td_part, bias_sum + bias_part, by_head + head_part, first + first_part

    def layer(left, here, there):
        n = here.shape[1]
        return dot_rows(left[:, 0:n], here[...]) + 0.5 * dot_rows(left[:, n:], there[...])

    grads[0:TWO, :] = first.T[0:TWO]
    grads[TWO:THREE, :] = layer(left2, here2, there2)[0 : HID + 1]
    grads[THREE:BODY, :] = layer(left3, here3, there3)[0 : HID + 1]
    grads[BODY : BODY + 1, :] = jnp.sum(by_head.T, axis=0, keepdims=True)
    lane = lax.broadcasted_iota(jnp.int32, (1, HID), 1)
    grads[BODY + 1 : BODY + 2, :] = jnp.where(lane == 0, 2.0 * bias_sum, 0.0)
    grads[BODY + 2 :, :] = jnp.zeros((grads.shape[0] - BODY - 2, HID), F32)
    sums[...] = jnp.where(lax.broadcasted_iota(jnp.int32, (1, 128), 1) == 0, td, 0.0)


def deal_kernel(place, critic, keep, got, *out):
    n = len(out)
    part = critic.shape[0] // n
    policy = keep[...] + got[...]
    for k in range(n):
        to = jnp.bitwise_xor(place[2], k)
        out[k][0:part, :] = critic[pl.ds(pl.multiple_of(to * part, 8), part), :]
        out[k][part:, :] = policy


def reduce_kernel(part, place, one, two, *refs):
    ins, (out, sums) = refs[:-2], refs[-2:]
    total = ins[0][...]
    for r in ins[1:]:
        total = total + r[...]
    out[...] = total
    critic, policy = total[:part], total[part:]
    square = jnp.sum(jnp.sum(critic * critic, axis=0, keepdims=True), axis=1, keepdims=True)
    once = (place[2] == 0).astype(F32)
    square = square + once * jnp.sum(jnp.sum(policy * policy, axis=0, keepdims=True), axis=1, keepdims=True)
    lane = lax.broadcasted_iota(jnp.int32, (1, 128), 1)
    row = one[...] + two[...] + jnp.where(lane == 5, square, 0.0)
    sums[...] = jnp.broadcast_to(row, sums.shape)


def piece_kernel(whole, out):
    out[...] = whole[0 : out.shape[0], :]


def adam(weights, moment, second, grads):
    moment_new = BETA_ONE * (moment + grads)
    second_new = BETA_TWO * (second + grads * grads)
    root = (1.0 / (1.0 - BETA_TWO**STEPS_DONE)) ** 0.5
    bottom = (root * second_new) * lax.rsqrt(second_new) + ADAM_EPSILON
    guess = pltpu.reciprocal(bottom, approx=True)
    inverse = guess * (2.0 - bottom * guess)
    step = ((LEARN_RATE / (1.0 - BETA_ONE**STEPS_DONE)) * moment_new) * inverse
    return (1.0 - LEARN_RATE * DECAY_RATE) * weights - step, moment_new, second_new


def scalars_kernel(log_temp, log_mom, log_sq, sums, loss, norm_out, lt, lm, ls, scale):
    total = jnp.sum(sums[...], axis=0, keepdims=True)
    entropy, count = total[:, 3:4], total[:, 4:5]
    grad_temp = -entropy / count
    norm = jnp.sqrt(total[:, 5:6] / (count * count) + grad_temp * grad_temp)
    factor = CLIP_NORM / jnp.maximum(norm, CLIP_NORM)
    lane = lax.broadcasted_iota(jnp.int32, (1, 128), 1)
    loss[...] = jnp.where(lane == 3, -log_temp[0] * entropy, total)[:, 0:5]
    norm_out[...] = norm
    one = lambda v: jnp.full((1, 1), v[0])
    put((lt, lm, ls), (slice(0, 1),), adam(one(log_temp), one(log_mom), one(log_sq), factor * grad_temp))
    scale[...] = jnp.broadcast_to(factor / count, (8, 128))


def put(refs, at, got):
    for r, value in zip(refs, got):
        r[at] = value.astype(r.dtype)


def critic_update_kernel(n_z, part, sources, n_pieces, place, scale, *refs):
    refs = list(refs)
    take = lambda n: [refs.pop(0) for _ in range(n)]
    pieces = take(n_pieces)
    w, m, v, t, hw, hm, hv, ht = take(8)
    outs, (total,), near, (sem, body_sem) = take(10), take(1), take(10), take(2)
    scale = scale[0:1, 0:1]
    for k, i, first, start, stop in sources:
        piece = pieces[i]
        c = jnp.bitwise_xor(place[1], k // n_z)
        z = jnp.bitwise_xor(place[2], k % n_z)
        for side in range(2):
            at = pl.ds(4 * (part * z + start) + 2 * side + c, stop - start, stride=4)
            total[at, :] = piece[first : first + stop - start, side * 128 : (side + 1) * 128]
    copies = []
    rows = w.shape[0]
    for i, start in enumerate(range(0, rows, BLOCK)):
        at = pl.ds(start, min(BLOCK, rows - start))
        new, mom, sq = adam(w[at, :], m[at, :], v[at, :], total[at, :] * scale)
        tgt = t[at, :] + POLYAK_RATE * (new - t[at, :])
        put(near[0:4], (at, slice(None)), (new, mom, sq, tgt))
        copies += start_copies([r.at[at, :] for r in near[0:4]], [r.at[at, :] for r in outs[0:4]], body_sem.at[i])
    near[4][...] = near[0][...].astype(BF16)
    copies += start_copies(near[4:5], outs[4:5], sem)
    grads = []
    for c in range(2):
        first = [4 * BODY + c, 4 * BODY + 2 + c, 4 * BODY + 4 + c]
        grads.append(jnp.concatenate([total[first[0] : first[0] + 1, :], total[first[1] : first[1] + 1, :], total[first[2] : first[2] + 1, 0:1]], axis=1))
    new, mom, sq = adam(hw[...], hm[...], hv[...], jnp.concatenate(grads, axis=0) * scale)
    tgt = ht[...] + POLYAK_RATE * (new - ht[...])
    put(near[5:10], (slice(None), slice(None)), (new, mom, sq, tgt, new))
    copies += start_copies(near[5:], outs[5:], sem.at[pl.ds(5, 5)])
    for copy in copies:
        copy.wait()


def policy_update_kernel(small, n_blocks, place, scale, *refs):
    refs = list(refs)
    take = lambda n: [refs.pop(0) for _ in range(n)]
    blocks, (w, m, v, hw, hm, hv), near, (policy, natural) = take(n_blocks), take(6), take(8), take(2)
    scale = scale[0:1, 0:1]
    for owner, block in enumerate(blocks):
        for x in range(2):
            at = 2 * jnp.bitwise_xor(place[0], owner) + jnp.bitwise_xor(place[1], x)
            policy[pl.ds(pl.multiple_of(at * small, 8), small), :] = block[x * small : (x + 1) * small, :]
    second, third = S_DIM + 1, S_DIM + 2 + HID
    natural[0:second, :] = policy[0:second, :]
    natural[second:third, :] = policy[P_TWO : P_TWO + HID + 1, :]
    natural[third:, :] = policy[P_THREE : P_THREE + HID + 1, :]
    new, mom, sq = adam(w[...], m[...], v[...], natural[...] * scale)
    put(near[0:4], (slice(None),), (new, mom, sq, new))
    by_head = policy[P_HEAD : P_HEAD + 16, :]
    last = jnp.broadcast_to(policy[P_LAST + 1 : P_LAST + 2, 0:16], (8, 16)).T[:, 0:1]
    grad = jnp.concatenate([by_head, last], axis=1)
    grad = jnp.concatenate([grad[1 : 1 + A_DIM], grad[9 : 9 + A_DIM]], axis=0)
    new, mom, sq = adam(hw[...], hm[...], hv[...], grad * scale)
    put(near[4:8], (slice(None), slice(None)), (new, mom, sq, new))


def join_kernel(n, plan, *refs):
    for out, slices in zip(refs[n:], plan):
        at = 0
        for i, start, stop in slices:
            out[at : at + stop - start, :] = refs[i][start:stop, :]
            at += stop - start


def join(arrays, plan):
    outs = [shape(sum(stop - start for _, start, stop in slices), HID) for slices in plan]
    return call(functools.partial(join_kernel, len(arrays), plan), outs, [VMEM] * len(arrays), us=0.3)(*arrays)


def flat(v):
    return jnp.transpose(v.reshape(2, -1, 2, 128), (1, 2, 0, 3)).reshape(-1, 128)


def unflat(v):
    return jnp.transpose(v.reshape(-1, 2, 2, 128), (2, 0, 1, 3)).reshape(2, -1, HID)


def per_device(
    members,
    dp,
    states,
    actions,
    rewards,
    next_states,
    terminal,
    valid_rows,
    noise_seeds,
    member_live,
    critic_body,
    critic_body_mom,
    critic_body_sq,
    critic_body_tgt,
    critic_head,
    critic_head_mom,
    critic_head_sq,
    critic_head_tgt,
    policy_body,
    policy_body_mom,
    policy_body_sq,
    policy_head,
    policy_head_mom,
    policy_head_sq,
    log_temp,
    log_temp_mom,
    log_temp_sq,
):
    rows = states.shape[0]
    n_z = dp // 2
    part = -(-CRITIC_ROWS // (8 * n_z)) * 8
    small = -(-POLICY_ROWS // (16 * members)) * 8
    m, d = lax.axis_index("member"), lax.axis_index("dp")
    place = jnp.stack([m, d // n_z, d % n_z]).astype(jnp.int32)

    def across(value, axis, n, to):
        return lax.ppermute(value, axis, [(i, to(i)) for i in range(n)])

    def to_member(value, bit):
        return across(value, "member", members, lambda i: i ^ bit)

    def to_pair(value):
        return across(value, "dp", dp, lambda i: i ^ n_z)

    def along(value, offset):
        return across(value, "dp", dp, lambda i: i ^ offset)

    square = lambda v: v.reshape(rows // 128, 128)
    turned = [policy_head.T, policy_head_mom.T, policy_head_sq.T]
    body, mom, sq, body_tgt = flat(critic_body), flat(critic_body_mom), flat(critic_body_sq), flat(critic_body_tgt)
    like = lambda *arrays: [shape(*a.shape, dtype=a.dtype) for a in arrays]
    first = call(first_kernel, shape(8, 128), [SMEM], us=8.0, limit=1)(place)
    xs, xn, xp, aux, *actor_weights = call(
        actor_kernel,
        [shape(24, rows), shape(24, rows), shape(24, rows), shape(32, rows)] + trunk_arrays(1, S_DIM),
        [VMEM] * 10 + [SMEM],
        us=3.0,
    )(
        first, states.T, actions.T, next_states.T, noise_seeds.T, square(rewards), square(terminal), square(valid_rows),
        policy_body, turned[0], log_temp,
    )
    xs_far = to_pair(xs)
    ensemble, saved, *weights = call(
        critic_kernel,
        [shape(16, rows), shape(5, HID, rows)] + trunk_arrays(1, X_DIM),
        [SMEM, SMEM] + [VMEM] * 7,
        trunk_scratch(3, X_DIM) + [pltpu.VMEM((4, HID, 128), F32)],
        us=8.0,
    )(
        member_live, place, xs, xn, xp, body, critic_head, body_tgt, critic_head_tgt
    )
    bit = 1
    while bit * 2 < members:
        other = to_member(ensemble, bit)
        k = lax.broadcasted_iota(jnp.int32, ensemble.shape, 0)
        ensemble = jnp.where(k == 7, jnp.minimum(ensemble, other), ensemble + other)
        bit *= 2
    sx, gx, sums_joint = call(
        joint_kernel, [shape(8, rows), shape(8, rows), shape(1, 128)], [VMEM, VMEM, VMEM, SMEM], us=0.7
    )(ensemble, to_member(ensemble, bit), aux, log_temp)
    sx_far = to_pair(sx)
    keep, give = call(
        policy_kernel,
        [shape(small, HID), shape(small, HID)],
        [SMEM] + [VMEM] * 7 + [SMEM],
        [pltpu.VMEM((2 * members * small, HID), F32)],
        us=3.0,
    )(place, xs, aux, gx, *actor_weights, turned[0], log_temp)
    got = to_pair(give)
    both = 2 * rows
    left, side = pltpu.VMEM((HID + 16, 2 * both), BF16), pltpu.VMEM((HID, both), BF16)
    scratch = [left, side, side, left, side, side]
    grads, sums_second = call(
        second_kernel,
        [shape(part * n_z, HID), shape(1, 128)],
        [SMEM, SMEM] + [VMEM] * 11,
        scratch,
        us=8.0,
        limit=42,
    )(member_live, place, xs, xs_far, sx, sx_far, gx, saved, *weights, body, critic_head)
    message = shape(part + small, HID)
    dealt = call(deal_kernel, [message] * n_z, [SMEM, VMEM, VMEM, VMEM], us=0.5)(place, grads, keep, got)
    arrived = [dealt[0]] + [along(dealt[k], k) for k in range(1, n_z)]
    whole, sums = call(
        functools.partial(reduce_kernel, part),
        [message, shape(members * dp, 128)],
        [SMEM] + [VMEM] * (2 + n_z),
    )(place, sums_joint, sums_second, *arrived)
    sums = lax.all_to_all(sums, ("member", "dp"), 0, 0, tiled=True)
    piece = call(piece_kernel, shape(part, HID), [VMEM], us=8.0)(whole)
    pieces, bit = {0: piece, n_z: to_pair(whole)}, 1
    while bit < n_z:
        pieces[bit] = along(piece, bit)
        bit *= 2
    at_hand = sorted(pieces)
    *values, sums = lax.optimization_barrier((*[pieces[k] for k in at_hand], sums))
    pieces = dict(zip(at_hand, values))
    found = {k: [(pieces[k], 0, 0, part)] for k in at_hand}
    actor = [[(0, part, part + small), (1, part, part + small)]]
    (block,) = join([whole, pieces[n_z]], actor)
    if dp > 2:
        found[dp - 1] = [(along(pieces[0], dp - 1), 0, 0, part)]
    bits = dp.bit_length() - 1
    for level in range(2, bits):
        paths = {}
        for k in range(dp):
            if bin(k).count("1") == level:
                low, rest = k & -k, k & (k - 1)
                cut = part // 32 * 8 if k < n_z and level == 2 else 0
                paths.setdefault(low, []).append((k, cut, part))
                if cut:
                    paths.setdefault(rest, []).append((k, 0, cut))
        inputs = sorted({k & ~bit for bit, slices in paths.items() for k, _, _ in slices})
        plan = []
        for bit, slices in paths.items():
            plan.append([])
            for k, start, stop in slices:
                first = found[k & ~bit][0][1]
                plan[-1].append((inputs.index(k & ~bit), first + start, first + stop))
        sent = join([found[k][0][0] for k in inputs], plan)
        level_found = {}
        for (bit, slices), message in zip(paths.items(), sent):
            came, at = along(message, bit), 0
            for k, start, stop in slices:
                level_found.setdefault(k, []).append((came, at, start, stop))
                at += stop - start
        if level + 1 < bits:
            whole_ones = sorted(level_found)
            rows_of = [join([v[0] for v in sorted(level_found[k], key=lambda v: v[2])], [[(i, v[1], v[1] + v[3] - v[2]) for i, v in enumerate(sorted(level_found[k], key=lambda v: v[2]))]])[0] for k in whole_ones]
            level_found = {k: [(v, 0, 0, part)] for k, v in zip(whole_ones, rows_of)}
        found.update(level_found)
    blocks = [block] + [to_member(block, k) for k in range(1, members)]
    arrays, sources = [], []
    for k, places in sorted(found.items()):
        for array, at, start, stop in places:
            if not any(array is other for other in arrays):
                arrays.append(array)
            sources.append((k, [array is other for other in arrays].index(True), at, start, stop))
    halved = lambda a: shape(*a.shape, dtype=BF16)
    heads = [critic_head, critic_head_mom, critic_head_sq, critic_head_tgt]
    single = shape(1, 1)
    loss, norm, lt_new, lt_mom, lt_sq, scale = call(
        scalars_kernel, [shape(1, 5), single, single, single, single, shape(8, 128)], [SMEM] * 3 + [VMEM], us=0.5
    )(log_temp, log_temp_mom, log_temp_sq, sums)
    outs = like(body, body, body, body) + [halved(body)] + like(*heads) + [halved(critic_head)]
    critic = call(
        functools.partial(critic_update_kernel, n_z, part, sources, len(arrays)),
        outs,
        [SMEM] + [VMEM] * (1 + len(arrays) + 8),
        [pltpu.VMEM((4 * n_z * part + 8, 128), F32)]
        + buffers(*outs)
        + [pltpu.SemaphoreType.DMA((-(-body.shape[0] // BLOCK), 4))],
        us=6.0,
        out_specs=[HBM] * len(outs),
    )(place, scale, *arrays, body, mom, sq, body_tgt, *heads)
    outs = like(policy_body, policy_body, policy_body) + [halved(policy_body)] + like(*turned) + [halved(turned[0])]
    policy = call(
        functools.partial(policy_update_kernel, small, len(blocks)),
        outs,
        [SMEM] + [VMEM] * (1 + len(blocks) + 6),
        [pltpu.VMEM((2 * members * small, HID), F32), pltpu.VMEM(policy_body.shape, F32)],
        us=0.2,
    )(place, scale, *blocks, policy_body, policy_body_mom, policy_body_sq, *turned)
    new = [unflat(v) for v in critic[:5]] + list(critic[5:]) + list(policy[:4]) + [v.T for v in policy[4:]]
    return (loss[0], norm[0], *new, lt_new[0], lt_mom[0], lt_sq[0])


def solution(mesh):
    row, line = P("dp", None), P("dp")
    stack, flat = P("member", None, None), P("member", None)
    return jax.shard_map(
        functools.partial(per_device, mesh.shape["member"], mesh.shape["dp"]),
        mesh=mesh,
        in_specs=(row, row, line, row, line, line, row, P("member")) + (stack,) * 4 + (flat,) * 4 + (P(),) * 9,
        out_specs=(P(), P()) + (stack,) * 5 + (flat,) * 5 + (P(),) * 11,
        check_vma=False,
    )
```

```python
import functools

import jax
import jax.numpy as jnp
from jax import lax
from jax.experimental import pallas as pl
from jax.experimental.pallas import tpu as pltpu
from jax.sharding import PartitionSpec as P

STEPS_DONE = 5
DISCOUNT = 0.99
POLYAK_RATE = 0.005
ENTROPY_TARGET = -6.0
DIVERSITY_WEIGHT = 1.0
LEARN_RATE = 0.05
BETA_ONE = 0.5
BETA_TWO = 0.5
DECAY_RATE = 0.01
ADAM_EPSILON = 1e-08
GRAD_FLOOR = 0.0001
CLIP_NORM = 1.0
LOGSTD_LOW = -5.0
LOGSTD_HIGH = 2.0
LOG_TWO = 0.6931471805599453
HALF_LOG_TWOPI = 0.9189385332046727
FAR_VALUE = 1e30

F32 = jnp.float32
BF16 = jnp.bfloat16
HID = 256
S_DIM = 17
A_DIM = 6
X_DIM = S_DIM + A_DIM
TWO = X_DIM + 1
THREE = TWO + HID + 1
BODY = THREE + HID + 1
CRITIC_ROWS = 544
P_TWO = 24
P_THREE = 288
P_LAST = 544
P_HEAD = 552
POLICY_ROWS = 576
BLOCK = 272
VMEM = pl.BlockSpec(memory_space=pltpu.VMEM)
SMEM = pl.BlockSpec(memory_space=pltpu.SMEM)
HBM = pl.BlockSpec(memory_space=pltpu.HBM)


def call(kernel, outs, in_specs, scratch=(), us=1.0, out_specs=None, limit=32):
    return pl.pallas_call(
        kernel,
        out_shape=outs,
        in_specs=in_specs,
        out_specs=out_specs or jax.tree.map(lambda _: VMEM, outs),
        scratch_shapes=list(scratch),
        compiler_params=pltpu.CompilerParams(vmem_limit_bytes=limit * 2**20),
        cost_estimate=pl.CostEstimate(flops=int(us * 1.15e9), bytes_accessed=0, transcendentals=0),
    )


def buffers(*arrays):
    return [pltpu.VMEM(a.shape, a.dtype) for a in arrays] + [pltpu.SemaphoreType.DMA((len(arrays),))]


def start_copies(sources, targets, sem):
    copies = [pltpu.make_async_copy(a, b, sem.at[i]) for i, (a, b) in enumerate(zip(sources, targets))]
    for copy in copies:
        copy.start()
    return copies


def shape(*dims, dtype=F32):
    return jax.ShapeDtypeStruct(dims, dtype)


def dot(a, b):
    return lax.dot_general(a, b, (((1,), (0,)), ((), ())), preferred_element_type=F32)


def dot_rows(a, b):
    return lax.dot_general(a, b, (((1,), (1,)), ((), ())), preferred_element_type=F32)


def halves(w):
    high = w.astype(BF16)
    return high, (w - high.astype(F32)).astype(BF16)


def stack_weights(w):
    high = (0.5 * w).astype(BF16).astype(F32)
    return jnp.concatenate([high, high, 0.5 * w - high], axis=0).T.astype(BF16)


def stack_inputs(v):
    high = v.astype(BF16).astype(F32)
    return jnp.concatenate([high, v - high, high], axis=0).astype(BF16)


def act(z):
    t = jnp.tanh(z)
    return z + z * t, t


def slope(h, t):
    return (1.0 + h) + t * (1.0 - h)


def curve(z, t):
    return (1.0 - t * t) * (1.0 - z * t)


def wide(column):
    return jnp.broadcast_to(column, (column.shape[0], 128))


def spread(column, rows):
    return jnp.concatenate([column] * (rows // 128), axis=1)


def action_rows(v):
    k = lax.broadcasted_iota(jnp.int32, v.shape, 0)
    return jnp.where((k >= 1) & (k <= A_DIM), v, 0.0)


def row_at(v, k, like):
    return jnp.where(lax.broadcasted_iota(jnp.int32, like.shape, 0) == k, v, like)


def lane_row(block):
    return jnp.concatenate([block[i : i + 1] for i in range(block.shape[0])], axis=1)


def interleave(*streams):
    results, active = [None] * len(streams), list(enumerate(streams))
    while active:
        left = []
        for i, stream in active:
            try:
                next(stream)
                left.append((i, stream))
            except StopIteration as end:
                results[i] = end.value
        active = left
    return results


def critic_rows(ref, c):
    def read(a, b):
        if b - a == 1:
            base = 4 * a // 8 * 8
            window = ref[base : base + 8, :]
            k = lax.broadcasted_iota(jnp.int32, window.shape, 0)
            picked = [jnp.where(k == 4 * a - base + 2 * t + c, window, 0.0) for t in range(2)]
            return jnp.concatenate([jnp.sum(v, axis=0, keepdims=True) for v in picked], axis=1)
        return jnp.concatenate([ref[pl.ds(4 * a + 2 * t + c, b - a, stride=4), :] for t in range(2)], axis=1)

    return read


def load_trunk(body, n_in, one, mats, bias, i, backward=False):
    one[i] = stack_weights(body(0, n_in + 1))
    yield
    for k, start in enumerate((n_in + 1, n_in + 2 + HID)):
        high, low = halves(0.5 * body(start, start + HID))
        mats[i, 4 * k] = high.T
        mats[i, 4 * k + 1] = low.T
        if backward:
            mats[i, 4 * k + 2] = high
            mats[i, 4 * k + 3] = low
        bias[i, k] = wide(0.5 * body(start + HID, start + HID + 1).T)
        yield


def trunk_arrays(n, n_in):
    return [shape(n, HID, 3 * (n_in + 1), dtype=BF16), shape(n, 8, HID, HID, dtype=BF16), shape(n, 2, HID, 128)]


def trunk_scratch(n, n_in):
    return [pltpu.VMEM(a.shape, a.dtype) for a in trunk_arrays(n, n_in)]


def times(w, k, h):
    mats, i = w
    return dot(mats[i, k], h) + dot(mats[i, k + 1], h)


def times_exact(w, k, h):
    mats, i = w
    high, low = halves(h)
    return dot(mats[i, k], high) + dot(mats[i, k + 1], high) + dot(mats[i, k], low)


def policy_head_rows(turned):
    one = jnp.zeros((1, HID + 1), F32)
    return jnp.concatenate([one, turned[:A_DIM], one, one, turned[A_DIM:], one], axis=0)


def noise_of(seed_row):
    k = lax.broadcasted_iota(jnp.int32, (8, seed_row.shape[1]), 0).astype(F32) - 1.0
    return 1.7 * jnp.sin(0.618034 * seed_row + 2.39996 * k)


def actor_stream(one, mats, bias, head, head_bias, x, noise):
    rows = x.shape[1]
    z = dot(one[0], stack_inputs(x))
    yield
    z = times((mats, 0), 0, act(z)[0].astype(BF16))
    yield
    z = times((mats, 0), 4, act(z + spread(bias[0, 0], rows))[0].astype(BF16))
    yield
    high, low = halves(act(z + spread(bias[0, 1], rows))[0])
    out = dot(head, high)
    out = out[:16] + out[16:] + dot(head[:16], low) + spread(head_bias, rows)
    yield
    mean, raw = out[:8], out[8:]
    turned = jnp.tanh(raw)
    log_std = LOGSTD_LOW + 0.5 * (LOGSTD_HIGH - LOGSTD_LOW) * (turned + 1.0)
    deviation = jnp.exp(log_std) * noise
    u = mean + deviation
    soft = jnp.maximum(-2.0 * u, 0.0) + jnp.log(1.0 + jnp.exp(-jnp.abs(2.0 * u)))
    squash = 2.0 * (LOG_TWO - u - soft)
    terms = -0.5 * noise * noise - log_std - HALF_LOG_TWOPI - squash
    log_prob = jnp.sum(action_rows(terms), axis=0, keepdims=True)
    return jnp.tanh(u), turned, deviation, log_prob


def first_kernel(place, out):
    out[...] = jnp.full(out.shape, (place[0] == 0).astype(F32))


def actor_kernel(
    first, states, actions, next_states, seeds, rewards, terminal, valid, body, head, log_temp, xs, xn, xp, aux, one, mats, bias
):
    rows = states.shape[1]
    ones = jnp.ones((1, rows), F32)
    for x, source in ((xs, states), (xn, next_states), (xp, states)):
        x[0:S_DIM, :] = source[...]
        x[X_DIM : X_DIM + 1, :] = ones
    xs[S_DIM:X_DIM, :] = actions[...]
    seed = seeds[...].astype(F32)
    loading = load_trunk(lambda a, b: body[a:b], S_DIM, one, mats, bias, 0, backward=True)
    next(loading)
    head_rows = policy_head_rows(head[...])
    head_w, head_b = jnp.concatenate(halves(head_rows[:, :HID]), axis=0), wide(head_rows[:, HID:])
    carry = 1.0 - lane_row(terminal[...].astype(F32))
    temper = jnp.exp(log_temp[0])
    now_in = jnp.concatenate([states[...], ones], axis=0)
    later_in = jnp.concatenate([next_states[...], ones], axis=0)
    half = rows // 2
    done = interleave(
        *[
            actor_stream(one, mats, bias, head_w, head_b, x[:, i : i + half], noise_of(seed[k : k + 1, i : i + half]))
            for i in (0, half)
            for x, k in ((later_in, 1), (now_in, 0))
        ],
        loading,
    )[:-1]
    later = [jnp.concatenate(v, axis=1) for v in zip(*done[0::2])]
    now = [jnp.concatenate(v, axis=1) for v in zip(*done[1::2])]
    xn[S_DIM:X_DIM, :] = later[0][1 : 1 + A_DIM]
    aux[0:1, :] = lane_row(rewards[...]) - DISCOUNT * carry * temper * later[3]
    aux[1:2, :] = DISCOUNT * carry
    aux[2:3, :] = lane_row(valid[...].astype(F32))
    action, turned, deviation, log_prob = now
    xp[S_DIM:X_DIM, :] = action[1 : 1 + A_DIM]
    aux[3:4, :] = log_prob
    aux[4:5, :] = spread(first[0:1], rows)
    aux[5:8, :] = jnp.zeros((3, rows), F32)
    aux[8:16, :] = action_rows(action)
    aux[16:24, :] = action_rows(turned)
    aux[24:32, :] = action_rows(deviation)


def head_column(head, c):
    row = head[pl.ds(c, 1), :]
    return row[:, :HID].T, row[:, HID:]


def inner_rows(read):
    high, low = halves(0.5 * read(16, 24))
    return jnp.concatenate([high.astype(F32), low.astype(F32)], axis=0).astype(BF16)


def action_gradient(inner, y):
    grad = dot(inner, y)
    return action_rows(grad[:8] + grad[8:])


def data_stream(one, mats, bias, i, column, inner, x, save):
    rows, w = x.shape[1], (mats, i)
    z = dot(one[i], x)
    save(0, z)
    yield
    h, t = act(z)
    d1 = slope(h, t)
    z = times_exact(w, 0, h)
    yield
    z = z + spread(bias[i, 0], rows)
    save(1, z)
    h, t = act(z)
    d2 = slope(h, t)
    z = times_exact(w, 4, h)
    yield
    z = z + spread(bias[i, 1], rows)
    save(2, z)
    h, t = act(z)
    c = times(w, 6, (spread(column, rows) * slope(h, t)).astype(BF16))
    yield
    save(3, c)
    c = times(w, 2, (c * d2).astype(BF16))
    yield
    save(4, c)
    grad = action_gradient(inner, (c * d1).astype(BF16))
    yield
    size = jnp.sum(grad * grad, axis=0, keepdims=True) + GRAD_FLOOR
    return grad * lax.rsqrt(size)


def target_stream(one, mats, bias, i, column, last, x):
    rows, w = x.shape[1], (mats, i)
    z = dot(one[i], x)
    yield
    z = times(w, 0, act(z)[0].astype(BF16))
    yield
    z = times(w, 4, act(z + spread(bias[i, 0], rows))[0].astype(BF16))
    yield
    h = act(z + spread(bias[i, 1], rows))[0]
    return jnp.sum(spread(column, rows) * h, axis=0, keepdims=True) + last


def chosen_stream(one, mats, bias, i, column, last, inner, x):
    rows = x.shape[1]
    z = dot(one[i], x)
    yield
    h, t = act(z)
    d1 = slope(h, t)
    z = dot(mats[i, 0], h.astype(BF16))
    yield
    h, t = act(z + spread(bias[i, 0], rows))
    d2 = slope(h, t)
    z = dot(mats[i, 4], h.astype(BF16))
    yield
    h, t = act(z + spread(bias[i, 1], rows))
    column = spread(column, rows)
    q = jnp.sum(column * h, axis=0, keepdims=True) + last
    c = dot(mats[i, 6], (column * slope(h, t)).astype(BF16))
    yield
    c = dot(mats[i, 2], (c * d2).astype(BF16))
    yield
    return q, action_gradient(inner, (c * d1).astype(BF16))


def critic_kernel(live, place, xs, xn, xp, body, head, body_tgt, head_tgt, out, saved, *refs):
    mine, scratch, columns = refs[:3], refs[3:6], refs[6]
    order = [place[1], 1 - place[1]]
    lasts, inners, trunks, loading = [], [], [], []
    for i in range(4):
        c = order[i % 2]
        read = critic_rows((body, body_tgt)[i // 2], c)
        trunks.append((*mine, 0) if i == 0 else (*scratch, i - 1))
        loading.append(load_trunk(read, X_DIM, *trunks[i], backward=i < 2))
        next(loading[-1])
        column, last = head_column((head, head_tgt)[i // 2], c)
        columns[i] = wide(column)
        lasts.append(last)
        if i < 2:
            inners.append(inner_rows(read))
    alive = [live[c].astype(F32) for c in order]
    rows = xs.shape[1]
    step = 256
    for start in range(0, rows, step):
        at = slice(start, start + step)
        data, later, chosen = stack_inputs(xs[:, at]), stack_inputs(xn[:, at]), stack_inputs(xp[:, at])

        def save(k, value, at=at):
            saved[k, :, at] = value

        done = interleave(
            data_stream(*trunks[0], columns[0], inners[0], data, save),
            data_stream(*trunks[1], columns[1], inners[1], data, lambda k, value: None),
            *[chosen_stream(*trunks[c], columns[c], lasts[c], inners[c], chosen) for c in range(2)],
            *[target_stream(*trunks[2 + c], columns[2 + c], lasts[2 + c], later) for c in range(2)],
            *loading,
        )
        loading = []
        unit, now, value = done[0:2], done[2:4], done[4:6]
        lowest = [jnp.where(alive[c] > 0, value[c], FAR_VALUE) for c in range(2)]
        total_n, total_q, total_g = [alive[0] * a + alive[1] * b for a, b in (unit, *zip(*now))]
        out[0:8, at] = row_at(jnp.minimum(lowest[0], lowest[1]), 7, row_at(alive[0] + alive[1], 0, total_n))
        out[8:16, at] = row_at(total_q, 0, total_g)


def merge(a, b):
    k = lax.broadcasted_iota(jnp.int32, a.shape, 0)
    return jnp.where(k == 7, jnp.minimum(a, b), a + b)


def joint_kernel(mine, other, aux, log_temp, sx, gx, sums):
    both = merge(mine[...], other[...])
    unit, grad = both[:8], both[8:]
    mask, log_prob = aux[2:3, :], aux[3:4, :]
    members = both[0:1]
    target = aux[0:1, :] + aux[1:2, :] * both[7:8]
    unit = action_rows(unit)
    sx[...] = row_at(target, 7, row_at(mask, 0, mask * unit))
    gx[...] = row_at(members, 7, grad)
    temper = jnp.exp(log_temp[0])
    spread = jnp.sum(mask * (jnp.sum(unit * unit, axis=0, keepdims=True) - members), axis=1, keepdims=True)
    actor = jnp.sum(mask * (temper * log_prob - both[8:9] / members), axis=1, keepdims=True)
    entropy = jnp.sum(mask * (log_prob + ENTROPY_TARGET), axis=1, keepdims=True)
    count = jnp.sum(mask, axis=1, keepdims=True)
    lane = lax.broadcasted_iota(jnp.int32, (1, 128), 1)
    row = jnp.where(lane == 1, spread, 0.0) + jnp.where(lane == 2, actor, 0.0)
    row = row + jnp.where(lane == 3, entropy, 0.0) + jnp.where(lane == 4, count, 0.0)
    sums[...] = row * aux[4:5, 0:128]


def policy_stream(one, mats, bias, head_back, x, rows8, by_log):
    rows, w = x.shape[1], (mats, 0)
    z = dot(one[0], stack_inputs(x))
    yield
    h, t = act(z)
    d1, h1 = slope(h, t), h.astype(BF16)
    z = times(w, 0, h1)
    yield
    h, t = act(z + spread(bias[0, 0], rows))
    d2, h2 = slope(h, t), h.astype(BF16)
    z = times(w, 4, h2)
    yield
    h, t = act(z + spread(bias[0, 1], rows))
    action, turned, deviation, by_action = rows8
    by_u = by_action * (1.0 - action * action) + by_log * 2.0 * action
    by_std = by_u * deviation - by_log
    by_raw = action_rows(by_std * (0.5 * (LOGSTD_HIGH - LOGSTD_LOW)) * (1.0 - turned * turned))
    by_out = jnp.concatenate([action_rows(by_u), by_raw], axis=0)
    high, low = halves(by_out)
    f3 = (dot(head_back, jnp.concatenate([high, low, high], axis=0)) * slope(h, t)).astype(BF16)
    yield
    f2 = (times(w, 6, f3) * d2).astype(BF16)
    yield
    f1 = (times(w, 2, f2) * d1).astype(BF16)
    yield
    return h1, h2, h.astype(BF16), f1, f2, f3, high, low, by_out


def policy_kernel(place, xs, aux, gx, one, mats, bias, head, log_temp, keep, give, full):
    rows = xs.shape[1]
    n = S_DIM
    head_high, head_low = halves(0.5 * policy_head_rows(head[...])[:, :HID])
    head_back = jnp.concatenate([head_high, head_high, head_low], axis=0).astype(F32).T.astype(BF16)
    x = row_at(1.0, n, xs[...])
    mask, members = aux[2:3, :], gx[7:8, :]
    by_action = -(mask / members) * action_rows(gx[...])
    by_log = jnp.exp(log_temp[0]) * mask
    rows8 = (aux[8:16, :], aux[16:24, :], aux[24:32, :], by_action)
    step = rows // 4
    cut = lambda v, i: v[:, i * step : (i + 1) * step]
    streams = [
        policy_stream(one, mats, bias, head_back, cut(x[: n + 1], i), [cut(v, i) for v in rows8], cut(by_log, i))
        for i in range(4)
    ]
    h1, h2, h3, f1, f2, f3, high, low, by_out = [jnp.concatenate(v, axis=1) for v in zip(*interleave(*streams))]
    ones = row_at(1.0, 0, jnp.zeros((16, rows), F32)).astype(BF16)
    start = jnp.where(lax.broadcasted_iota(jnp.int32, x.shape, 0) <= n, x, 0.0).astype(BF16)
    full[0:P_TWO, :] = dot_rows(start, f1)
    full[P_TWO:P_THREE, :] = dot_rows(jnp.concatenate([h1, ones], axis=0), f2)[: HID + 8]
    layer = dot_rows(jnp.concatenate([h2, ones], axis=0), f3)
    full[P_THREE : P_THREE + HID, :] = layer[:HID]
    last = wide(jnp.sum(by_out, axis=1, keepdims=True)).T[0:1]
    last = jnp.concatenate([last, jnp.zeros((1, HID - 16), F32)], axis=1)
    full[P_LAST:P_HEAD, :] = row_at(last, 1, layer[HID : HID + 8])
    by_head = dot_rows(jnp.concatenate([high, low], axis=0), h3)
    full[P_HEAD : P_HEAD + 16, :] = by_head[:16] + by_head[16:]
    full[P_HEAD + 16 :, :] = jnp.zeros((full.shape[0] - P_HEAD - 16, HID), F32)
    size = keep.shape[0]
    for out, x in ((keep, place[1]), (give, 1 - place[1])):
        out[...] = full[pl.ds(pl.multiple_of((2 * place[0] + x) * size, 8), size), :]


def padded(parts, rows):
    return jnp.concatenate([v if n == 0 else jnp.zeros((n, rows), F32) for n, v in parts], axis=0).astype(BF16)


def second_stream(
    one, mats, bias, column, last, inner, inner_stack, alive, weight, x, s, saved, here, left3, here3, there3, left2, here2,
    there2,
):
    rows, w = x.shape[1], (mats, 0)
    total = left3.shape[1] // 2
    there = slice(total + here.start, total + here.stop)
    one_row = row_at(1.0, 0, jnp.zeros((16, rows), F32))
    none = jnp.zeros((16, rows), BF16)
    mask, target = s[0:1], s[7:8]
    for left in (left2, left3):
        left[HID : HID + 16, here] = one_row.astype(BF16)
        left[HID : HID + 16, there] = none
    z = dot(one[0], stack_inputs(x)) if saved is None else saved[0]
    yield
    h, t = act(z)
    d1, e1 = slope(h, t), curve(z, t)
    left2[0:HID, here] = h.astype(BF16)
    if saved is None:
        z = times_exact(w, 0, h)
        yield
        z = z + spread(bias[0, 0], rows)
    else:
        z = saved[1]
        yield
    h, t = act(z)
    d2, e2 = slope(h, t), curve(z, t)
    left3[0:HID, here] = h.astype(BF16)
    if saved is None:
        z = times_exact(w, 4, h)
        yield
        z = z + spread(bias[0, 1], rows)
    else:
        z = saved[2]
        yield
    h, t = act(z)
    d3, e3 = slope(h, t), curve(z, t)
    column = spread(column, rows)
    q = jnp.sum(column * h, axis=0, keepdims=True) + last
    miss = q - target
    half_a = alive * mask * miss
    td = jnp.sum(half_a * miss, axis=1, keepdims=True)
    head = (2.0 * half_a) * h
    b3 = column * d3
    e3 = column * e3
    cut = b3.astype(BF16)
    there3[:, here] = cut
    c2 = times(w, 6, cut) if saved is None else saved[3]
    yield
    b2 = c2 * d2
    e2 = c2 * e2
    cut = b2.astype(BF16)
    there2[:, here] = cut
    c1 = times(w, 2, cut) if saved is None else saved[4]
    yield
    b1 = c1 * d1
    e1 = c1 * e1
    cut = b1.astype(BF16)
    there1 = cut
    grad = action_gradient(inner, cut)
    yield
    size = jnp.sum(grad * grad, axis=0, keepdims=True) + GRAD_FLOOR
    cot = action_rows(s) * weight
    along = jnp.sum(grad * cot, axis=0, keepdims=True)
    v = lax.rsqrt(size) * (cot - grad * (along / size))
    first = dot_rows(there1, padded([(16, 0), (0, 0.5 * v), (8, 0)], rows))
    t1 = dot(inner_stack, stack_inputs(v))
    yield
    cut = (d1 * t1).astype(BF16)
    left2[0:HID, there] = cut
    t2 = times(w, 0, cut)
    yield
    cut = (d2 * t2).astype(BF16)
    left3[0:HID, there] = cut
    t3 = times(w, 4, cut)
    yield
    head = head + d3 * t3
    head = sum(head[:, i : i + 128] for i in range(0, rows, 128))
    r = e3 * t3
    here3[:, here] = (half_a * b3 + r).astype(BF16)
    r = dot(mats[0, 6], r.astype(BF16)) * d2 + e2 * t2
    yield
    here2[:, here] = (half_a * b2 + r).astype(BF16)
    r = dot(mats[0, 2], r.astype(BF16)) * d1 + e1 * t1
    yield
    first = first + dot_rows((half_a * b1 + r).astype(BF16), padded([(0, x), (8, 0)], rows))
    return td, jnp.sum(half_a, axis=1, keepdims=True), head, first


def second_kernel(live, place, xs, xs_far, sx, sx_far, gx, saved, one, mats, bias, body, head, *refs):
    (grads, sums), scratch = refs[:2], refs[2:]
    left3, here3, there3, left2, here2, there2 = scratch
    rows = xs.shape[1]
    mine = place[1]
    alive = jnp.where(mine == 0, live[0], live[1]).astype(F32)
    read = critic_rows(body, mine)
    column, last = head_column(head, mine)
    column = wide(column)
    inner, inner_stack = inner_rows(read), stack_weights(read(16, 24))
    weight = 2.0 * DIVERSITY_WEIGHT * alive / (gx[7:8, :] - 1.0)
    td = bias_sum = jnp.zeros((1, 1), F32)
    step = rows // 2
    by_head, first = jnp.zeros((HID, 128), F32), jnp.zeros((HID, 32), F32)
    for td_part, bias_part, head_part, first_part in interleave(
        *[
            second_stream(
                one, mats, bias, column, last, inner, inner_stack, alive, weight[:, start : start + step],
                x[:, start : start + step], s[:, start : start + step],
                None if i else [saved[k, :, start : start + step] for k in range(5)],
                slice(i * rows + start, i * rows + start + step), *scratch,
            )
            for start in range(0, rows, step)
            for i, (x, s) in enumerate(((xs, sx), (xs_far, sx_far)))
        ]
    ):
        td, bias_sum, by_head, first = td + td_part, bias_sum + bias_part, by_head + head_part, first + first_part

    def layer(left, here, there):
        n = here.shape[1]
        return dot_rows(left[:, 0:n], here[...]) + 0.5 * dot_rows(left[:, n:], there[...])

    grads[0:TWO, :] = first.T[0:TWO]
    grads[TWO:THREE, :] = layer(left2, here2, there2)[0 : HID + 1]
    grads[THREE:BODY, :] = layer(left3, here3, there3)[0 : HID + 1]
    grads[BODY : BODY + 1, :] = jnp.sum(by_head.T, axis=0, keepdims=True)
    lane = lax.broadcasted_iota(jnp.int32, (1, HID), 1)
    grads[BODY + 1 : BODY + 2, :] = jnp.where(lane == 0, 2.0 * bias_sum, 0.0)
    grads[BODY + 2 :, :] = jnp.zeros((grads.shape[0] - BODY - 2, HID), F32)
    sums[...] = jnp.where(lax.broadcasted_iota(jnp.int32, (1, 128), 1) == 0, td, 0.0)


def deal_kernel(place, critic, keep, got, *out):
    part = critic.shape[0] // (len(out) + 1)
    policy = keep[...] + got[...]
    for k, message in enumerate(out, 1):
        to = jnp.bitwise_xor(place[2], k)
        message[0:part, :] = critic[pl.ds(pl.multiple_of(to * part, 8), part), :]
        message[part:, :] = policy


def reduce_kernel(part, place, one, two, own, keep, got, *refs):
    ins, (out, sums) = refs[:-2], refs[-2:]
    own = own[pl.ds(pl.multiple_of(place[2] * part, 8), part), :]
    total = jnp.concatenate([own, keep[...] + got[...]], axis=0)
    for r in ins:
        total = total + r[...]
    out[...] = total
    critic, policy = total[:part], total[part:]
    square = jnp.sum(jnp.sum(critic * critic, axis=0, keepdims=True), axis=1, keepdims=True)
    once = (place[2] == 0).astype(F32)
    square = square + once * jnp.sum(jnp.sum(policy * policy, axis=0, keepdims=True), axis=1, keepdims=True)
    lane = lax.broadcasted_iota(jnp.int32, (1, 128), 1)
    row = one[...] + two[...] + jnp.where(lane == 5, square, 0.0)
    sums[...] = jnp.broadcast_to(row, sums.shape)


def piece_kernel(whole, out):
    out[...] = whole[0 : out.shape[0], :]


def adam(weights, moment, second, grads):
    moment_new = BETA_ONE * (moment + grads)
    second_new = BETA_TWO * (second + grads * grads)
    root = (1.0 / (1.0 - BETA_TWO**STEPS_DONE)) ** 0.5
    bottom = (root * second_new) * lax.rsqrt(second_new) + ADAM_EPSILON
    guess = pltpu.reciprocal(bottom, approx=True)
    inverse = guess * (2.0 - bottom * guess)
    step = ((LEARN_RATE / (1.0 - BETA_ONE**STEPS_DONE)) * moment_new) * inverse
    return (1.0 - LEARN_RATE * DECAY_RATE) * weights - step, moment_new, second_new


def scalars_kernel(log_temp, log_mom, log_sq, sums, loss, norm_out, lt, lm, ls, scale):
    total = jnp.sum(sums[...], axis=0, keepdims=True)
    entropy, count = total[:, 3:4], total[:, 4:5]
    grad_temp = -entropy / count
    norm = jnp.sqrt(total[:, 5:6] / (count * count) + grad_temp * grad_temp)
    factor = CLIP_NORM / jnp.maximum(norm, CLIP_NORM)
    lane = lax.broadcasted_iota(jnp.int32, (1, 128), 1)
    loss[...] = jnp.where(lane == 3, -log_temp[0] * entropy, total)[:, 0:5]
    norm_out[...] = norm
    one = lambda v: jnp.full((1, 1), v[0])
    put((lt, lm, ls), (slice(0, 1),), adam(one(log_temp), one(log_mom), one(log_sq), factor * grad_temp))
    scale[...] = jnp.broadcast_to(factor / count, (8, 128))


def put(refs, at, got):
    for r, value in zip(refs, got):
        r[at] = value.astype(r.dtype)


def critic_update_kernel(n_z, part, sources, n_pieces, place, scale, *refs):
    refs = list(refs)
    take = lambda n: [refs.pop(0) for _ in range(n)]
    pieces = take(n_pieces)
    w, m, v, t, hw, hm, hv, ht = take(8)
    outs, (total,), near, (sem, body_sem) = take(10), take(1), take(10), take(2)
    scale = scale[0:1, 0:1]
    for k, i, first, start, stop in sources:
        piece = pieces[i]
        c = jnp.bitwise_xor(place[1], k // n_z)
        z = jnp.bitwise_xor(place[2], k % n_z)
        for side in range(2):
            at = pl.ds(4 * (part * z + start) + 2 * side + c, stop - start, stride=4)
            total[at, :] = piece[first : first + stop - start, side * 128 : (side + 1) * 128]
    copies = []
    rows = w.shape[0]
    for i, start in enumerate(range(0, rows, BLOCK)):
        at = pl.ds(start, min(BLOCK, rows - start))
        new, mom, sq = adam(w[at, :], m[at, :], v[at, :], total[at, :] * scale)
        tgt = t[at, :] + POLYAK_RATE * (new - t[at, :])
        put(near[0:4], (at, slice(None)), (new, mom, sq, tgt))
        copies += start_copies([r.at[at, :] for r in near[0:4]], [r.at[at, :] for r in outs[0:4]], body_sem.at[i])
    near[4][...] = near[0][...].astype(BF16)
    copies += start_copies(near[4:5], outs[4:5], sem)
    grads = []
    for c in range(2):
        first = [4 * BODY + c, 4 * BODY + 2 + c, 4 * BODY + 4 + c]
        grads.append(jnp.concatenate([total[first[0] : first[0] + 1, :], total[first[1] : first[1] + 1, :], total[first[2] : first[2] + 1, 0:1]], axis=1))
    new, mom, sq = adam(hw[...], hm[...], hv[...], jnp.concatenate(grads, axis=0) * scale)
    tgt = ht[...] + POLYAK_RATE * (new - ht[...])
    put(near[5:10], (slice(None), slice(None)), (new, mom, sq, tgt, new))
    copies += start_copies(near[5:], outs[5:], sem.at[pl.ds(5, 5)])
    for copy in copies:
        copy.wait()


def policy_update_kernel(small, n_blocks, place, scale, *refs):
    refs = list(refs)
    take = lambda n: [refs.pop(0) for _ in range(n)]
    blocks, (w, m, v, hw, hm, hv), near, (policy, natural) = take(n_blocks), take(6), take(8), take(2)
    scale = scale[0:1, 0:1]
    for owner, block in enumerate(blocks):
        for x in range(2):
            at = 2 * jnp.bitwise_xor(place[0], owner) + jnp.bitwise_xor(place[1], x)
            policy[pl.ds(pl.multiple_of(at * small, 8), small), :] = block[x * small : (x + 1) * small, :]
    second, third = S_DIM + 1, S_DIM + 2 + HID
    natural[0:second, :] = policy[0:second, :]
    natural[second:third, :] = policy[P_TWO : P_TWO + HID + 1, :]
    natural[third:, :] = policy[P_THREE : P_THREE + HID + 1, :]
    new, mom, sq = adam(w[...], m[...], v[...], natural[...] * scale)
    put(near[0:4], (slice(None),), (new, mom, sq, new))
    by_head = policy[P_HEAD : P_HEAD + 16, :]
    last = jnp.broadcast_to(policy[P_LAST + 1 : P_LAST + 2, 0:16], (8, 16)).T[:, 0:1]
    grad = jnp.concatenate([by_head, last], axis=1)
    grad = jnp.concatenate([grad[1 : 1 + A_DIM], grad[9 : 9 + A_DIM]], axis=0)
    new, mom, sq = adam(hw[...], hm[...], hv[...], grad * scale)
    put(near[4:8], (slice(None), slice(None)), (new, mom, sq, new))


def join_kernel(n, plan, *refs):
    for out, slices in zip(refs[n:], plan):
        at = 0
        for i, start, stop in slices:
            out[at : at + stop - start, :] = refs[i][start:stop, :]
            at += stop - start


def join(arrays, plan):
    outs = [shape(sum(stop - start for _, start, stop in slices), HID) for slices in plan]
    return call(functools.partial(join_kernel, len(arrays), plan), outs, [VMEM] * len(arrays), us=0.3)(*arrays)


def flat(v):
    return jnp.transpose(v.reshape(2, -1, 2, 128), (1, 2, 0, 3)).reshape(-1, 128)


def unflat(v):
    return jnp.transpose(v.reshape(-1, 2, 2, 128), (2, 0, 1, 3)).reshape(2, -1, HID)


def per_device(
    members,
    dp,
    states,
    actions,
    rewards,
    next_states,
    terminal,
    valid_rows,
    noise_seeds,
    member_live,
    critic_body,
    critic_body_mom,
    critic_body_sq,
    critic_body_tgt,
    critic_head,
    critic_head_mom,
    critic_head_sq,
    critic_head_tgt,
    policy_body,
    policy_body_mom,
    policy_body_sq,
    policy_head,
    policy_head_mom,
    policy_head_sq,
    log_temp,
    log_temp_mom,
    log_temp_sq,
):
    rows = states.shape[0]
    n_z = dp // 2
    part = -(-CRITIC_ROWS // (8 * n_z)) * 8
    small = -(-POLICY_ROWS // (16 * members)) * 8
    m, d = lax.axis_index("member"), lax.axis_index("dp")
    place = jnp.stack([m, d // n_z, d % n_z]).astype(jnp.int32)

    def across(value, axis, n, to):
        return lax.ppermute(value, axis, [(i, to(i)) for i in range(n)])

    def to_member(value, bit):
        return across(value, "member", members, lambda i: i ^ bit)

    def to_pair(value):
        return across(value, "dp", dp, lambda i: i ^ n_z)

    def along(value, offset):
        return across(value, "dp", dp, lambda i: i ^ offset)

    square = lambda v: v.reshape(rows // 128, 128)
    turned = [policy_head.T, policy_head_mom.T, policy_head_sq.T]
    body, mom, sq, body_tgt = flat(critic_body), flat(critic_body_mom), flat(critic_body_sq), flat(critic_body_tgt)
    like = lambda *arrays: [shape(*a.shape, dtype=a.dtype) for a in arrays]
    first = call(first_kernel, shape(8, 128), [SMEM], us=8.0, limit=1)(place)
    xs, xn, xp, aux, *actor_weights = call(
        actor_kernel,
        [shape(24, rows), shape(24, rows), shape(24, rows), shape(32, rows)] + trunk_arrays(1, S_DIM),
        [VMEM] * 10 + [SMEM],
        us=3.0,
    )(
        first, states.T, actions.T, next_states.T, noise_seeds.T, square(rewards), square(terminal), square(valid_rows),
        policy_body, turned[0], log_temp,
    )
    xs_far = to_pair(xs)
    ensemble, saved, *weights = call(
        critic_kernel,
        [shape(16, rows), shape(5, HID, rows)] + trunk_arrays(1, X_DIM),
        [SMEM, SMEM] + [VMEM] * 7,
        trunk_scratch(3, X_DIM) + [pltpu.VMEM((4, HID, 128), F32)],
        us=8.0,
    )(
        member_live, place, xs, xn, xp, body, critic_head, body_tgt, critic_head_tgt
    )
    bit = 1
    while bit * 2 < members:
        other = to_member(ensemble, bit)
        k = lax.broadcasted_iota(jnp.int32, ensemble.shape, 0)
        ensemble = jnp.where(k == 7, jnp.minimum(ensemble, other), ensemble + other)
        bit *= 2
    sx, gx, sums_joint = call(
        joint_kernel, [shape(8, rows), shape(8, rows), shape(1, 128)], [VMEM, VMEM, VMEM, SMEM], us=0.7
    )(ensemble, to_member(ensemble, bit), aux, log_temp)
    sx_far = to_pair(sx)
    keep, give = call(
        policy_kernel,
        [shape(small, HID), shape(small, HID)],
        [SMEM] + [VMEM] * 7 + [SMEM],
        [pltpu.VMEM((2 * members * small, HID), F32)],
        us=3.0,
    )(place, xs, aux, gx, *actor_weights, turned[0], log_temp)
    got = to_pair(give)
    both = 2 * rows
    left, side = pltpu.VMEM((HID + 16, 2 * both), BF16), pltpu.VMEM((HID, both), BF16)
    scratch = [left, side, side, left, side, side]
    grads, sums_second = call(
        second_kernel,
        [shape(part * n_z, HID), shape(1, 128)],
        [SMEM, SMEM] + [VMEM] * 11,
        scratch,
        us=8.0,
        limit=42,
    )(member_live, place, xs, xs_far, sx, sx_far, gx, saved, *weights, body, critic_head)
    message = shape(part + small, HID)
    dealt = call(deal_kernel, [message] * (n_z - 1), [SMEM, VMEM, VMEM, VMEM], us=0.5)(place, grads, keep, got)
    arrived = [along(dealt[k - 1], k) for k in range(1, n_z)]
    whole, sums = call(
        functools.partial(reduce_kernel, part),
        [message, shape(members * dp, 128)],
        [SMEM] + [VMEM] * (4 + n_z),
    )(place, sums_joint, sums_second, grads, keep, got, *arrived)
    sums = lax.all_to_all(sums, ("member", "dp"), 0, 0, tiled=True)
    piece = call(piece_kernel, shape(part, HID), [VMEM], us=8.0)(whole)
    pieces, bit = {0: piece, n_z: to_pair(whole)}, 1
    while bit < n_z:
        pieces[bit] = along(piece, bit)
        bit *= 2
    at_hand = sorted(pieces)
    *values, sums = lax.optimization_barrier((*[pieces[k] for k in at_hand], sums))
    pieces = dict(zip(at_hand, values))
    found = {k: [(pieces[k], 0, 0, part)] for k in at_hand}
    actor = [[(0, part, part + small), (1, part, part + small)]]
    (block,) = join([whole, pieces[n_z]], actor)
    if dp > 2:
        found[dp - 1] = [(along(pieces[0], dp - 1), 0, 0, part)]
    bits = dp.bit_length() - 1
    for level in range(2, bits):
        paths = {}
        for k in range(dp):
            if bin(k).count("1") == level:
                low, rest = k & -k, k & (k - 1)
                cut = part // 32 * 8 if k < n_z and level == 2 else 0
                paths.setdefault(low, []).append((k, cut, part))
                if cut:
                    paths.setdefault(rest, []).append((k, 0, cut))
        inputs = sorted({k & ~bit for bit, slices in paths.items() for k, _, _ in slices})
        plan = []
        for bit, slices in paths.items():
            plan.append([])
            for k, start, stop in slices:
                first = found[k & ~bit][0][1]
                plan[-1].append((inputs.index(k & ~bit), first + start, first + stop))
        sent = join([found[k][0][0] for k in inputs], plan)
        level_found = {}
        for (bit, slices), message in zip(paths.items(), sent):
            came, at = along(message, bit), 0
            for k, start, stop in slices:
                level_found.setdefault(k, []).append((came, at, start, stop))
                at += stop - start
        if level + 1 < bits:
            whole_ones = sorted(level_found)
            rows_of = [join([v[0] for v in sorted(level_found[k], key=lambda v: v[2])], [[(i, v[1], v[1] + v[3] - v[2]) for i, v in enumerate(sorted(level_found[k], key=lambda v: v[2]))]])[0] for k in whole_ones]
            level_found = {k: [(v, 0, 0, part)] for k, v in zip(whole_ones, rows_of)}
        found.update(level_found)
    blocks = [block] + [to_member(block, k) for k in range(1, members)]
    arrays, sources = [], []
    for k, places in sorted(found.items()):
        for array, at, start, stop in places:
            if not any(array is other for other in arrays):
                arrays.append(array)
            sources.append((k, [array is other for other in arrays].index(True), at, start, stop))
    halved = lambda a: shape(*a.shape, dtype=BF16)
    heads = [critic_head, critic_head_mom, critic_head_sq, critic_head_tgt]
    single = shape(1, 1)
    loss, norm, lt_new, lt_mom, lt_sq, scale = call(
        scalars_kernel, [shape(1, 5), single, single, single, single, shape(8, 128)], [SMEM] * 3 + [VMEM], us=0.5
    )(log_temp, log_temp_mom, log_temp_sq, sums)
    outs = like(body, body, body, body) + [halved(body)] + like(*heads) + [halved(critic_head)]
    critic = call(
        functools.partial(critic_update_kernel, n_z, part, sources, len(arrays)),
        outs,
        [SMEM] + [VMEM] * (1 + len(arrays) + 8),
        [pltpu.VMEM((4 * n_z * part + 8, 128), F32)]
        + buffers(*outs)
        + [pltpu.SemaphoreType.DMA((-(-body.shape[0] // BLOCK), 4))],
        us=6.0,
        out_specs=[HBM] * len(outs),
    )(place, scale, *arrays, body, mom, sq, body_tgt, *heads)
    outs = like(policy_body, policy_body, policy_body) + [halved(policy_body)] + like(*turned) + [halved(turned[0])]
    policy = call(
        functools.partial(policy_update_kernel, small, len(blocks)),
        outs,
        [SMEM] + [VMEM] * (1 + len(blocks) + 6),
        [pltpu.VMEM((2 * members * small, HID), F32), pltpu.VMEM(policy_body.shape, F32)],
        us=0.2,
    )(place, scale, *blocks, policy_body, policy_body_mom, policy_body_sq, *turned)
    new = [unflat(v) for v in critic[:5]] + list(critic[5:]) + list(policy[:4]) + [v.T for v in policy[4:]]
    return (loss[0], norm[0], *new, lt_new[0], lt_mom[0], lt_sq[0])


def solution(mesh):
    row, line = P("dp", None), P("dp")
    stack, flat = P("member", None, None), P("member", None)
    return jax.shard_map(
        functools.partial(per_device, mesh.shape["member"], mesh.shape["dp"]),
        mesh=mesh,
        in_specs=(row, row, line, row, line, line, row, P("member")) + (stack,) * 4 + (flat,) * 4 + (P(),) * 9,
        out_specs=(P(), P()) + (stack,) * 5 + (flat,) * 5 + (P(),) * 11,
        check_vma=False,
    )
```
